32 devices in a mesh: slab: 4 (over y, x), seq: 8 (over z, core).
Axes of the slice: x: 2, y: 2, z: 4, core: 2. Of those that a mesh axis runs over, the one named last changes fastest.
Arguments:
- video_tokens: bfloat16 [128, 128, 1152], P(('slab', 'seq')), may hold values from -40 to 40
- modulation: float32 [128, 3, 1152], P(('slab', 'seq')), may hold values from -3 to 3
- qkv_weight: bfloat16 [1152, 3456], P(None, 'seq'), may hold values from -1.5 to 1.5
- out_weight: bfloat16 [1152, 1152], P(None, 'seq'), may hold values from -0.1875 to 0.1875
Outputs:
- restored: bfloat16 [128, 128, 1152], P(('slab', 'seq'))
The draws below stay inside these ranges and needn't reach their ends.
All inputs are finite; a program needn't handle non-finite values.
Results may differ from the reference program's by a relative error of at most 0.004.
Values may be sent and summed in bfloat16 or wider, within the bound.
No kernel may reach another device: no remote copies, remote signals or barrier semaphores. Data moves between devices by JAX's collectives and lax.ppermute only.
A program may use at most 128 MiB of HBM per device.

```python
import jax
import jax.numpy as jnp
from jax import lax

D = 1152
H = 16
HD = 72
FRS = 32
POS_DEV = 16
S = 128
FRAMES = 128
N_SEQ = 8


def draw_video_tokens(key, part):
    key_common = jax.random.fold_in(key, 11)
    values = jax.random.normal(key_common, (FRAMES, S, D), jnp.float32)
    return jnp.clip(values, -40.0, 40.0).astype(jnp.bfloat16)


def draw_qkv_weight(key, part):
    values = jax.random.normal(jax.random.fold_in(key, 21), (D, 3 * D), jnp.float32) * D ** (-0.5)
    return jnp.clip(values, -1.5, 1.5).astype(jnp.bfloat16)


def levels(stream_key, shape, split, smallest, largest):
    level = 1.0
    for position, blocks in split:
        draws = jax.random.uniform(jax.random.fold_in(jax.random.fold_in(stream_key, 6), position), (blocks,), jnp.float32, smallest / len(split), largest / len(split))
        level = level * jnp.repeat(jnp.exp(draws), shape[position] // blocks).reshape((-1,) + (1,) * (len(shape) - 1 - position))
    return level


def noise(own_key, shape, spread, bound, split=(), held_as=jnp.bfloat16):
    entries = spread * jax.random.normal(own_key, shape, jnp.float32)
    if split:
        entries = entries * levels(own_key, shape, split, -0.22, 0.18)
    return jnp.clip(entries, -bound, bound).astype(held_as)


def setup_inputs(seed: int = 0) -> dict:
    splits = jax.random.split(jax.random.key(seed), 5)
    video_tokens = draw_video_tokens(jax.random.fold_in(splits[4], 71), 0)
    modulation = noise(splits[1], (FRAMES, 3, D), 0.5, 3.0, ((0, 32),), jnp.float32)
    qkv_weight = draw_qkv_weight(jax.random.fold_in(splits[4], 71), 0)
    out_weight = noise(splits[3], (D, D), D ** -0.5, 0.1875, ((1, 8),))
    return dict(video_tokens=video_tokens, modulation=modulation, qkv_weight=qkv_weight, out_weight=out_weight)


epsilon = 1e-06

def modulate(tokens, modulation):
    values = tokens.astype(jnp.float32)
    average = lax.optimization_barrier(jnp.mean(values, axis=-1, keepdims=True))
    centered = values - average
    variance = lax.optimization_barrier(jnp.mean(centered * centered, axis=-1, keepdims=True))
    normed = centered * lax.rsqrt(variance + epsilon)
    return (normed * (1.0 + modulation[:, 1][:, None, :]) + modulation[:, 0][:, None, :]).astype(jnp.bfloat16)

def attend(queries, key_rows, value_rows):
    scores = jnp.einsum('wtphd,wsphd->wphts', queries.astype(jnp.float32), key_rows.astype(jnp.float32))
    scores = scores * queries.shape[-1] ** (-0.5)
    scores = scores - lax.optimization_barrier(jnp.max(scores, axis=-1, keepdims=True))
    exponent = jnp.exp(scores)
    softmaxed = (exponent / lax.optimization_barrier(jnp.sum(exponent, axis=-1, keepdims=True))).astype(jnp.bfloat16)
    result = jnp.einsum('wphts,wsphd->wtphd', softmaxed.astype(jnp.float32), value_rows.astype(jnp.float32))
    return result.astype(jnp.bfloat16)

def windows(values):
    return values.reshape(FRAMES // FRS, FRS, values.shape[1], values.shape[2], values.shape[3])

def reference(video_tokens, modulation, qkv_weight, out_weight):
    heads_half = H // 2

    def one_block(block_index):
        offset = (block_index * POS_DEV).astype(jnp.int32)
        tokens = lax.dynamic_slice_in_dim(video_tokens, offset, POS_DEV, 1)
        normed = modulate(tokens, modulation)
        token_rows = normed.reshape(FRAMES * POS_DEV, D)
        projected = jnp.dot(token_rows, qkv_weight, preferred_element_type=jnp.float32).astype(jnp.bfloat16)
        grouped = projected.reshape(FRAMES, POS_DEV, 6, heads_half, HD)
        windowed = attend(windows(grouped[:, :, 0]), windows(grouped[:, :, 1]), windows(grouped[:, :, 2]))
        windowed = windowed.reshape(FRAMES, POS_DEV, heads_half, HD)
        rolled = jnp.roll(grouped[:, :, 3:], FRS // 2, axis=0)
        shifted = attend(windows(rolled[:, :, 0]), windows(rolled[:, :, 1]), windows(rolled[:, :, 2]))
        shifted = jnp.roll(shifted.reshape(FRAMES, POS_DEV, heads_half, HD), -(FRS // 2), axis=0)
        attended = jnp.concatenate([windowed, shifted], axis=2).reshape(FRAMES * POS_DEV, D)
        output_rows = jnp.dot(attended, out_weight, preferred_element_type=jnp.float32).astype(jnp.bfloat16)
        output_rows = output_rows.reshape(FRAMES, POS_DEV, D)
        restored = tokens.astype(jnp.float32) + modulation[:, 2][:, None, :] * output_rows.astype(jnp.float32)
        return restored.astype(jnp.bfloat16)
    blocks_out = lax.map(one_block, jnp.arange(N_SEQ, dtype=jnp.int32))
    return jnp.transpose(blocks_out, (1, 0, 2, 3)).reshape(FRAMES, S, D)
```

```python
import functools

import jax
import jax.numpy as jnp
from jax import lax
from jax.experimental import pallas as pl
from jax.experimental.pallas import tpu as pltpu
from jax.sharding import PartitionSpec as P

H = 16
FRS = 32
EPSILON = 1e-06
LANES = 128
ROWS = 16
VMEM_BYTES = 50 * 1024 * 1024


def padded(width):
    return -(-width // LANES) * LANES


def norm_kernel(index_ref, tokens_ref, modulation_ref, *refs):
    out_refs, mixed = refs[:-1], refs[-1]
    frames = tokens_ref.shape[0]
    groups, rows, width = out_refs[0].shape
    positions = groups * rows // frames
    index = index_ref[0]
    for d, out_ref in enumerate(out_refs):
        start = pl.multiple_of(lax.bitwise_xor(index, d) * positions, positions)
        for f in range(frames):
            values = tokens_ref[f, pl.ds(start, positions), :].astype(jnp.float32)
            average = jnp.mean(values, axis=-1, keepdims=True)
            centered = values - average
            variance = jnp.mean(centered * centered, axis=-1, keepdims=True)
            normed = centered * lax.rsqrt(variance + EPSILON)
            result = normed * (1.0 + modulation_ref[f, 1:2, :]) + modulation_ref[f, 0:1, :]
            for t in range(width // LANES):
                mixed[t, pl.ds(f, positions, stride=frames), :] = result[:, t * LANES : (t + 1) * LANES]
        for t in range(width // LANES):
            out_ref[:, :, t * LANES : (t + 1) * LANES] = mixed[t].astype(out_ref.dtype).reshape(groups, rows, LANES)


def restore_kernel(index_ref, tokens_ref, modulation_ref, *refs):
    in_refs, out_ref, mixed = refs[:-2], refs[-2], refs[-1]
    frames = tokens_ref.shape[0]
    groups, rows, width = in_refs[0].shape
    positions = groups * rows // frames
    index = index_ref[0]
    for d, in_ref in enumerate(in_refs):
        start = pl.multiple_of(lax.bitwise_xor(index, d) * positions, positions)
        for t in range(width // LANES):
            part = in_ref[:, :, t * LANES : (t + 1) * LANES]
            mixed[t] = part.reshape(groups * rows, LANES).astype(jnp.float32)
        for f in range(frames):
            values = tokens_ref[f, pl.ds(start, positions), :].astype(jnp.float32)
            projected = jnp.concatenate(
                [mixed[t, pl.ds(f, positions, stride=frames), :] for t in range(width // LANES)], axis=1
            )
            result = values + modulation_ref[f, 2:3, :] * projected
            out_ref[f, pl.ds(start, positions), :] = result.astype(out_ref.dtype)


def nt_dot(left, right):
    return lax.dot_general(left, right, (((1,), (1,)), ((), ())), preferred_element_type=jnp.float32)


def head_window(head, head_size, shift):
    first = shift + head * head_size
    last = first + head_size
    low = first // LANES * LANES
    return first, last, low, padded(last)


def masked(values, first, last, low):
    lane = lax.broadcasted_iota(jnp.int32, values.shape, 1) + low
    return jnp.where((lane >= first) & (lane < last), values, jnp.zeros_like(values))


def softmax(scores, same, scale):
    scores = jnp.where(same, scores, -jnp.inf)
    top = jnp.max(scores, axis=-1, keepdims=True)
    exponent = jnp.exp((scores - top) * scale)
    total = jnp.sum(exponent, axis=-1, keepdims=True)
    return (exponent * (1.0 / total)).astype(jnp.bfloat16)


def block_kernel(plan, frames, index_ref, *refs):
    count, extra, weights = plan["count"], plan["extra"], plan["weights"]
    refs = list(refs)
    x_refs = [refs.pop(0) for _ in range(count)]
    e_refs = [refs.pop(0) for _ in range(extra)]
    w_refs = [refs.pop(0) for _ in range(weights)]
    out_refs = [refs.pop(0) for _ in range(count)]
    xs, xe, wall, qkv, ext, att, ys, sems, wsems = refs
    groups, _, rows, width = xs.shape
    half, lanes = plan["half"], plan["lanes"]
    heads_half = H // 2
    head_size = width // H
    scale = head_size ** (-0.5)
    slot = count * rows
    index, slab = index_ref[0], index_ref[1]

    copies = []
    for d in range(count):
        owner = lax.bitwise_xor(index, d)
        copies.append((x_refs[d], xs.at[:, owner]))
        copies.append((e_refs[d // 2].at[d % 2], xe.at[:, owner]))
    copies = [pltpu.make_async_copy(a, b, sems.at[n]) for n, (a, b) in enumerate(copies)]
    moves = []
    for operand, at, size, owner, part in plan["moves"]:
        if owner is None:
            row = part * lanes + (lanes - half if part == 5 else 0)
            row = row if part < 6 else 6 * lanes + (part - 6) * half
            moves.append((w_refs[operand].at[at[0]], wall.at[pl.ds(row, size)]))
            continue
        device = lax.bitwise_xor(index, owner)
        piece = lax.bitwise_xor(slab, part[1]) if part[0] == "xor" else jnp.int32(part[1])
        column = device * plan["columns"] + piece * size
        block = column // half
        row = block * lanes + (column - block * half)
        row = row + jnp.where(block == 5, lanes - half, 0)
        row = jnp.where(piece * size < plan["columns"], row,
                        6 * lanes + device * plan["outs"] + piece * size - plan["columns"])
        source = w_refs[operand]
        for step in at:
            source = source.at[step]
        moves.append((source, wall.at[pl.ds(pl.multiple_of(row, ROWS), size)]))
    moves = [pltpu.make_async_copy(a, b, wsems.at[n]) for n, (a, b) in enumerate(moves)]
    for copy in moves + copies:
        copy.start()
    gap = lanes - half
    for block in range(6):
        edge = block * lanes + (0 if block == 5 else half)
        if gap:
            wall[edge : edge + gap, :] = jnp.zeros((gap, width), wall.dtype)
    for copy in moves + copies:
        copy.wait()

    tokens = groups * slot
    own = xs[...].reshape(tokens, width)
    for block in range(6):
        part = wall[block * lanes : (block + 1) * lanes, :]
        qkv[block] = nt_dot(own, part).astype(qkv.dtype)
        if block >= 4:
            ext[block - 4] = nt_dot(xe[...].reshape(tokens, width), part).astype(ext.dtype)

    def one_group(g, carry):
        here = pl.ds(pl.multiple_of(g * slot, slot), slot)
        row = lax.broadcasted_iota(jnp.int32, (slot, slot), 0)
        column = lax.broadcasted_iota(jnp.int32, (slot, slot), 1)
        same = (row % rows) // frames == (column % rows) // frames
        low_half = lax.broadcasted_iota(jnp.int32, (slot, 1), 0) < slot // 2
        tiles = [None] * (width // LANES)

        def add(first_tile, value):
            for n in range(value.shape[1] // LANES):
                piece = value[:, n * LANES : (n + 1) * LANES]
                t = first_tile + n
                tiles[t] = piece if tiles[t] is None else tiles[t] + piece

        for head in range(heads_half):
            first, last, low, high = head_window(head, head_size, 0)
            queries = qkv[0, here, low:high]
            keys = masked(qkv[1, here, low:high], first, last, low)
            values = masked(qkv[2, here, low:high], first, last, low)
            probs = softmax(nt_dot(queries, keys), same, scale)
            add(low // LANES, jnp.dot(probs, values, preferred_element_type=jnp.float32))
        for head in range(heads_half):
            first, last, low, high = head_window(head, head_size, 0)
            queries = qkv[3, here, low:high]
            own_keys = masked(qkv[4, here, low:high], first, last, low)
            ext_keys = masked(ext[0, here, low:high], first, last, low)
            first, last, low, high = head_window(head, head_size, gap)
            own_values = masked(qkv[5, here, low:high], first, last, low)
            ext_values = masked(ext[1, here, low:high], first, last, low)
            mid = slot // 2
            keys = jnp.where(low_half, own_keys, ext_keys)
            later = jnp.where(low_half, ext_keys, own_keys)
            values = jnp.where(low_half, own_values, ext_values)
            later_values = jnp.where(low_half, ext_values, own_values)
            scores = jnp.concatenate([nt_dot(queries[:mid], keys), nt_dot(queries[mid:], later)], axis=0)
            probs = softmax(scores, same, scale)
            result = jnp.concatenate([
                jnp.dot(probs[:mid], values, preferred_element_type=jnp.float32),
                jnp.dot(probs[mid:], later_values, preferred_element_type=jnp.float32),
            ], axis=0)
            add((width // 2 - gap + low) // LANES, result)
        att[here, :] = jnp.concatenate(tiles, axis=1).astype(att.dtype)
        return carry

    lax.fori_loop(0, groups, one_group, 0)
    y = nt_dot(att[...], wall[6 * lanes :, :]).astype(ys.dtype)
    ys[...] = y.reshape(ys.shape)
    for d in range(count):
        out_refs[d][...] = ys[:, lax.bitwise_xor(index, d)]


def per_device(video_tokens, modulation, qkv_weight, out_weight):
    frames, positions, width = video_tokens.shape
    count, slabs = lax.axis_size("seq"), lax.axis_size("slab")
    index, slab = lax.axis_index("seq"), lax.axis_index("slab")
    block_positions = positions // count
    block_rows = block_positions * frames
    groups = block_rows // ROWS
    block = jax.ShapeDtypeStruct((groups, ROWS, width), jnp.bfloat16)
    own_index = jnp.stack([index, slab]).astype(jnp.int32)
    smem = pl.BlockSpec(memory_space=pltpu.SMEM)
    vmem = pl.BlockSpec(memory_space=pltpu.VMEM)
    anywhere = pl.BlockSpec(memory_space=pl.ANY)
    params = pltpu.CompilerParams(vmem_limit_bytes=VMEM_BYTES)

    def hop(value, seq_xor, slab_xor=0):
        pairs = [(s * count + i, (s ^ slab_xor) * count + (i ^ seq_xor)) for s in range(slabs) for i in range(count)]
        return lax.ppermute(value, ("slab", "seq"), pairs)

    half = width // 2
    lanes = padded(half)
    columns, outs = qkv_weight.shape[1], out_weight.shape[1]
    shard = jnp.concatenate([qkv_weight.T, out_weight.T], axis=0)
    unit = (columns + outs) // slabs
    moves = []
    if unit % ROWS == 0 and columns % unit == 0 and half % unit == 0:
        parts = shard.reshape(slabs, unit, width)
        mine = lax.dynamic_index_in_dim(parts, slab, 0, keepdims=False)
        operands = [parts, hop(parts, 1)]
        for sibling in range(2):
            for n in range(slabs):
                moves.append((sibling, (n,), unit, sibling, ("at", n)))
        received = {z: hop(mine, 2 * z) for z in range(1, count // 2)}
        bundles = [([1], True)]
        if count > 4:
            bundles.append((list(range(2, count // 2)), False))
        for zs, reverse in bundles:
            base = jnp.stack([received[z] for z in zs])
            held = {0: base}
            bits = [1 << b for b in range(slabs.bit_length() - 1)]
            for bit in reversed(bits) if reverse else bits:
                for e in list(held):
                    held[e ^ bit] = hop(held[e], 0, bit)
            for e in sorted(held):
                for sibling in range(2):
                    operands.append(held[e] if sibling == 0 else hop(held[e], 1))
                    for n, z in enumerate(zs):
                        moves.append((len(operands) - 1, (n,), unit, (2 * z) ^ sibling, ("xor", e)))
        plan_columns, plan_outs = columns, outs
    else:
        full_qkv = lax.all_gather(qkv_weight.T, "seq", axis=0, tiled=True)
        full_out = lax.all_gather(out_weight.T, "seq", axis=0, tiled=True)
        operands = [full_qkv.reshape(6, half, width), full_out.reshape(2, half, width)]
        operands = [jnp.concatenate(operands, axis=0)]
        moves = [(0, (n,), half, None, n) for n in range(8)]
        plan_columns, plan_outs = columns, outs

    sent = pl.pallas_call(
        norm_kernel,
        out_shape=[block] * count,
        in_specs=[smem, vmem, vmem],
        out_specs=[vmem] * count,
        scratch_shapes=[pltpu.VMEM((width // LANES, block_rows, LANES), jnp.float32)],
        compiler_params=params,
        name="norm",
    )(own_index, video_tokens, modulation)
    blocks = [sent[0]] + [hop(sent[d], d) for d in range(1, count)]
    middle = count // 2
    extras = []
    for z in range(count // 2):
        pairs = []
        for s in range(slabs):
            for i in range(count):
                step = 1 if (i ^ (2 * z)) >= middle else -1
                pairs.append((s * count + i, (s + step) % slabs * count + i))
        extras.append(lax.ppermute(jnp.stack(blocks[2 * z : 2 * z + 2]), ("slab", "seq"), pairs))

    plan = dict(count=count, extra=len(extras), weights=len(operands), half=half, lanes=lanes, moves=moves,
                columns=plan_columns, outs=plan_outs)
    tokens = count * block_rows
    flops = 2 * tokens * width * (6 * lanes + 2 * lanes + width)
    projected = pl.pallas_call(
        functools.partial(block_kernel, plan, frames),
        out_shape=[block] * count,
        in_specs=[smem] + [anywhere] * (count + len(extras) + len(operands)),
        out_specs=[vmem] * count,
        scratch_shapes=[
            pltpu.VMEM((groups, count, ROWS, width), jnp.bfloat16),
            pltpu.VMEM((groups, count, ROWS, width), jnp.bfloat16),
            pltpu.VMEM((6 * lanes + width, width), jnp.bfloat16),
            pltpu.VMEM((6, tokens, lanes), jnp.bfloat16),
            pltpu.VMEM((2, tokens, lanes), jnp.bfloat16),
            pltpu.VMEM((tokens, width), jnp.bfloat16),
            pltpu.VMEM((groups, count, ROWS, width), jnp.bfloat16),
            pltpu.SemaphoreType.DMA((2 * count,)),
            pltpu.SemaphoreType.DMA((len(moves),)),
        ],
        compiler_params=params,
        cost_estimate=pl.CostEstimate(flops=flops, bytes_accessed=16 * 1024 * 1024, transcendentals=0),
        name="block",
    )(own_index, *blocks, *extras, *operands)
    returned = [projected[0]] + [hop(projected[d], d) for d in range(1, count)]
    return pl.pallas_call(
        restore_kernel,
        out_shape=jax.ShapeDtypeStruct(video_tokens.shape, video_tokens.dtype),
        in_specs=[smem, vmem, vmem] + [vmem] * count,
        out_specs=vmem,
        scratch_shapes=[pltpu.VMEM((width // LANES, block_rows, LANES), jnp.float32)],
        compiler_params=params,
        name="restore",
    )(own_index, video_tokens, modulation, *returned)


def solution(mesh):
    return jax.shard_map(
        per_device,
        mesh=mesh,
        in_specs=(
            P(("slab", "seq"), None, None),
            P(("slab", "seq"), None, None),
            P(None, "seq"),
            P(None, "seq"),
        ),
        out_specs=P(("slab", "seq"), None, None),
        check_vma=False,
    )
```

```python
import functools

import jax
import jax.numpy as jnp
from jax import lax
from jax.experimental import pallas as pl
from jax.experimental.pallas import tpu as pltpu
from jax.sharding import PartitionSpec as P

H = 16
FRS = 32
EPSILON = 1e-06
LANES = 128
ROWS = 16
VMEM_BYTES = 50 * 1024 * 1024


def padded(width):
    return -(-width // LANES) * LANES


def norm_kernel(index_ref, tokens_ref, modulation_ref, keep_ref, give_ref, mixed):
    frames = tokens_ref.shape[0]
    chips, groups, rows, width = keep_ref.shape
    positions = groups * rows // frames
    index = index_ref[0]
    for d in range(2 * chips):
        out_ref = (keep_ref, give_ref)[d % 2]
        start = pl.multiple_of(lax.bitwise_xor(index, d) * positions, positions)
        for f in range(frames):
            values = tokens_ref[f, pl.ds(start, positions), :].astype(jnp.float32)
            average = jnp.mean(values, axis=-1, keepdims=True)
            centered = values - average
            variance = jnp.mean(centered * centered, axis=-1, keepdims=True)
            normed = centered * lax.rsqrt(variance + EPSILON)
            result = normed * (1.0 + modulation_ref[f, 1:2, :]) + modulation_ref[f, 0:1, :]
            for t in range(width // LANES):
                mixed[t, pl.ds(f, positions, stride=frames), :] = result[:, t * LANES : (t + 1) * LANES]
        for t in range(width // LANES):
            part = mixed[t].astype(out_ref.dtype).reshape(groups, rows, LANES)
            out_ref[d // 2, :, :, t * LANES : (t + 1) * LANES] = part


def restore_kernel(index_ref, tokens_ref, modulation_ref, *refs):
    in_refs, out_ref, mixed = refs[:-2], refs[-2], refs[-1]
    frames = tokens_ref.shape[0]
    groups, rows, width = in_refs[0].shape
    positions = groups * rows // frames
    index = index_ref[0]
    for d, in_ref in enumerate(in_refs):
        start = pl.multiple_of(lax.bitwise_xor(index, d) * positions, positions)
        for t in range(width // LANES):
            part = in_ref[:, :, t * LANES : (t + 1) * LANES]
            mixed[t] = part.reshape(groups * rows, LANES).astype(jnp.float32)
        for f in range(frames):
            values = tokens_ref[f, pl.ds(start, positions), :].astype(jnp.float32)
            projected = jnp.concatenate(
                [mixed[t, pl.ds(f, positions, stride=frames), :] for t in range(width // LANES)], axis=1
            )
            result = values + modulation_ref[f, 2:3, :] * projected
            out_ref[f, pl.ds(start, positions), :] = result.astype(out_ref.dtype)


def nt_dot(left, right):
    return lax.dot_general(left, right, (((1,), (1,)), ((), ())), preferred_element_type=jnp.float32)


def head_window(head, head_size, shift):
    first = shift + head * head_size
    last = first + head_size
    low = first // LANES * LANES
    return first, last, low, padded(last)


def masked(values, first, last, low):
    lane = lax.broadcasted_iota(jnp.int32, values.shape, 1) + low
    return jnp.where((lane >= first) & (lane < last), values, jnp.zeros_like(values))


def softmax(scores, same, scale):
    scores = jnp.where(same, scores, -jnp.inf)
    top = jnp.max(scores, axis=0, keepdims=True)
    exponent = jnp.exp((scores - top) * scale)
    total = jnp.sum(exponent, axis=0, keepdims=True)
    return exponent * (1.0 / total)


def block_kernel(plan, frames, index_ref, *refs):
    count, extra, weights = plan["count"], plan["extra"], plan["weights"]
    refs = list(refs)
    x_refs = [refs.pop(0) for _ in range(extra)]
    e_refs = [refs.pop(0) for _ in range(extra)]
    w_refs = [refs.pop(0) for _ in range(weights)]
    out_refs = [refs.pop(0) for _ in range(count)]
    xs, xe, wall, qt, kn, vt, ken, vet, att, ys, sems, wsems = refs
    groups, _, rows, width = xs.shape
    half, lanes = plan["half"], plan["lanes"]
    heads_half = H // 2
    head_size = width // H
    scale = head_size ** (-0.5)
    slot = count * rows
    index, slab = index_ref[0], index_ref[1]

    copies = []
    for d in range(count):
        owner = lax.bitwise_xor(index, d)
        copies.append((x_refs[d // 2].at[d % 2], xs.at[:, owner]))
        copies.append((e_refs[d // 2].at[d % 2], xe.at[:, owner]))
    copies = [pltpu.make_async_copy(a, b, sems.at[n]) for n, (a, b) in enumerate(copies)]
    moves = []
    for operand, at, size, owner, part in plan["moves"]:
        if owner is None:
            row = part * size
        else:
            device = lax.bitwise_xor(index, owner)
            piece = lax.bitwise_xor(slab, part[1]) if part[0] == "xor" else jnp.int32(part[1])
            start = piece * size
            row = jnp.where(start < plan["columns"], device * plan["columns"] + start,
                            6 * half + device * plan["outs"] + start - plan["columns"])
        source = w_refs[operand]
        for step in at:
            source = source.at[step]
        moves.append((source, wall.at[pl.ds(pl.multiple_of(row, ROWS), size)]))
    moves = [pltpu.make_async_copy(a, b, wsems.at[n]) for n, (a, b) in enumerate(moves)]
    for copy in moves + copies:
        copy.start()
    gap = lanes - half
    if gap:
        for kind in range(2):
            qt[kind, half:, :] = jnp.zeros((gap, qt.shape[2]), qt.dtype)
            kn[kind, :, half:] = jnp.zeros((kn.shape[1], gap), kn.dtype)
        ken[:, half:] = jnp.zeros((ken.shape[0], gap), ken.dtype)
    for copy in moves + copies:
        copy.wait()

    tokens = groups * slot
    own = xs[...].reshape(tokens, width)
    for kind in range(2):
        parts = [wall[(3 * kind + n) * half : (3 * kind + n + 1) * half, :] for n in range(3)]
        qt[kind, :half, :] = nt_dot(parts[0], own).astype(qt.dtype)
        kn[kind, :, :half] = nt_dot(own, parts[1]).astype(kn.dtype)
        vt[kind] = nt_dot(parts[2], own).astype(vt.dtype)
        if kind == 1:
            others = xe[...].reshape(tokens, width)
            ken[:, :half] = nt_dot(others, parts[1]).astype(ken.dtype)
            vet[...] = nt_dot(parts[2], others).astype(vet.dtype)

    def one_group(g, carry):
        here = pl.ds(pl.multiple_of(g * slot, slot), slot)
        row = lax.broadcasted_iota(jnp.int32, (slot, slot), 0)
        column = lax.broadcasted_iota(jnp.int32, (slot, slot), 1)
        same = (row % rows) // frames == (column % rows) // frames
        near = (row < slot // 2) == (column < slot // 2)
        windows = [head_window(head, head_size, 0) for head in range(heads_half)]
        results = []
        scores = []
        for first, last, low, high in windows:
            keys = masked(kn[0, here, low:high], first, last, low)
            scores.append(jnp.dot(keys, qt[0, low:high, here], preferred_element_type=jnp.float32))
        probs = [softmax(score, same, scale).astype(jnp.bfloat16) for score in scores]
        for head, prob in enumerate(probs):
            values = vt[0, head * head_size : (head + 1) * head_size, here]
            results.append(jnp.dot(values, prob, preferred_element_type=jnp.float32))
        scores = []
        for first, last, low, high in windows:
            queries = qt[1, low:high, here]
            own_keys = masked(kn[1, here, low:high], first, last, low)
            other_keys = masked(ken[here, low:high], first, last, low)
            scores.append(jnp.where(
                near,
                jnp.dot(own_keys, queries, preferred_element_type=jnp.float32),
                jnp.dot(other_keys, queries, preferred_element_type=jnp.float32),
            ))
        probs = [softmax(score, same, scale) for score in scores]
        for head, prob in enumerate(probs):
            at = slice(head * head_size, (head + 1) * head_size)
            own_probs = jnp.where(near, prob, 0.0).astype(jnp.bfloat16)
            other_probs = jnp.where(near, 0.0, prob).astype(jnp.bfloat16)
            results.append(
                jnp.dot(vt[1, at, here], own_probs, preferred_element_type=jnp.float32)
                + jnp.dot(vet[at, here], other_probs, preferred_element_type=jnp.float32)
            )
        att[here, :] = jnp.concatenate(results, axis=0).T.astype(att.dtype)
        return carry

    lax.fori_loop(0, groups, one_group, 0)
    y = nt_dot(att[...], wall[6 * half :, :]).astype(ys.dtype)
    ys[...] = y.reshape(ys.shape)
    for d in range(count):
        out_refs[d][...] = ys[:, lax.bitwise_xor(index, d)]


def per_device(video_tokens, modulation, qkv_weight, out_weight):
    frames, positions, width = video_tokens.shape
    count, slabs = lax.axis_size("seq"), lax.axis_size("slab")
    index, slab = lax.axis_index("seq"), lax.axis_index("slab")
    block_positions = positions // count
    block_rows = block_positions * frames
    groups = block_rows // ROWS
    block = jax.ShapeDtypeStruct((groups, ROWS, width), jnp.bfloat16)
    own_index = jnp.stack([index, slab]).astype(jnp.int32)
    smem = pl.BlockSpec(memory_space=pltpu.SMEM)
    vmem = pl.BlockSpec(memory_space=pltpu.VMEM)
    anywhere = pl.BlockSpec(memory_space=pl.ANY)
    params = pltpu.CompilerParams(vmem_limit_bytes=VMEM_BYTES)

    def hop(value, seq_xor, slab_xor=0):
        pairs = [(s * count + i, (s ^ slab_xor) * count + (i ^ seq_xor)) for s in range(slabs) for i in range(count)]
        return lax.ppermute(value, ("slab", "seq"), pairs)

    half = width // 2
    lanes = padded(half)
    columns, outs = qkv_weight.shape[1], out_weight.shape[1]
    chips = count // 2
    unit = (columns + outs) // slabs
    moves = []
    if unit % ROWS == 0 and columns % unit == 0 and outs == unit and half % unit == 0:
        wide, narrow = qkv_weight.T, out_weight.T
        pieces = columns // unit
        first = lax.dynamic_slice_in_dim(wide, jnp.minimum(slab, pieces - 1) * unit, unit, 0)
        mine = jnp.where(slab < pieces, first, narrow)
        received = {0: mine}
        for bit in reversed(range(chips.bit_length() - 1)):
            for z in list(received):
                received[z ^ (1 << bit)] = hop(received[z], 2 << bit)
        operands = []

        def both_cores(value, entries):
            for sibling in range(2):
                operands.append(hop(value, 1) if sibling else value)
                for at, size, z, part in entries:
                    moves.append((len(operands) - 1, at, size, (2 * z) ^ sibling, part))

        both_cores(wide, [((pl.ds(n * unit, unit),), unit, 0, ("at", n)) for n in range(pieces)])
        both_cores(narrow, [((), unit, 0, ("at", pieces))])
        near = list(range(1, chips - 1)) or [1]
        bundles = [(near, False)] + ([([chips - 1], True)] if chips - 1 not in near else [])
        for zs, reverse in bundles:
            base = jnp.stack([received[z] for z in zs])
            held = {0: base}
            bits = [1 << b for b in range(slabs.bit_length() - 1)]
            for bit in reversed(bits) if reverse else bits:
                for e in list(held):
                    held[e ^ bit] = hop(held[e], 0, bit)
            for e in sorted(held):
                both_cores(held[e], [((n,), unit, z, ("xor", e)) for n, z in enumerate(zs)])
    else:
        full_qkv = lax.all_gather(qkv_weight.T, "seq", axis=0, tiled=True)
        full_out = lax.all_gather(out_weight.T, "seq", axis=0, tiled=True)
        operands = [full_qkv.reshape(6, half, width), full_out.reshape(2, half, width)]
        operands = [jnp.concatenate(operands, axis=0)]
        moves = [(0, (n,), half, None, n) for n in range(8)]

    keep, give = pl.pallas_call(
        norm_kernel,
        out_shape=[jax.ShapeDtypeStruct((chips,) + block.shape, block.dtype)] * 2,
        in_specs=[smem, vmem, vmem],
        out_specs=[vmem] * 2,
        scratch_shapes=[pltpu.VMEM((width // LANES, block_rows, LANES), jnp.float32)],
        compiler_params=params,
        name="norm",
    )(own_index, video_tokens, modulation)
    swapped = hop(give, 1)
    middle = count // 2
    blocks, extras = [], []
    for z in range(chips):
        pair = jnp.stack([keep[z], swapped[z]])
        blocks.append(hop(pair, 2 * z) if z else pair)
        pairs = []
        for s in range(slabs):
            for i in range(count):
                step = 1 if (i ^ (2 * z)) >= middle else -1
                pairs.append((s * count + i, (s + step) % slabs * count + i))
        extras.append(lax.ppermute(blocks[z], ("slab", "seq"), pairs))

    plan = dict(count=count, extra=len(extras), weights=len(operands), half=half, lanes=lanes, moves=moves,
                columns=columns, outs=outs)
    tokens = count * block_rows
    flops = 2 * tokens * width * (6 * lanes + 2 * lanes + width)
    projected = pl.pallas_call(
        functools.partial(block_kernel, plan, frames),
        out_shape=[block] * count,
        in_specs=[smem] + [anywhere] * (2 * len(extras) + len(operands)),
        out_specs=[vmem] * count,
        scratch_shapes=[
            pltpu.VMEM((groups, count, ROWS, width), jnp.bfloat16),
            pltpu.VMEM((groups, count, ROWS, width), jnp.bfloat16),
            pltpu.VMEM((6 * half + width, width), jnp.bfloat16),
            pltpu.VMEM((2, lanes, tokens), jnp.bfloat16),
            pltpu.VMEM((2, tokens, lanes), jnp.bfloat16),
            pltpu.VMEM((2, half, tokens), jnp.bfloat16),
            pltpu.VMEM((tokens, lanes), jnp.bfloat16),
            pltpu.VMEM((half, tokens), jnp.bfloat16),
            pltpu.VMEM((tokens, width), jnp.bfloat16),
            pltpu.VMEM((groups, count, ROWS, width), jnp.bfloat16),
            pltpu.SemaphoreType.DMA((2 * count,)),
            pltpu.SemaphoreType.DMA((len(moves),)),
        ],
        compiler_params=params,
        cost_estimate=pl.CostEstimate(flops=flops, bytes_accessed=16 * 1024 * 1024, transcendentals=0),
        name="block",
    )(own_index, *blocks, *extras, *operands)
    returned = [projected[0]] + [hop(projected[d], d) for d in range(1, count)]
    return pl.pallas_call(
        restore_kernel,
        out_shape=jax.ShapeDtypeStruct(video_tokens.shape, video_tokens.dtype),
        in_specs=[smem, vmem, vmem] + [vmem] * count,
        out_specs=vmem,
        scratch_shapes=[pltpu.VMEM((width // LANES, block_rows, LANES), jnp.float32)],
        compiler_params=params,
        name="restore",
    )(own_index, video_tokens, modulation, *returned)


def solution(mesh):
    return jax.shard_map(
        per_device,
        mesh=mesh,
        in_specs=(
            P(("slab", "seq"), None, None),
            P(("slab", "seq"), None, None),
            P(None, "seq"),
            P(None, "seq"),
        ),
        out_specs=P(("slab", "seq"), None, None),
        check_vma=False,
    )
```

```python
import functools

import jax
import jax.numpy as jnp
from jax import lax
from jax.experimental import pallas as pl
from jax.experimental.pallas import tpu as pltpu
from jax.sharding import PartitionSpec as P

H = 16
FRS = 32
EPSILON = 1e-06
LANES = 128
ROWS = 16
SPACE_FLOPS = 40 * 10**9
VMEM_BYTES = 50 * 1024 * 1024


def padded(width):
    return -(-width // LANES) * LANES


def norm_kernel(index_ref, tokens_ref, modulation_ref, keep_ref, give_ref, mixed):
    frames = tokens_ref.shape[0]
    chips, groups, rows, width = keep_ref.shape
    positions = groups * rows // frames
    index = index_ref[0]
    for d in range(2 * chips):
        out_ref = (keep_ref, give_ref)[d % 2]
        start = pl.multiple_of(lax.bitwise_xor(index, d) * positions, positions)
        for f in range(frames):
            values = tokens_ref[f, pl.ds(start, positions), :].astype(jnp.float32)
            average = jnp.mean(values, axis=-1, keepdims=True)
            centered = values - average
            variance = jnp.mean(centered * centered, axis=-1, keepdims=True)
            normed = centered * lax.rsqrt(variance + EPSILON)
            result = normed * (1.0 + modulation_ref[f, 1:2, :]) + modulation_ref[f, 0:1, :]
            for t in range(width // LANES):
                mixed[t, pl.ds(f, positions, stride=frames), :] = result[:, t * LANES : (t + 1) * LANES]
        for t in range(width // LANES):
            part = mixed[t].astype(out_ref.dtype).reshape(groups, rows, LANES)
            out_ref[d // 2, :, :, t * LANES : (t + 1) * LANES] = part


def restore_kernel(index_ref, tokens_ref, modulation_ref, *refs):
    in_refs, out_ref, mixed = refs[:-2], refs[-2], refs[-1]
    frames = tokens_ref.shape[0]
    groups, rows, width = in_refs[0].shape
    positions = groups * rows // frames
    index = index_ref[0]
    for d, in_ref in enumerate(in_refs):
        start = pl.multiple_of(lax.bitwise_xor(index, d) * positions, positions)
        for t in range(width // LANES):
            part = in_ref[:, :, t * LANES : (t + 1) * LANES]
            mixed[t] = part.reshape(groups * rows, LANES).astype(jnp.float32)
        for f in range(frames):
            values = tokens_ref[f, pl.ds(start, positions), :].astype(jnp.float32)
            projected = jnp.concatenate(
                [mixed[t, pl.ds(f, positions, stride=frames), :] for t in range(width // LANES)], axis=1
            )
            result = values + modulation_ref[f, 2:3, :] * projected
            out_ref[f, pl.ds(start, positions), :] = result.astype(out_ref.dtype)


def nt_dot(left, right):
    return lax.dot_general(left, right, (((1,), (1,)), ((), ())), preferred_element_type=jnp.float32)


def head_window(head, head_size, shift):
    first = shift + head * head_size
    last = first + head_size
    low = first // LANES * LANES
    return first, last, low, padded(last)


def masked(values, first, last, low):
    lane = lax.broadcasted_iota(jnp.int32, values.shape, 1) + low
    return jnp.where((lane >= first) & (lane < last), values, jnp.zeros_like(values))


def softmax(scores, same, scale):
    scores = jnp.where(same, scores, -jnp.inf)
    top = jnp.max(scores, axis=0, keepdims=True)
    exponent = jnp.exp((scores - top) * scale)
    total = jnp.sum(exponent, axis=0, keepdims=True)
    return exponent * (1.0 / total)


def block_kernel(plan, frames, index_ref, *refs):
    kind, weights, half = plan["kind"], plan["weights"], plan["half"]
    refs = list(refs)
    x_refs = [refs.pop(0) for _ in range(plan["inputs"])]
    w_refs = [refs.pop(0) for _ in range(weights)]
    out_refs = [refs.pop(0) for _ in range(2)]
    xs, wall, qt, kn, vt, sems, wsems = refs
    groups, count, rows, width = xs.shape
    lanes = qt.shape[0]
    heads_half = H // 2
    head_size = width // H
    scale = head_size ** (-0.5)
    slot = count * rows
    index, slab = index_ref[0], index_ref[1]

    upper = index >= count // 2
    sources = []
    for d in range(count):
        owner = lax.bitwise_xor(index, d)
        source = x_refs[-1].at[d // 2, d % 2] if kind == 1 and d < count // 2 else x_refs[d // 2].at[d % 2]
        sources.append(pltpu.make_async_copy(source, xs.at[:, owner], sems.at[d]))
    choices = []
    for chosen, entries in plan["moves"]:
        moves = []
        for operand, at, size, owner, part in entries:
            source = w_refs[operand]
            for step in at:
                source = source.at[step]
            if owner is None:
                moves.append((source, wall.at[pl.ds(part * size, size)]))
                continue
            base = lax.bitwise_xor(index, owner) * plan["columns"] - kind * 3 * half
            if part is None:
                moves.append((source, wall.at[pl.ds(pl.multiple_of(base, ROWS), size)]))
                continue
            piece, over, spare = lax.bitwise_xor(slab, part[0]), plan["over"], part[1]
            ends = piece == plan["pieces"] - 1
            row = base + piece * size
            skip = jnp.where(ends, over, 0)
            moves.append((source.at[pl.ds(pl.multiple_of(skip, ROWS), size - over)],
                          wall.at[pl.ds(pl.multiple_of(row, ROWS), size - over)]))
            if over:
                row = jnp.where(ends, 3 * half + spare * over, row + size - over)
                moves.append((source.at[pl.ds(size - over, over)],
                              wall.at[pl.ds(pl.multiple_of(row, ROWS), over)]))
        moves = [pltpu.make_async_copy(a, b, wsems.at[n]) for n, (a, b) in enumerate(moves)]
        choices.append((None if chosen is None else upper == chosen, moves))

    def on_choice(act):
        for condition, moves in choices:
            if condition is None:
                for copy in moves:
                    act(copy)
            else:
                @pl.when(condition)
                def _():
                    for copy in moves:
                        act(copy)

    choices.append((None, sources))
    on_choice(lambda copy: copy.start())
    gap = lanes - half
    if gap:
        qt[half:, :] = jnp.zeros((gap, qt.shape[1]), qt.dtype)
        kn[:, half:] = jnp.zeros((kn.shape[0], gap), kn.dtype)
    on_choice(lambda copy: copy.wait())

    tokens = groups * slot
    own = xs[...].reshape(tokens, width)
    parts = [wall[n * half : (n + 1) * half, :] for n in range(3)]
    qt[:half, :] = nt_dot(parts[0], own).astype(qt.dtype)
    kn[:, :half] = nt_dot(own, parts[1]).astype(kn.dtype)
    vt[...] = nt_dot(parts[2], own).astype(vt.dtype)

    def one_group(g, carry):
        here = pl.ds(pl.multiple_of(g * slot, slot), slot)
        row = lax.broadcasted_iota(jnp.int32, (slot, slot), 0)
        column = lax.broadcasted_iota(jnp.int32, (slot, slot), 1)
        same = (row % rows) // frames == (column % rows) // frames
        scores = []
        for head in range(heads_half):
            first, last, low, high = head_window(head, head_size, 0)
            keys = masked(kn[here, low:high], first, last, low)
            scores.append(jnp.dot(keys, qt[low:high, here], preferred_element_type=jnp.float32))
        probs = [softmax(score, same, scale).astype(jnp.bfloat16) for score in scores]
        results = []
        for head, prob in enumerate(probs):
            values = vt[head * head_size : (head + 1) * head_size, here]
            results.append(jnp.dot(values, prob, preferred_element_type=jnp.float32))
        if gap:
            space = jnp.zeros((gap, slot), jnp.float32)
            results = [space] + results if kind else results + [space]
        result = jnp.concatenate(results, axis=0).T.astype(jnp.bfloat16)
        earlier, later = result[: slot // 2], result[slot // 2 :]
        out_refs[0][g] = jnp.where(upper, later, earlier).reshape(count // 2, rows, lanes)
        out_refs[1][g] = jnp.where(upper, earlier, later).reshape(count // 2, rows, lanes)
        return carry

    lax.fori_loop(0, groups, one_group, 0, unroll=True)


def project_kernel(plan, index_ref, first_near, first_far, second_near, second_far, *refs):
    count, moves = plan["count"], plan["moves"]
    refs = list(refs)
    w_refs = [refs.pop(0) for _ in range(plan["weights"])]
    out_refs = [refs.pop(0) for _ in range(count)]
    wall, ys, sems = refs
    index = index_ref[0]
    tokens = ys.shape[0] * ys.shape[1] * ys.shape[2]
    copies = []
    for n, (operand, at, owner) in enumerate(moves):
        source = w_refs[operand]
        for step in at:
            source = source.at[step]
        size = source.shape[0]
        row = pl.multiple_of(lax.bitwise_xor(index, owner[0]) * size, ROWS) if isinstance(owner, tuple) else owner * size
        copies.append(pltpu.make_async_copy(source, wall.at[pl.ds(row, size)], sems.at[n]))
    for copy in copies:
        copy.start()
    for copy in copies:
        copy.wait()
    upper = index >= count // 2

    def in_order(near_ref, far_ref):
        near, far = near_ref[...], far_ref[...]
        both = [jnp.where(upper, far, near), jnp.where(upper, near, far)]
        return jnp.concatenate(both, axis=1).reshape(tokens, -1)

    first, second = in_order(first_near, first_far), in_order(second_near, second_far)
    cut = 2 * first.shape[1] - wall.shape[1]
    parts = [first[:, : first.shape[1] - cut], first[:, first.shape[1] - cut :] + second[:, :cut], second[:, cut:]]
    attended = jnp.concatenate(parts if cut else [first, second], axis=1)
    ys[...] = nt_dot(attended, wall[...]).astype(ys.dtype).reshape(ys.shape)
    for d in range(count):
        out_refs[d][...] = ys[:, lax.bitwise_xor(index, d)]


def per_device(video_tokens, modulation, qkv_weight, out_weight):
    frames, positions, width = video_tokens.shape
    count, slabs = lax.axis_size("seq"), lax.axis_size("slab")
    index, slab = lax.axis_index("seq"), lax.axis_index("slab")
    block_positions = positions // count
    block_rows = block_positions * frames
    groups = block_rows // ROWS
    block = jax.ShapeDtypeStruct((groups, ROWS, width), jnp.bfloat16)
    own_index = jnp.stack([index, slab]).astype(jnp.int32)
    smem = pl.BlockSpec(memory_space=pltpu.SMEM)
    vmem = pl.BlockSpec(memory_space=pltpu.VMEM)
    anywhere = pl.BlockSpec(memory_space=pl.ANY)
    params = pltpu.CompilerParams(vmem_limit_bytes=VMEM_BYTES)

    def hop(value, seq_xor, slab_xor=0):
        pairs = [(s * count + i, (s ^ slab_xor) * count + (i ^ seq_xor)) for s in range(slabs) for i in range(count)]
        return lax.ppermute(value, ("slab", "seq"), pairs)

    half = width // 2
    lanes = padded(half)
    columns, outs = qkv_weight.shape[1], out_weight.shape[1]
    chips = count // 2
    middle = chips
    size = -(-columns // (slabs * ROWS)) * ROWS
    over = slabs * size - columns
    shared = columns % ROWS == 0 and outs % ROWS == 0 and over < size and chips == 4 and slabs == 4
    tie = lax.optimization_barrier

    keep, give = pl.pallas_call(
        norm_kernel,
        out_shape=[jax.ShapeDtypeStruct((chips,) + block.shape, block.dtype)] * 2,
        in_specs=[smem, vmem, vmem],
        out_specs=[vmem] * 2,
        scratch_shapes=[pltpu.VMEM((width // LANES, block_rows, LANES), jnp.float32)],
        compiler_params=params,
        name="norm",
    )(own_index, video_tokens, modulation)
    swapped = hop(give, 1)
    pair = [jnp.stack([keep[z], swapped[z]]) for z in range(chips)]

    def to_neighbour(value, step):
        pairs = [(s * count + i, (s + (step if i < middle else -step)) % slabs * count + i)
                 for s in range(slabs) for i in range(count)]
        return lax.ppermute(value, ("slab", "seq"), pairs)

    def following_of(values):
        return to_neighbour(jnp.stack(values), -1)

    wide, narrow = qkv_weight.T, out_weight.T
    out_operands, out_moves = [], []
    operands, moves = [], []
    if shared:
        mine = lax.dynamic_slice_in_dim(wide, jnp.minimum(slab * size, columns - size), size, 0)

        def with_sibling(value, entries, other):
            for sibling in range(2):
                operands.append(other if sibling else value)
                for at, length, z, part in entries:
                    part = part if part is None else (part, 2 * z + sibling)
                    moves.append((len(operands) - 1, at, length, (2 * z) ^ sibling, part))

        x, y = 1, 2
        blocks = [pair[0], None, None, None]
        far = hop(mine, 4)
        wide_other, narrow_other = hop(wide, 1), hop(narrow, 1)
        blocks[1] = hop(pair[1], 2)
        far, mine, pair, wide_other, narrow_other, blocks[1] = tie((far, mine, pair, wide_other, narrow_other, blocks[1]))
        ax, ay = hop(far, 0, x), hop(far, 0, y)
        rest = hop(jnp.stack([mine, far]), 2)
        blocks[2] = hop(pair[2], 4)
        following = following_of(blocks[:2])
        ax, ay, rest, blocks[2], following, pair[3] = tie((ax, ay, rest, blocks[2], following, pair[3]))
        bx, by = hop(rest, 0, x), hop(rest, 0, y)
        blocks[3] = hop(pair[3], 6)

        ay, bx, by, blocks[3], narrow = tie((ay, bx, by, blocks[3], narrow))
        axy = hop(ay, 0, x)
        bxy = hop(bx, 0, y)
        out_far = hop(narrow, 4)
        swaps = [hop(value, 1) for value in (far, ax, ay)]
        swaps += [None] + [hop(value, 1) for value in (rest, bx, by)]
        bxy, swaps = tie((bxy, swaps))
        swaps.append(hop(bxy, 1))
        swaps[3] = hop(axy, 1)
        with_sibling(wide, [((), columns, 0, None)], wide_other)
        for e, value in enumerate((far, ax, ay, axy)):
            with_sibling(value, [((), size, 2, e)], swaps[e])
        for e, value in enumerate((rest, bx, by, bxy)):
            with_sibling(value, [((n,), size, z, e) for n, z in enumerate((1, 3))], swaps[4 + e])
        near_half = [m for m in moves if m[3] < middle]
        far_half = [m for m in moves if m[3] >= middle]
        by_kind = [[(False, near_half), (True, far_half)], [(True, near_half), (False, far_half)]]
    else:
        operands = [lax.all_gather(wide, "seq", axis=0, tiled=True).reshape(6, half, width)]
        out_operands = [lax.all_gather(narrow, "seq", axis=0, tiled=True)]
        by_kind = [[(None, [(0, (3 * kind + n,), half, None, n) for n in range(3)])] for kind in range(2)]
        out_moves = [(0, (), 0)]
        blocks = [hop(pair[z], 2 * z) if z else pair[z] for z in range(chips)]
        following = following_of(blocks[: chips // 2])

    tokens = count * block_rows

    def attention(kind, inputs):
        plan = dict(kind=kind, weights=len(operands), inputs=len(inputs), half=half, moves=by_kind[kind],
                    columns=columns, over=over, pieces=slabs)
        copies = max(2 * len(entries) for _, entries in by_kind[kind])
        return pl.pallas_call(
            functools.partial(block_kernel, plan, frames),
            out_shape=[jax.ShapeDtypeStruct((groups, middle, ROWS, lanes), jnp.bfloat16)] * 2,
            in_specs=[smem] + [anywhere] * (len(inputs) + len(operands)),
            out_specs=[vmem] * 2,
            scratch_shapes=[
                pltpu.VMEM((groups, count, ROWS, width), jnp.bfloat16),
                pltpu.VMEM((3 * half + count * over, width), jnp.bfloat16),
                pltpu.VMEM((lanes, tokens), jnp.bfloat16),
                pltpu.VMEM((tokens, lanes), jnp.bfloat16),
                pltpu.VMEM((half, tokens), jnp.bfloat16),
                pltpu.SemaphoreType.DMA((count,)),
                pltpu.SemaphoreType.DMA((copies,)),
            ],
            compiler_params=params,
            cost_estimate=pl.CostEstimate(flops=SPACE_FLOPS, bytes_accessed=8 * 1024 * 1024,
                                          transcendentals=0),
            name=("windowed", "shifted")[kind],
        )(own_index, *inputs, *operands)

    second_near, second_far = attention(1, blocks + [following])
    if shared:
        out_rest = hop(jnp.stack([narrow, out_far]), 2)
    second_near = to_neighbour(second_near, 1)
    first_near, first_far = attention(0, blocks)
    if shared:
        out_rest, first_near, second_near = tie((out_rest, first_near, second_near))
        out_operands = [narrow, narrow_other, out_far, hop(out_far, 1), out_rest, hop(out_rest, 1)]
        out_moves = [(0, (), (0,)), (1, (), (1,)), (2, (), (4,)), (3, (), (5,)), (4, (0,), (2,)), (5, (0,), (3,)),
                     (4, (1,), (6,)), (5, (1,), (7,))]
    plan = dict(count=count, weights=len(out_operands), moves=out_moves)
    projected = pl.pallas_call(
        functools.partial(project_kernel, plan),
        out_shape=[block] * count,
        in_specs=[smem] + [vmem] * 4 + [anywhere] * len(out_operands),
        out_specs=[vmem] * count,
        scratch_shapes=[
            pltpu.VMEM((width, width), jnp.bfloat16),
            pltpu.VMEM((groups, count, ROWS, width), jnp.bfloat16),
            pltpu.SemaphoreType.DMA((len(out_moves),)),
        ],
        compiler_params=params,
        cost_estimate=pl.CostEstimate(flops=2 * tokens * width * width, bytes_accessed=4 * 1024 * 1024,
                                      transcendentals=0),
        name="project",
    )(own_index, first_near, first_far, second_near, second_far, *out_operands)
    returned = [projected[0]] + [hop(projected[d], d) for d in range(1, count)]
    return pl.pallas_call(
        restore_kernel,
        out_shape=jax.ShapeDtypeStruct(video_tokens.shape, video_tokens.dtype),
        in_specs=[smem, vmem, vmem] + [vmem] * count,
        out_specs=vmem,
        scratch_shapes=[pltpu.VMEM((width // LANES, block_rows, LANES), jnp.float32)],
        compiler_params=params,
        name="restore",
    )(own_index, video_tokens, modulation, *returned)


def solution(mesh):
    return jax.shard_map(
        per_device,
        mesh=mesh,
        in_specs=(
            P(("slab", "seq"), None, None),
            P(("slab", "seq"), None, None),
            P(None, "seq"),
            P(None, "seq"),
        ),
        out_specs=P(("slab", "seq"), None, None),
        check_vma=False,
    )
```

```python
import functools

import jax
import jax.numpy as jnp
from jax import lax
from jax.experimental import pallas as pl
from jax.experimental.pallas import tpu as pltpu
from jax.sharding import PartitionSpec as P

H = 16
FRS = 32
EPSILON = 1e-06
LANES = 128
ROWS = 16
SPACE_FLOPS = 40 * 10**9
VMEM_BYTES = 24 * 1024 * 1024


def padded(width):
    return -(-width // LANES) * LANES


def norm_kernel(index_ref, tokens_ref, modulation_ref, keep_ref, give_ref, mixed):
    frames = tokens_ref.shape[0]
    chips, groups, rows, width = keep_ref.shape
    positions = groups * rows // frames
    index = index_ref[0]
    for d in range(2 * chips):
        out_ref = (keep_ref, give_ref)[d % 2]
        start = pl.multiple_of(lax.bitwise_xor(index, d) * positions, positions)
        for f in range(frames):
            values = tokens_ref[f, pl.ds(start, positions), :].astype(jnp.float32)
            average = jnp.mean(values, axis=-1, keepdims=True)
            centered = values - average
            variance = jnp.mean(centered * centered, axis=-1, keepdims=True)
            normed = centered * lax.rsqrt(variance + EPSILON)
            result = normed * (1.0 + modulation_ref[f, 1:2, :]) + modulation_ref[f, 0:1, :]
            for t in range(width // LANES):
                mixed[t, pl.ds(f, positions, stride=frames), :] = result[:, t * LANES : (t + 1) * LANES]
        for t in range(width // LANES):
            part = mixed[t].astype(out_ref.dtype).reshape(groups, rows, LANES)
            out_ref[d // 2, :, :, t * LANES : (t + 1) * LANES] = part


def nt_dot(left, right):
    return lax.dot_general(left, right, (((1,), (1,)), ((), ())), preferred_element_type=jnp.float32)


def head_window(head, head_size, shift):
    first = shift + head * head_size
    last = first + head_size
    low = first // LANES * LANES
    return first, last, low, padded(last)


def masked(values, first, last, low):
    lane = lax.broadcasted_iota(jnp.int32, values.shape, 1) + low
    return jnp.where((lane >= first) & (lane < last), values, jnp.zeros_like(values))


def softmax(scores, same, scale):
    scores = jnp.where(same, scores, -jnp.inf)
    top = jnp.max(scores, axis=0, keepdims=True)
    exponent = jnp.exp((scores - top) * scale)
    total = jnp.sum(exponent, axis=0, keepdims=True)
    return exponent * (1.0 / total)


def piece_moves(plan, index, slab, entries, w_refs, wall, first_row, rows):
    moves = []
    for operand, at, size, owner, part in entries:
        source = w_refs[operand]
        for step in at:
            source = source.at[step]
        base = lax.bitwise_xor(index, owner) * plan["columns"] - first_row
        if part is None:
            moves.append((source, wall.at[pl.ds(pl.multiple_of(base, ROWS), size)]))
            continue
        piece, over, spare = lax.bitwise_xor(slab, part[0]), plan["over"], part[1]
        ends = piece == plan["pieces"] - 1
        row = base + piece * size
        skip = jnp.where(ends, over, 0)
        moves.append((source.at[pl.ds(pl.multiple_of(skip, ROWS), size - over)],
                      wall.at[pl.ds(pl.multiple_of(row, ROWS), size - over)]))
        if over:
            row = jnp.where(ends, rows + spare * over, row + size - over)
            moves.append((source.at[pl.ds(size - over, over)], wall.at[pl.ds(pl.multiple_of(row, ROWS), over)]))
    return moves


def gather_kernel(plan, index_ref, *refs):
    w_refs, wall, sems = refs[:-2], refs[-2], refs[-1]
    moves = piece_moves(plan, index_ref[0], index_ref[1], plan["moves"], w_refs, wall, 0, 6 * plan["half"])
    moves = [pltpu.make_async_copy(a, b, sems.at[n]) for n, (a, b) in enumerate(moves)]
    for move in moves:
        move.start()
    for move in moves:
        move.wait()


def block_kernel(plan, frames, index_ref, *refs):
    kind, weights, half = plan["kind"], plan["weights"], plan["half"]
    refs = list(refs)
    x_refs = [refs.pop(0) for _ in range(plan["inputs"])]
    full_ref = refs.pop(0)
    w_refs = [refs.pop(0) for _ in range(weights)]
    out_refs = [refs.pop(0) for _ in range(2)]
    xs, wall, qt, kn, vt, sems, full_sem, wsems = refs
    groups, count, rows, width = xs.shape
    lanes = qt.shape[0]
    heads_half = H // 2
    head_size = width // H
    scale = head_size ** (-0.5)
    slot = count * rows
    index, slab = index_ref[0], index_ref[1]
    upper = index >= count // 2
    full = pltpu.make_async_copy(full_ref.at[pl.ds(3 * kind * half, 3 * half)], wall.at[pl.ds(0, 3 * half)], full_sem.at[0])
    full.start()

    sources = []
    for d in range(count):
        owner = lax.bitwise_xor(index, d)
        source = x_refs[-1].at[d // 2, d % 2] if kind == 1 and d < count // 2 else x_refs[d // 2].at[d % 2]
        sources.append(pltpu.make_async_copy(source, xs.at[:, owner], sems.at[d]))
    for copy in sources:
        copy.start()
    full.wait()
    choices = []
    for chosen, entries in plan["moves"]:
        moves = piece_moves(plan, index, slab, entries, w_refs, wall, 3 * kind * half, 3 * half)
        choices.append((chosen, [pltpu.make_async_copy(a, b, wsems.at[n]) for n, (a, b) in enumerate(moves)]))

    def on_choice(act):
        for chosen, moves in choices:
            @pl.when(upper == chosen)
            def _():
                for copy in moves:
                    act(copy)

    on_choice(lambda copy: copy.start())
    gap = lanes - half
    if gap:
        qt[half:, :] = jnp.zeros((gap, qt.shape[1]), qt.dtype)
        kn[:, half:] = jnp.zeros((kn.shape[0], gap), kn.dtype)
    for copy in sources:
        copy.wait()
    on_choice(lambda copy: copy.wait())

    tokens = groups * slot
    own = xs[...].reshape(tokens, width)
    parts = [wall[n * half : (n + 1) * half, :] for n in range(3)]
    qt[:half, :] = nt_dot(parts[0], own).astype(qt.dtype)
    kn[:, :half] = nt_dot(own, parts[1]).astype(kn.dtype)
    vt[...] = nt_dot(parts[2], own).astype(vt.dtype)

    def one_group(g, carry):
        here = pl.ds(pl.multiple_of(g * slot, slot), slot)
        row = lax.broadcasted_iota(jnp.int32, (slot, slot), 0)
        column = lax.broadcasted_iota(jnp.int32, (slot, slot), 1)
        same = (row % rows) // frames == (column % rows) // frames
        scores = []
        for head in range(heads_half):
            first, last, low, high = head_window(head, head_size, 0)
            keys = masked(kn[here, low:high], first, last, low)
            scores.append(jnp.dot(keys, qt[low:high, here], preferred_element_type=jnp.float32))
        probs = [softmax(score, same, scale).astype(jnp.bfloat16) for score in scores]
        results = []
        for head, prob in enumerate(probs):
            values = vt[head * head_size : (head + 1) * head_size, here]
            results.append(jnp.dot(values, prob, preferred_element_type=jnp.float32))
        if gap:
            space = jnp.zeros((gap, slot), jnp.float32)
            results = [space] + results if kind else results + [space]
        result = jnp.concatenate(results, axis=0).T.astype(jnp.bfloat16)
        earlier, later = result[: slot // 2], result[slot // 2 :]
        out_refs[0][g] = jnp.where(upper, later, earlier).reshape(count // 2, rows, lanes)
        out_refs[1][g] = jnp.where(upper, earlier, later).reshape(count // 2, rows, lanes)
        return carry

    lax.fori_loop(0, groups, one_group, 0, unroll=True)


def merge_kernel(first_d, index_ref, first_ref, second_ref, *out_refs):
    index = index_ref[0]
    for n, out_ref in enumerate(out_refs):
        at = lax.rem(lax.bitwise_xor(index, first_d + n), len(out_refs))
        first, second = first_ref[:, at], second_ref[:, at]
        lanes = first.shape[-1]
        cut = 2 * lanes - out_ref.shape[-1]
        if cut:
            out_ref[..., : lanes - cut] = first[..., : lanes - cut]
            out_ref[..., lanes - cut : lanes] = first[..., lanes - cut :] + second[..., :cut]
            out_ref[..., lanes:] = second[..., cut:]
        else:
            out_ref[..., :lanes] = first
            out_ref[..., lanes:] = second


def restore_kernel(plan, index_ref, tokens_ref, modulation_ref, *refs):
    count, moves = plan["count"], plan["moves"]
    refs = list(refs)
    in_refs = [refs.pop(0) for _ in range(count)]
    w_refs = [refs.pop(0) for _ in range(plan["weights"])]
    out_ref, wall, mixed, sems = refs
    index = index_ref[0]
    copies = []
    for n, (operand, at, owner) in enumerate(moves):
        source = w_refs[operand]
        for step in at:
            source = source.at[step]
        size = source.shape[0]
        row = pl.multiple_of(lax.bitwise_xor(index, owner[0]) * size, ROWS) if isinstance(owner, tuple) else owner * size
        copies.append(pltpu.make_async_copy(source, wall.at[pl.ds(row, size)], sems.at[n]))
    for copy in copies:
        copy.start()
    for copy in copies:
        copy.wait()
    frames = tokens_ref.shape[0]
    groups, rows, width = in_refs[0].shape
    block_rows = groups * rows
    positions = block_rows // frames
    attended = jnp.concatenate([in_ref[...].reshape(block_rows, width) for in_ref in in_refs], axis=0)
    projected = nt_dot(attended, wall[...]).astype(jnp.bfloat16).astype(jnp.float32)
    for t in range(width // LANES):
        mixed[t] = projected[:, t * LANES : (t + 1) * LANES]
    for d in range(count):
        start = pl.multiple_of(lax.bitwise_xor(index, d) * positions, positions)
        for f in range(frames):
            values = tokens_ref[f, pl.ds(start, positions), :].astype(jnp.float32)
            rows_of = pl.ds(d * block_rows + f, positions, stride=frames)
            update = jnp.concatenate([mixed[t, rows_of, :] for t in range(width // LANES)], axis=1)
            result = values + modulation_ref[f, 2:3, :] * update
            out_ref[f, pl.ds(start, positions), :] = result.astype(out_ref.dtype)


def per_device(video_tokens, modulation, qkv_weight, out_weight):
    frames, positions, width = video_tokens.shape
    count, slabs = lax.axis_size("seq"), lax.axis_size("slab")
    index, slab = lax.axis_index("seq"), lax.axis_index("slab")
    block_positions = positions // count
    block_rows = block_positions * frames
    groups = block_rows // ROWS
    block = jax.ShapeDtypeStruct((groups, ROWS, width), jnp.bfloat16)
    own_index = jnp.stack([index, slab]).astype(jnp.int32)
    smem = pl.BlockSpec(memory_space=pltpu.SMEM)
    vmem = pl.BlockSpec(memory_space=pltpu.VMEM)
    anywhere = pl.BlockSpec(memory_space=pl.ANY)
    params = pltpu.CompilerParams(vmem_limit_bytes=VMEM_BYTES)

    def hop(value, seq_xor, slab_xor=0):
        pairs = [(s * count + i, (s ^ slab_xor) * count + (i ^ seq_xor)) for s in range(slabs) for i in range(count)]
        return lax.ppermute(value, ("slab", "seq"), pairs)

    half = width // 2
    lanes = padded(half)
    columns, outs = qkv_weight.shape[1], out_weight.shape[1]
    chips = count // 2
    middle = chips
    size = -(-columns // (slabs * ROWS)) * ROWS
    over = slabs * size - columns
    shared = columns % ROWS == 0 and outs % ROWS == 0 and over < size and chips == 4 and slabs == 4
    tie = lax.optimization_barrier

    keep, give = pl.pallas_call(
        norm_kernel,
        out_shape=[jax.ShapeDtypeStruct((chips,) + block.shape, block.dtype)] * 2,
        in_specs=[smem, vmem, vmem],
        out_specs=[vmem] * 2,
        scratch_shapes=[pltpu.VMEM((width // LANES, block_rows, LANES), jnp.float32)],
        compiler_params=params,
        name="norm",
    )(own_index, video_tokens, modulation)
    swapped = hop(give, 1)
    pair = [jnp.stack([keep[z], swapped[z]]) for z in range(chips)]

    def to_neighbour(value, step):
        pairs = [(s * count + i, (s + (step if i < middle else -step)) % slabs * count + i)
                 for s in range(slabs) for i in range(count)]
        return lax.ppermute(value, ("slab", "seq"), pairs)

    def following_of(values):
        return to_neighbour(jnp.stack(values), -1)

    wide, narrow = qkv_weight.T, out_weight.T
    out_operands, out_moves = [], []
    operands, moves = [], []
    if shared:
        mine = lax.dynamic_slice_in_dim(wide, jnp.minimum(slab * size, columns - size), size, 0)

        def with_sibling(value, entries, other):
            for sibling in range(2):
                operands.append(other if sibling else value)
                for at, length, z, part in entries:
                    part = part if part is None else (part, 2 * z + sibling)
                    moves.append((len(operands) - 1, at, length, (2 * z) ^ sibling, part))

        x, y = 1, 2
        blocks = [pair[0], None, None, None]
        far = hop(mine, 4)
        wide_other, narrow_other = hop(wide, 1), hop(narrow, 1)
        blocks[1] = hop(pair[1], 2)
        far, mine, pair, wide_other, narrow_other, blocks[1] = tie((far, mine, pair, wide_other, narrow_other, blocks[1]))
        ax, ay = hop(far, 0, x), hop(far, 0, y)
        rest = hop(jnp.stack([mine, far]), 2)
        blocks[2] = hop(pair[2], 4)
        following = following_of(blocks[:2])
        ax, ay, rest, blocks[2], following, narrow = tie((ax, ay, rest, blocks[2], following, narrow))
        bx, by = hop(rest, 0, x), hop(rest, 0, y)
        out_far = hop(narrow, 4)
        ay, bx, by, pair[3], out_far = tie((ay, bx, by, pair[3], out_far))
        blocks[3] = hop(pair[3], 6)
        axy = hop(ay, 0, x)
        bxy = hop(bx, 0, y)
        swaps = [hop(value, 1) for value in (far, ax, ay)]
        swaps += [None] + [hop(value, 1) for value in (rest, bx, by)]
        with_sibling(wide, [((), columns, 0, None)], wide_other)
        for e, value in enumerate((far, ax, ay)):
            with_sibling(value, [((), size, 2, e)], swaps[e])
        for e, value in enumerate((rest, bx, by)):
            with_sibling(value, [((n,), size, z, e) for n, z in enumerate((1, 3))], swaps[4 + e])
        full_rows = 6 * half + count * over
        plan = dict(half=half, columns=columns, over=over, pieces=slabs, moves=moves)
        full = pl.pallas_call(
            functools.partial(gather_kernel, plan),
            out_shape=jax.ShapeDtypeStruct((full_rows, width), jnp.bfloat16),
            in_specs=[smem] + [anywhere] * len(operands),
            out_specs=anywhere,
            scratch_shapes=[pltpu.SemaphoreType.DMA((2 * len(moves),))],
            compiler_params=params,
            cost_estimate=pl.CostEstimate(flops=2 * 10**9, bytes_accessed=8 * 1024 * 1024, transcendentals=0),
            name="gather",
        )(own_index, *operands)
        operands.clear()
        moves.clear()
        bxy, swaps, out_far, blocks[3], full = tie((bxy, swaps, out_far, blocks[3], full))
        swaps.append(hop(bxy, 1))
        swaps[3] = hop(axy, 1)
        with_sibling(axy, [((), size, 2, 3)], swaps[3])
        with_sibling(bxy, [((n,), size, z, 3) for n, z in enumerate((1, 3))], swaps[7])
        near_half = [m for m in moves if m[3] < middle]
        far_half = [m for m in moves if m[3] >= middle]
        by_kind = [[(False, near_half), (True, far_half)], [(True, near_half), (False, far_half)]]
    else:
        full = lax.all_gather(wide, "seq", axis=0, tiled=True)
        by_kind = [[], []]
        out_operands = [lax.all_gather(narrow, "seq", axis=0, tiled=True)]
        out_moves = [(0, (), 0)]
        blocks = [hop(pair[z], 2 * z) if z else pair[z] for z in range(chips)]
        following = following_of(blocks[: chips // 2])

    tokens = count * block_rows

    def attention(kind, inputs):
        plan = dict(kind=kind, weights=len(operands), inputs=len(inputs), half=half, moves=by_kind[kind],
                    columns=columns, over=over, pieces=slabs)
        copies = max([1] + [2 * len(entries) for _, entries in by_kind[kind]])
        return pl.pallas_call(
            functools.partial(block_kernel, plan, frames),
            out_shape=[jax.ShapeDtypeStruct((groups, middle, ROWS, lanes), jnp.bfloat16)] * 2,
            in_specs=[smem] + [anywhere] * (len(inputs) + 1 + len(operands)),
            out_specs=[vmem] * 2,
            scratch_shapes=[
                pltpu.VMEM((groups, count, ROWS, width), jnp.bfloat16),
                pltpu.VMEM((3 * half + count * over, width), jnp.bfloat16),
                pltpu.VMEM((lanes, tokens), jnp.bfloat16),
                pltpu.VMEM((tokens, lanes), jnp.bfloat16),
                pltpu.VMEM((half, tokens), jnp.bfloat16),
                pltpu.SemaphoreType.DMA((count,)),
                pltpu.SemaphoreType.DMA((1,)),
                pltpu.SemaphoreType.DMA((copies,)),
            ],
            compiler_params=params,
            cost_estimate=pl.CostEstimate(flops=SPACE_FLOPS, bytes_accessed=8 * 1024 * 1024,
                                          transcendentals=0),
            name=("windowed", "shifted")[kind],
        )(own_index, *inputs, full, *operands)

    second_near, second_far = attention(1, blocks + [following])
    if shared:
        out_rest = hop(jnp.stack([narrow, out_far]), 2)
    second_near = to_neighbour(second_near, 1)
    first_near, first_far = attention(0, blocks)
    if shared:
        out_rest, first_near, first_far, second_near = tie((out_rest, first_near, first_far, second_near))
        out_operands = [narrow, narrow_other, out_far, hop(out_far, 1), out_rest, hop(out_rest, 1)]
        out_moves = [(0, (), (0,)), (1, (), (1,)), (2, (), (4,)), (3, (), (5,)), (4, (0,), (2,)), (5, (0,), (3,)),
                     (4, (1,), (6,)), (5, (1,), (7,))]

    def merged(first_d, first, second, flops):
        return pl.pallas_call(
            functools.partial(merge_kernel, first_d),
            out_shape=[block] * middle,
            in_specs=[smem] + [vmem] * 2,
            out_specs=[vmem] * middle,
            compiler_params=params,
            cost_estimate=pl.CostEstimate(flops=flops, bytes_accessed=4 * 1024 * 1024, transcendentals=0),
            name="merge",
        )(own_index, first, second)

    sent_far = merged(middle, first_far, second_far, 0)
    sent_near = merged(0, first_near, second_near, 0)
    sent_far, sent_near, out_operands = tie((sent_far, sent_near, out_operands))
    returned = [sent_near[0]] + [hop(sent_near[d], d) for d in range(1, middle)]
    returned += [hop(value, middle + n) for n, value in enumerate(sent_far)]
    plan = dict(count=count, weights=len(out_operands), moves=out_moves)
    return pl.pallas_call(
        functools.partial(restore_kernel, plan),
        out_shape=jax.ShapeDtypeStruct(video_tokens.shape, video_tokens.dtype),
        in_specs=[smem, vmem, vmem] + [vmem] * count + [anywhere] * len(out_operands),
        out_specs=vmem,
        scratch_shapes=[
            pltpu.VMEM((width, width), jnp.bfloat16),
            pltpu.VMEM((width // LANES, tokens, LANES), jnp.float32),
            pltpu.SemaphoreType.DMA((len(out_moves),)),
        ],
        compiler_params=params,
        name="restore",
    )(own_index, video_tokens, modulation, *returned, *out_operands)


def solution(mesh):
    return jax.shard_map(
        per_device,
        mesh=mesh,
        in_specs=(
            P(("slab", "seq"), None, None),
            P(("slab", "seq"), None, None),
            P(None, "seq"),
            P(None, "seq"),
        ),
        out_specs=P(("slab", "seq"), None, None),
        check_vma=False,
    )
```

```python
import functools

import jax
import jax.numpy as jnp
from jax import lax
from jax.experimental import pallas as pl
from jax.experimental.pallas import tpu as pltpu
from jax.sharding import PartitionSpec as P

H = 16
FRS = 32
EPSILON = 1e-06
LANES = 128
ROWS = 16
SPACE_FLOPS = 40 * 10**9
VMEM_BYTES = 24 * 1024 * 1024


def padded(width):
    return -(-width // LANES) * LANES


def norm_kernel(index_ref, tokens_ref, modulation_ref, keep_ref, give_ref, mixed):
    frames = tokens_ref.shape[0]
    chips, groups, rows, width = keep_ref.shape
    positions = groups * rows // frames
    index = index_ref[0]
    for d in range(2 * chips):
        out_ref = (keep_ref, give_ref)[d % 2]
        start = pl.multiple_of(lax.bitwise_xor(index, d) * positions, positions)
        for f in range(frames):
            values = tokens_ref[f, pl.ds(start, positions), :].astype(jnp.float32)
            average = jnp.mean(values, axis=-1, keepdims=True)
            centered = values - average
            variance = jnp.mean(centered * centered, axis=-1, keepdims=True)
            normed = centered * lax.rsqrt(variance + EPSILON)
            result = normed * (1.0 + modulation_ref[1, f : f + 1, :]) + modulation_ref[0, f : f + 1, :]
            for t in range(width // LANES):
                mixed[t, pl.ds(f, positions, stride=frames), :] = result[:, t * LANES : (t + 1) * LANES]
        for t in range(width // LANES):
            part = mixed[t].astype(out_ref.dtype).reshape(groups, rows, LANES)
            out_ref[d // 2, :, :, t * LANES : (t + 1) * LANES] = part


def nt_dot(left, right):
    return lax.dot_general(left, right, (((1,), (1,)), ((), ())), preferred_element_type=jnp.float32)


def head_window(head, head_size, shift):
    first = shift + head * head_size
    last = first + head_size
    low = first // LANES * LANES
    return first, last, low, padded(last)


def masked(values, first, last, low):
    lane = lax.broadcasted_iota(jnp.int32, values.shape, 1) + low
    return jnp.where((lane >= first) & (lane < last), values, jnp.zeros_like(values))


def softmax(scores, same, scale):
    scores = jnp.where(same, scores, -jnp.inf)
    top = jnp.max(scores, axis=0, keepdims=True)
    exponent = jnp.exp((scores - top) * scale)
    total = jnp.sum(exponent, axis=0, keepdims=True)
    return exponent * (1.0 / total)


def piece_moves(plan, index, slab, entries, w_refs, wall, first_row, rows):
    moves = []
    for operand, at, size, owner, part in entries:
        source = w_refs[operand]
        for step in at:
            source = source.at[step]
        base = lax.bitwise_xor(index, owner) * plan["columns"] - first_row
        if part is None:
            moves.append((source, wall.at[pl.ds(pl.multiple_of(base, ROWS), size)]))
            continue
        piece, over, spare = lax.bitwise_xor(slab, part[0]), plan["over"], part[1]
        ends = piece == plan["pieces"] - 1
        row = base + piece * size
        skip = jnp.where(ends, over, 0)
        moves.append((source.at[pl.ds(pl.multiple_of(skip, ROWS), size - over)],
                      wall.at[pl.ds(pl.multiple_of(row, ROWS), size - over)]))
        if over:
            row = jnp.where(ends, rows + spare * over, row + size - over)
            moves.append((source.at[pl.ds(size - over, over)], wall.at[pl.ds(pl.multiple_of(row, ROWS), over)]))
    return moves


def gather_kernel(plan, index_ref, *refs):
    w_refs, wall, sems = refs[:-2], refs[-2], refs[-1]
    moves = piece_moves(plan, index_ref[0], index_ref[1], plan["moves"], w_refs, wall, 0, 6 * plan["half"])
    moves = [pltpu.make_async_copy(a, b, sems.at[n]) for n, (a, b) in enumerate(moves)]
    for move in moves:
        move.start()
    for move in moves:
        move.wait()


def block_kernel(plan, frames, index_ref, *refs):
    kind, weights, half = plan["kind"], plan["weights"], plan["half"]
    refs = list(refs)
    x_refs = [refs.pop(0) for _ in range(plan["inputs"])]
    full_ref = refs.pop(0)
    w_refs = [refs.pop(0) for _ in range(weights)]
    out_refs = [refs.pop(0) for _ in range(2)]
    xs, wall, qt, kn, vt, sems, full_sem, wsems = refs
    groups, count, rows, width = xs.shape
    lanes = qt.shape[0]
    heads_half = H // 2
    head_size = width // H
    scale = head_size ** (-0.5)
    slot = count * rows
    index, slab = index_ref[0], index_ref[1]
    upper = index >= count // 2
    full = pltpu.make_async_copy(full_ref.at[pl.ds(3 * kind * half, 3 * half)], wall.at[pl.ds(0, 3 * half)], full_sem.at[0])
    full.start()

    sources = []
    for d in range(count):
        owner = lax.bitwise_xor(index, d)
        source = x_refs[-1].at[d // 2, d % 2] if kind == 1 and d < count // 2 else x_refs[d // 2].at[d % 2]
        sources.append(pltpu.make_async_copy(source, xs.at[:, owner], sems.at[d]))
    for copy in sources:
        copy.start()
    full.wait()
    choices = []
    for chosen, entries in plan["moves"]:
        moves = piece_moves(plan, index, slab, entries, w_refs, wall, 3 * kind * half, 3 * half)
        choices.append((chosen, [pltpu.make_async_copy(a, b, wsems.at[n]) for n, (a, b) in enumerate(moves)]))

    def on_choice(act):
        for chosen, moves in choices:
            @pl.when(upper == chosen)
            def _():
                for copy in moves:
                    act(copy)

    on_choice(lambda copy: copy.start())
    gap = lanes - half
    if gap:
        qt[half:, :] = jnp.zeros((gap, qt.shape[1]), qt.dtype)
        kn[:, half:] = jnp.zeros((kn.shape[0], gap), kn.dtype)
    for copy in sources:
        copy.wait()
    on_choice(lambda copy: copy.wait())

    tokens = groups * slot
    own = xs[...].reshape(tokens, width)
    parts = [wall[n * half : (n + 1) * half, :] for n in range(3)]
    qt[:half, :] = nt_dot(parts[0], own).astype(qt.dtype)
    kn[:, :half] = nt_dot(own, parts[1]).astype(kn.dtype)
    vt[...] = nt_dot(parts[2], own).astype(vt.dtype)

    def one_group(g, carry):
        here = pl.ds(pl.multiple_of(g * slot, slot), slot)
        row = lax.broadcasted_iota(jnp.int32, (slot, slot), 0)
        column = lax.broadcasted_iota(jnp.int32, (slot, slot), 1)
        same = (row % rows) // frames == (column % rows) // frames
        scores = []
        for head in range(heads_half):
            first, last, low, high = head_window(head, head_size, 0)
            keys = masked(kn[here, low:high], first, last, low)
            scores.append(jnp.dot(keys, qt[low:high, here], preferred_element_type=jnp.float32))
        probs = [softmax(score, same, scale).astype(jnp.bfloat16) for score in scores]
        results = []
        for head, prob in enumerate(probs):
            values = vt[head * head_size : (head + 1) * head_size, here]
            results.append(jnp.dot(values, prob, preferred_element_type=jnp.float32))
        if gap:
            space = jnp.zeros((gap, slot), jnp.float32)
            results = [space] + results if kind else results + [space]
        result = jnp.concatenate(results, axis=0).T.astype(jnp.bfloat16)
        earlier, later = result[: slot // 2], result[slot // 2 :]
        out_refs[0][g] = jnp.where(upper, later, earlier).reshape(count // 2, rows, lanes)
        out_refs[1][g] = jnp.where(upper, earlier, later).reshape(count // 2, rows, lanes)
        return carry

    lax.fori_loop(0, groups, one_group, 0, unroll=True)


def merge_kernel(first_z, index_ref, first_ref, second_ref, *out_refs):
    index = index_ref[0]
    lanes = first_ref.shape[-1]
    for n, out_ref in enumerate(out_refs):
        cut = 2 * lanes - out_ref.shape[-1]
        for sibling in range(2):
            at = lax.rem(lax.bitwise_xor(index, 2 * (first_z + n) + sibling), 2 * len(out_refs))
            first, second = first_ref[:, at], second_ref[:, at]
            if cut:
                out_ref[sibling, ..., : lanes - cut] = first[..., : lanes - cut]
                out_ref[sibling, ..., lanes - cut : lanes] = first[..., lanes - cut :] + second[..., :cut]
                out_ref[sibling, ..., lanes:] = second[..., cut:]
            else:
                out_ref[sibling, ..., :lanes] = first
                out_ref[sibling, ..., lanes:] = second


def restore_kernel(plan, index_ref, tokens_ref, modulation_ref, *refs):
    count, moves = plan["count"], plan["moves"]
    refs = list(refs)
    in_refs = [refs.pop(0).at[n % 2] for n in range(count)]
    w_refs = [refs.pop(0) for _ in range(plan["weights"])]
    out_ref, wall, mixed, sems = refs
    index = index_ref[0]
    copies = []
    for n, (operand, at, owner) in enumerate(moves):
        source = w_refs[operand]
        for step in at:
            source = source.at[step]
        size = source.shape[0]
        row = pl.multiple_of(lax.bitwise_xor(index, owner[0]) * size, ROWS) if isinstance(owner, tuple) else owner * size
        copies.append(pltpu.make_async_copy(source, wall.at[pl.ds(row, size)], sems.at[n]))
    for copy in copies:
        copy.start()
    for copy in copies:
        copy.wait()
    frames = tokens_ref.shape[0]
    groups, rows, width = in_refs[0].shape
    block_rows = groups * rows
    positions = block_rows // frames
    attended = jnp.concatenate([in_ref[...].reshape(block_rows, width) for in_ref in in_refs], axis=0)
    projected = nt_dot(attended, wall[...]).astype(jnp.bfloat16).astype(jnp.float32)
    for t in range(width // LANES):
        mixed[t] = projected[:, t * LANES : (t + 1) * LANES]
    for d in range(count):
        start = pl.multiple_of(lax.bitwise_xor(index, d) * positions, positions)
        for f in range(frames):
            values = tokens_ref[f, pl.ds(start, positions), :].astype(jnp.float32)
            rows_of = pl.ds(d * block_rows + f, positions, stride=frames)
            update = jnp.concatenate([mixed[t, rows_of, :] for t in range(width // LANES)], axis=1)
            result = values + modulation_ref[2, f : f + 1, :] * update
            out_ref[f, pl.ds(start, positions), :] = result.astype(out_ref.dtype)


def per_device(video_tokens, modulation, qkv_weight, out_weight):
    frames, positions, width = video_tokens.shape
    count, slabs = lax.axis_size("seq"), lax.axis_size("slab")
    index, slab = lax.axis_index("seq"), lax.axis_index("slab")
    block_positions = positions // count
    block_rows = block_positions * frames
    groups = block_rows // ROWS
    block = jax.ShapeDtypeStruct((groups, ROWS, width), jnp.bfloat16)
    own_index = jnp.stack([index, slab]).astype(jnp.int32)
    kinds = jnp.transpose(modulation, (1, 0, 2))
    smem = pl.BlockSpec(memory_space=pltpu.SMEM)
    vmem = pl.BlockSpec(memory_space=pltpu.VMEM)
    anywhere = pl.BlockSpec(memory_space=pl.ANY)
    params = pltpu.CompilerParams(vmem_limit_bytes=VMEM_BYTES)

    def hop(value, seq_xor, slab_xor=0):
        pairs = [(s * count + i, (s ^ slab_xor) * count + (i ^ seq_xor)) for s in range(slabs) for i in range(count)]
        return lax.ppermute(value, ("slab", "seq"), pairs)

    half = width // 2
    lanes = padded(half)
    columns, outs = qkv_weight.shape[1], out_weight.shape[1]
    chips = count // 2
    middle = chips
    size = -(-columns // (slabs * ROWS)) * ROWS
    over = slabs * size - columns
    shared = columns % ROWS == 0 and outs % ROWS == 0 and over < size and chips == 4 and slabs == 4
    tie = lax.optimization_barrier

    keep, give = pl.pallas_call(
        norm_kernel,
        out_shape=[jax.ShapeDtypeStruct((chips,) + block.shape, block.dtype)] * 2,
        in_specs=[smem, vmem, vmem],
        out_specs=[vmem] * 2,
        scratch_shapes=[pltpu.VMEM((width // LANES, block_rows, LANES), jnp.float32)],
        compiler_params=params,
        name="norm",
    )(own_index, video_tokens, kinds)
    swapped = hop(give, 1)
    pair = [jnp.stack([keep[z], swapped[z]]) for z in range(chips)]

    def to_neighbour(value, step):
        pairs = [(s * count + i, (s + (step if i < middle else -step)) % slabs * count + i)
                 for s in range(slabs) for i in range(count)]
        return lax.ppermute(value, ("slab", "seq"), pairs)

    def following_of(values):
        return to_neighbour(jnp.stack(values), -1)

    wide, narrow = qkv_weight.T, out_weight.T
    out_operands, out_moves = [], []
    operands, moves = [], []
    if shared:
        mine = lax.dynamic_slice_in_dim(wide, jnp.minimum(slab * size, columns - size), size, 0)

        def with_sibling(value, entries, other):
            for sibling in range(2):
                operands.append(other if sibling else value)
                for at, length, z, part in entries:
                    part = part if part is None else (part, 2 * z + sibling)
                    moves.append((len(operands) - 1, at, length, (2 * z) ^ sibling, part))

        x, y = 1, 2
        blocks = [pair[0], None, None, None]
        far = hop(mine, 4)
        wide_other, narrow_other = hop(wide, 1), hop(narrow, 1)
        blocks[1] = hop(pair[1], 2)
        far, mine, pair, wide_other, narrow_other, blocks[1] = tie((far, mine, pair, wide_other, narrow_other, blocks[1]))
        ax, ay = hop(far, 0, x), hop(far, 0, y)
        rest = hop(jnp.stack([mine, far]), 2)
        blocks[2] = hop(pair[2], 4)
        following = following_of(blocks[:2])
        ax, ay, rest, blocks[2], following, narrow = tie((ax, ay, rest, blocks[2], following, narrow))
        bx, by = hop(rest, 0, x), hop(rest, 0, y)
        out_far = hop(narrow, 4)
        ay, bx, by, pair[3], out_far = tie((ay, bx, by, pair[3], out_far))
        blocks[3] = hop(pair[3], 6)
        axy = hop(ay, 0, x)
        bxy = hop(bx, 0, y)
        swaps = [hop(value, 1) for value in (far, ax, ay)]
        swaps += [None] + [hop(value, 1) for value in (rest, bx, by)]
        with_sibling(wide, [((), columns, 0, None)], wide_other)
        for e, value in enumerate((far, ax, ay)):
            with_sibling(value, [((), size, 2, e)], swaps[e])
        for e, value in enumerate((rest, bx, by)):
            with_sibling(value, [((n,), size, z, e) for n, z in enumerate((1, 3))], swaps[4 + e])
        full_rows = 6 * half + count * over
        plan = dict(half=half, columns=columns, over=over, pieces=slabs, moves=moves)
        full = pl.pallas_call(
            functools.partial(gather_kernel, plan),
            out_shape=jax.ShapeDtypeStruct((full_rows, width), jnp.bfloat16),
            in_specs=[smem] + [anywhere] * len(operands),
            out_specs=anywhere,
            scratch_shapes=[pltpu.SemaphoreType.DMA((2 * len(moves),))],
            compiler_params=params,
            cost_estimate=pl.CostEstimate(flops=2 * 10**9, bytes_accessed=8 * 1024 * 1024, transcendentals=0),
            name="gather",
        )(own_index, *operands)
        operands.clear()
        moves.clear()
        bxy, swaps, out_far, blocks[3], full = tie((bxy, swaps, out_far, blocks[3], full))
        swaps.append(hop(bxy, 1))
        swaps[3] = hop(axy, 1)
        with_sibling(axy, [((), size, 2, 3)], swaps[3])
        with_sibling(bxy, [((n,), size, z, 3) for n, z in enumerate((1, 3))], swaps[7])
        near_half = [m for m in moves if m[3] < middle]
        far_half = [m for m in moves if m[3] >= middle]
        by_kind = [[(False, near_half), (True, far_half)], [(True, near_half), (False, far_half)]]
    else:
        full = lax.all_gather(wide, "seq", axis=0, tiled=True)
        by_kind = [[], []]
        out_operands = [lax.all_gather(narrow, "seq", axis=0, tiled=True)]
        out_moves = [(0, (), 0)]
        blocks = [hop(pair[z], 2 * z) if z else pair[z] for z in range(chips)]
        following = following_of(blocks[: chips // 2])

    tokens = count * block_rows

    def attention(kind, inputs):
        plan = dict(kind=kind, weights=len(operands), inputs=len(inputs), half=half, moves=by_kind[kind],
                    columns=columns, over=over, pieces=slabs)
        copies = max([1] + [2 * len(entries) for _, entries in by_kind[kind]])
        return pl.pallas_call(
            functools.partial(block_kernel, plan, frames),
            out_shape=[jax.ShapeDtypeStruct((groups, middle, ROWS, lanes), jnp.bfloat16)] * 2,
            in_specs=[smem] + [anywhere] * (len(inputs) + 1 + len(operands)),
            out_specs=[vmem] * 2,
            scratch_shapes=[
                pltpu.VMEM((groups, count, ROWS, width), jnp.bfloat16),
                pltpu.VMEM((3 * half + count * over, width), jnp.bfloat16),
                pltpu.VMEM((lanes, tokens), jnp.bfloat16),
                pltpu.VMEM((tokens, lanes), jnp.bfloat16),
                pltpu.VMEM((half, tokens), jnp.bfloat16),
                pltpu.SemaphoreType.DMA((count,)),
                pltpu.SemaphoreType.DMA((1,)),
                pltpu.SemaphoreType.DMA((copies,)),
            ],
            compiler_params=params,
            cost_estimate=pl.CostEstimate(flops=SPACE_FLOPS, bytes_accessed=8 * 1024 * 1024,
                                          transcendentals=0),
            name=("windowed", "shifted")[kind],
        )(own_index, *inputs, full, *operands)

    second_near, second_far = attention(1, blocks + [following])
    if shared:
        out_rest = hop(jnp.stack([narrow, out_far]), 2)
    second_near = to_neighbour(second_near, 1)
    first_near, first_far = attention(0, blocks)
    def merged(first_z, first, second, flops):
        return pl.pallas_call(
            functools.partial(merge_kernel, first_z),
            out_shape=[jax.ShapeDtypeStruct((2,) + block.shape, block.dtype)] * (chips // 2),
            in_specs=[smem] + [vmem] * 2,
            out_specs=[vmem] * (chips // 2),
            compiler_params=params,
            cost_estimate=pl.CostEstimate(flops=flops, bytes_accessed=4 * 1024 * 1024, transcendentals=0),
            name="merge",
        )(own_index, first, second)

    sent_far = merged(chips // 2, first_far, second_far, 0)
    sent_near = merged(0, first_near, second_near, 0)
    sent = sent_near + sent_far
    arrived = [hop(sent[z], 2 * z) if z else sent[z] for z in range(chips)]
    if shared:
        out_rest, arrived = tie((out_rest, arrived))
    returned = []
    for value in arrived:
        returned += [value, hop(value, 1)]
    if shared:
        out_operands = [narrow, narrow_other, out_far, hop(out_far, 1), out_rest, hop(out_rest, 1)]
        out_moves = [(0, (), (0,)), (1, (), (1,)), (2, (), (4,)), (3, (), (5,)), (4, (0,), (2,)), (5, (0,), (3,)),
                     (4, (1,), (6,)), (5, (1,), (7,))]

    plan = dict(count=count, weights=len(out_operands), moves=out_moves)
    return pl.pallas_call(
        functools.partial(restore_kernel, plan),
        out_shape=jax.ShapeDtypeStruct(video_tokens.shape, video_tokens.dtype),
        in_specs=[smem, vmem, vmem] + [vmem] * count + [anywhere] * len(out_operands),
        out_specs=vmem,
        scratch_shapes=[
            pltpu.VMEM((width, width), jnp.bfloat16),
            pltpu.VMEM((width // LANES, tokens, LANES), jnp.float32),
            pltpu.SemaphoreType.DMA((len(out_moves),)),
        ],
        compiler_params=params,
        name="restore",
    )(own_index, video_tokens, kinds, *returned, *out_operands)


def solution(mesh):
    return jax.shard_map(
        per_device,
        mesh=mesh,
        in_specs=(
            P(("slab", "seq"), None, None),
            P(("slab", "seq"), None, None),
            P(None, "seq"),
            P(None, "seq"),
        ),
        out_specs=P(("slab", "seq"), None, None),
        check_vma=False,
    )
```

```python
import functools

import jax
import jax.numpy as jnp
from jax import lax
from jax.experimental import pallas as pl
from jax.experimental.pallas import tpu as pltpu
from jax.sharding import PartitionSpec as P

H = 16
FRS = 32
EPSILON = 1e-06
LANES = 128
ROWS = 16
SPACE_FLOPS = 40 * 10**9
VMEM_BYTES = 24 * 1024 * 1024


def padded(width):
    return -(-width // LANES) * LANES


def norm_kernel(index_ref, tokens_ref, modulation_ref, keep_ref, give_ref, mixed):
    frames = tokens_ref.shape[0]
    chips, groups, rows, width = keep_ref.shape
    positions = groups * rows // frames
    index = index_ref[0]
    for d in range(2 * chips):
        out_ref = (keep_ref, give_ref)[d % 2]
        start = pl.multiple_of(lax.bitwise_xor(index, d) * positions, positions)
        for f in range(frames):
            values = tokens_ref[f, pl.ds(start, positions), :].astype(jnp.float32)
            average = jnp.mean(values, axis=-1, keepdims=True)
            centered = values - average
            variance = jnp.mean(centered * centered, axis=-1, keepdims=True)
            normed = centered * lax.rsqrt(variance + EPSILON)
            result = normed * (1.0 + modulation_ref[1, f : f + 1, :]) + modulation_ref[0, f : f + 1, :]
            for t in range(width // LANES):
                mixed[t, pl.ds(f, positions, stride=frames), :] = result[:, t * LANES : (t + 1) * LANES]
        for t in range(width // LANES):
            part = mixed[t].astype(out_ref.dtype).reshape(groups, rows, LANES)
            out_ref[d // 2, :, :, t * LANES : (t + 1) * LANES] = part


def nt_dot(left, right):
    return lax.dot_general(left, right, (((1,), (1,)), ((), ())), preferred_element_type=jnp.float32)


def head_window(head, head_size, shift):
    first = shift + head * head_size
    last = first + head_size
    low = first // LANES * LANES
    return first, last, low, padded(last)


def masked(values, first, last, low):
    lane = lax.broadcasted_iota(jnp.int32, values.shape, 1) + low
    return jnp.where((lane >= first) & (lane < last), values, jnp.zeros_like(values))


def softmax(scores, same, scale):
    scores = jnp.where(same, scores, -jnp.inf)
    top = jnp.max(scores, axis=0, keepdims=True)
    exponent = jnp.exp((scores - top) * scale)
    total = jnp.sum(exponent, axis=0, keepdims=True)
    return exponent * (1.0 / total)


def piece_moves(plan, index, slab, entries, w_refs, wall, first_row, rows):
    moves = []
    for operand, at, size, owner, part in entries:
        source = w_refs[operand]
        for step in at:
            source = source.at[step]
        base = lax.bitwise_xor(index, owner) * plan["columns"] - first_row
        if part is None:
            moves.append((source, wall.at[pl.ds(pl.multiple_of(base, ROWS), size)]))
            continue
        piece, over, spare = lax.bitwise_xor(slab, part[0]), plan["over"], part[1]
        ends = piece == plan["pieces"] - 1
        row = base + piece * size
        skip = jnp.where(ends, over, 0)
        moves.append((source.at[pl.ds(pl.multiple_of(skip, ROWS), size - over)],
                      wall.at[pl.ds(pl.multiple_of(row, ROWS), size - over)]))
        if over:
            row = jnp.where(ends, rows + spare * over, row + size - over)
            moves.append((source.at[pl.ds(size - over, over)], wall.at[pl.ds(pl.multiple_of(row, ROWS), over)]))
    return moves


def gather_kernel(plan, index_ref, *refs):
    w_refs, wall, sems = refs[:-2], refs[-2], refs[-1]
    moves = piece_moves(plan, index_ref[0], index_ref[1], plan["moves"], w_refs, wall, 0, 6 * plan["half"])
    moves = [pltpu.make_async_copy(a, b, sems.at[n]) for n, (a, b) in enumerate(moves)]
    for move in moves:
        move.start()
    for move in moves:
        move.wait()


def block_kernel(plan, frames, index_ref, *refs):
    kind, weights, half = plan["kind"], plan["weights"], plan["half"]
    refs = list(refs)
    x_refs = [refs.pop(0) for _ in range(plan["inputs"])]
    full_ref = refs.pop(0)
    w_refs = [refs.pop(0) for _ in range(weights)]
    out_refs = [refs.pop(0) for _ in range(2)]
    xs, wall, qt, kn, vt, sems, full_sem, wsems = refs
    groups, count, rows, width = xs.shape
    lanes = qt.shape[0]
    heads_half = H // 2
    head_size = width // H
    scale = head_size ** (-0.5)
    slot = count * rows
    index, slab = index_ref[0], index_ref[1]
    upper = index >= count // 2
    full = pltpu.make_async_copy(full_ref.at[pl.ds(3 * kind * half, 3 * half)], wall.at[pl.ds(0, 3 * half)], full_sem.at[0])
    full.start()

    sources = []
    for d in range(count):
        owner = lax.bitwise_xor(index, d)
        near = kind == 1 and d < count // 2
        source = (x_refs[-1] if near else x_refs[d // 2]).at[pl.ds((d if near else d % 2) * groups, groups)]
        sources.append(pltpu.make_async_copy(source, xs.at[:, owner], sems.at[d]))
    for copy in sources:
        copy.start()
    full.wait()
    choices = []
    for chosen, entries in plan["moves"]:
        moves = piece_moves(plan, index, slab, entries, w_refs, wall, 3 * kind * half, 3 * half)
        choices.append((chosen, [pltpu.make_async_copy(a, b, wsems.at[n]) for n, (a, b) in enumerate(moves)]))

    def on_choice(act):
        for chosen, moves in choices:
            @pl.when(upper == chosen)
            def _():
                for copy in moves:
                    act(copy)

    on_choice(lambda copy: copy.start())
    gap = lanes - half
    if gap:
        qt[half:, :] = jnp.zeros((gap, qt.shape[1]), qt.dtype)
        kn[:, half:] = jnp.zeros((kn.shape[0], gap), kn.dtype)
    for copy in sources:
        copy.wait()
    on_choice(lambda copy: copy.wait())

    tokens = groups * slot
    own = xs[...].reshape(tokens, width)
    parts = [wall[n * half : (n + 1) * half, :] for n in range(3)]
    qt[:half, :] = nt_dot(parts[0], own).astype(qt.dtype)
    kn[:, :half] = nt_dot(own, parts[1]).astype(kn.dtype)
    vt[...] = nt_dot(parts[2], own).astype(vt.dtype)

    def one_group(g, carry):
        here = pl.ds(pl.multiple_of(g * slot, slot), slot)
        row = lax.broadcasted_iota(jnp.int32, (slot, slot), 0)
        column = lax.broadcasted_iota(jnp.int32, (slot, slot), 1)
        same = (row % rows) // frames == (column % rows) // frames
        scores = []
        for head in range(heads_half):
            first, last, low, high = head_window(head, head_size, 0)
            keys = masked(kn[here, low:high], first, last, low)
            scores.append(jnp.dot(keys, qt[low:high, here], preferred_element_type=jnp.float32))
        probs = [softmax(score, same, scale).astype(jnp.bfloat16) for score in scores]
        results = []
        for head, prob in enumerate(probs):
            values = vt[head * head_size : (head + 1) * head_size, here]
            results.append(jnp.dot(values, prob, preferred_element_type=jnp.float32))
        if gap:
            space = jnp.zeros((gap, slot), jnp.float32)
            results = [space] + results if kind else results + [space]
        result = jnp.concatenate(results, axis=0).T.astype(jnp.bfloat16)
        earlier, later = result[: slot // 2], result[slot // 2 :]
        out_refs[0][g] = jnp.where(upper, later, earlier).reshape(count // 2, rows, lanes)
        out_refs[1][g] = jnp.where(upper, earlier, later).reshape(count // 2, rows, lanes)
        return carry

    lax.fori_loop(0, groups, one_group, 0, unroll=True)


def merge_kernel(first_z, index_ref, first_ref, second_ref, *out_refs):
    index = index_ref[0]
    lanes = first_ref.shape[-1]
    for n, out_ref in enumerate(out_refs):
        cut = 2 * lanes - out_ref.shape[-1]
        for sibling in range(2):
            at = lax.rem(lax.bitwise_xor(index, 2 * (first_z + n) + sibling), 2 * len(out_refs))
            first, second = first_ref[:, at], second_ref[:, at]
            if cut:
                out_ref[sibling, ..., : lanes - cut] = first[..., : lanes - cut]
                out_ref[sibling, ..., lanes - cut : lanes] = first[..., lanes - cut :] + second[..., :cut]
                out_ref[sibling, ..., lanes:] = second[..., cut:]
            else:
                out_ref[sibling, ..., :lanes] = first
                out_ref[sibling, ..., lanes:] = second


def restore_kernel(plan, index_ref, tokens_ref, modulation_ref, *refs):
    count, moves = plan["count"], plan["moves"]
    refs = list(refs)
    in_refs = [refs.pop(0) for _ in range(count)]
    in_refs = [ref.at[n % ref.shape[0]] for n, ref in enumerate(in_refs)]
    w_refs = [refs.pop(0) for _ in range(plan["weights"])]
    out_ref, wall, mixed, sems = refs
    index = index_ref[0]
    copies = []
    for n, (operand, at, owner) in enumerate(moves):
        source = w_refs[operand]
        for step in at:
            source = source.at[step]
        size = source.shape[0]
        row = pl.multiple_of(lax.bitwise_xor(index, owner[0]) * size, ROWS) if isinstance(owner, tuple) else owner * size
        copies.append(pltpu.make_async_copy(source, wall.at[pl.ds(row, size)], sems.at[n]))
    for copy in copies:
        copy.start()
    for copy in copies:
        copy.wait()
    frames = tokens_ref.shape[0]
    groups, rows, width = in_refs[0].shape
    block_rows = groups * rows
    positions = block_rows // frames
    attended = jnp.concatenate([in_ref[...].reshape(block_rows, width) for in_ref in in_refs], axis=0)
    projected = nt_dot(attended, wall[...]).astype(jnp.bfloat16).astype(jnp.float32)
    for t in range(width // LANES):
        mixed[t] = projected[:, t * LANES : (t + 1) * LANES]
    for d in range(count):
        start = pl.multiple_of(lax.bitwise_xor(index, d) * positions, positions)
        for f in range(frames):
            values = tokens_ref[f, pl.ds(start, positions), :].astype(jnp.float32)
            rows_of = pl.ds(d * block_rows + f, positions, stride=frames)
            update = jnp.concatenate([mixed[t, rows_of, :] for t in range(width // LANES)], axis=1)
            result = values + modulation_ref[2, f : f + 1, :] * update
            out_ref[f, pl.ds(start, positions), :] = result.astype(out_ref.dtype)


def per_device(video_tokens, modulation, qkv_weight, out_weight):
    frames, positions, width = video_tokens.shape
    count, slabs = lax.axis_size("seq"), lax.axis_size("slab")
    index, slab = lax.axis_index("seq"), lax.axis_index("slab")
    block_positions = positions // count
    block_rows = block_positions * frames
    groups = block_rows // ROWS
    block = jax.ShapeDtypeStruct((groups, ROWS, width), jnp.bfloat16)
    own_index = jnp.stack([index, slab]).astype(jnp.int32)
    kinds = jnp.transpose(modulation, (1, 0, 2))
    smem = pl.BlockSpec(memory_space=pltpu.SMEM)
    vmem = pl.BlockSpec(memory_space=pltpu.VMEM)
    anywhere = pl.BlockSpec(memory_space=pl.ANY)
    params = pltpu.CompilerParams(vmem_limit_bytes=VMEM_BYTES)

    def hop(value, seq_xor, slab_xor=0):
        pairs = [(s * count + i, (s ^ slab_xor) * count + (i ^ seq_xor)) for s in range(slabs) for i in range(count)]
        return lax.ppermute(value, ("slab", "seq"), pairs)

    half = width // 2
    lanes = padded(half)
    columns, outs = qkv_weight.shape[1], out_weight.shape[1]
    chips = count // 2
    middle = chips
    size = -(-columns // (slabs * ROWS)) * ROWS
    over = slabs * size - columns
    shared = columns % ROWS == 0 and outs % ROWS == 0 and over < size and chips == 4 and slabs == 4
    tie = lax.optimization_barrier

    keep, give = pl.pallas_call(
        norm_kernel,
        out_shape=[jax.ShapeDtypeStruct((chips,) + block.shape, block.dtype)] * 2,
        in_specs=[smem, vmem, vmem],
        out_specs=[vmem] * 2,
        scratch_shapes=[pltpu.VMEM((width // LANES, block_rows, LANES), jnp.float32)],
        compiler_params=params,
        name="norm",
    )(own_index, video_tokens, kinds)
    swapped = hop(give, 1)
    pair = [jnp.stack([keep[z], swapped[z]]) for z in range(chips)]

    def to_neighbour(value, step):
        pairs = [(s * count + i, (s + (step if i < middle else -step)) % slabs * count + i)
                 for s in range(slabs) for i in range(count)]
        return lax.ppermute(value, ("slab", "seq"), pairs)

    def following_of(values):
        return to_neighbour(jnp.stack(values), -1)

    wide, narrow = qkv_weight.T, out_weight.T
    out_operands, out_moves = [], []
    operands, moves = [], []
    if shared:
        mine = lax.dynamic_slice_in_dim(wide, jnp.minimum(slab * size, columns - size), size, 0)

        def with_sibling(value, entries, other):
            for sibling in range(2):
                operands.append(other if sibling else value)
                for at, length, z, part in entries:
                    part = part if part is None else (part, 2 * z + sibling)
                    moves.append((len(operands) - 1, at, length, (2 * z) ^ sibling, part))

        x, y = 1, 2
        blocks = [pair[0], None, None, None]
        far = hop(mine, 4)
        wide_other, narrow_other = hop(wide, 1), hop(narrow, 1)
        blocks[1] = hop(pair[1], 2)
        far, mine, pair, wide_other, narrow_other, blocks[1] = tie((far, mine, pair, wide_other, narrow_other, blocks[1]))
        ax, ay = hop(far, 0, x), hop(far, 0, y)
        rest = hop(jnp.stack([mine, far]), 2)
        blocks[2] = hop(pair[2], 4)
        following = following_of(blocks[:2])
        ax, ay, rest, blocks[2], following, pair[3] = tie((ax, ay, rest, blocks[2], following, pair[3]))
        bx, by = hop(rest, 0, x), hop(rest, 0, y)
        both = jnp.concatenate([pair[3].reshape(-1, ROWS, width), narrow.reshape(-1, ROWS, width)], axis=0)
        blocks[3] = hop(both, 6)
        early = [hop(far, 1), hop(rest, 1)]
        ay, bx, by, early, ax = tie((ay, bx, by, early, ax))
        axy = hop(ay, 0, x)
        bxy = jnp.stack([hop(bx[0], 0, y), hop(by[1], 0, x)])
        swaps = [early[0], hop(ax, 1), hop(ay, 1), None]
        swaps += [early[1], hop(bx, 1), hop(by, 1)]
        with_sibling(wide, [((), columns, 0, None)], wide_other)
        for e, value in enumerate((far, ax, ay)):
            with_sibling(value, [((), size, 2, e)], swaps[e])
        for e, value in enumerate((rest, bx, by)):
            with_sibling(value, [((n,), size, z, e) for n, z in enumerate((1, 3))], swaps[4 + e])
        full_rows = 6 * half + count * over
        plan = dict(half=half, columns=columns, over=over, pieces=slabs, moves=moves)
        full = pl.pallas_call(
            functools.partial(gather_kernel, plan),
            out_shape=jax.ShapeDtypeStruct((full_rows, width), jnp.bfloat16),
            in_specs=[smem] + [anywhere] * len(operands),
            out_specs=anywhere,
            scratch_shapes=[pltpu.SemaphoreType.DMA((2 * len(moves),))],
            compiler_params=params,
            cost_estimate=pl.CostEstimate(flops=0, bytes_accessed=0, transcendentals=0),
            name="gather",
        )(own_index, *operands)
        operands.clear()
        moves.clear()
        bxy, swaps, blocks[3], full = tie((bxy, swaps, blocks[3], full))
        out_far = blocks[3][2 * groups :].reshape(narrow.shape)
        swaps.append(hop(bxy, 1))
        swaps[3] = hop(axy, 1)
        with_sibling(axy, [((), size, 2, 3)], swaps[3])
        with_sibling(bxy, [((n,), size, z, 3) for n, z in enumerate((1, 3))], swaps[7])
        near_half = [m for m in moves if m[3] < middle]
        far_half = [m for m in moves if m[3] >= middle]
        by_kind = [[(False, near_half), (True, far_half)], [(True, near_half), (False, far_half)]]
    else:
        full = lax.all_gather(wide, "seq", axis=0, tiled=True)
        by_kind = [[], []]
        out_operands = [lax.all_gather(narrow, "seq", axis=0, tiled=True)]
        out_moves = [(0, (), 0)]
        blocks = [hop(pair[z], 2 * z) if z else pair[z] for z in range(chips)]
        following = following_of(blocks[: chips // 2])

    tokens = count * block_rows

    def attention(kind, inputs):
        inputs = [value.reshape((-1,) + block.shape[1:]) for value in inputs]
        plan = dict(kind=kind, weights=len(operands), inputs=len(inputs), half=half, moves=by_kind[kind],
                    columns=columns, over=over, pieces=slabs)
        copies = max([1] + [2 * len(entries) for _, entries in by_kind[kind]])
        return pl.pallas_call(
            functools.partial(block_kernel, plan, frames),
            out_shape=[jax.ShapeDtypeStruct((groups, middle, ROWS, lanes), jnp.bfloat16)] * 2,
            in_specs=[smem] + [anywhere] * (len(inputs) + 1 + len(operands)),
            out_specs=[vmem] * 2,
            scratch_shapes=[
                pltpu.VMEM((groups, count, ROWS, width), jnp.bfloat16),
                pltpu.VMEM((3 * half + count * over, width), jnp.bfloat16),
                pltpu.VMEM((lanes, tokens), jnp.bfloat16),
                pltpu.VMEM((tokens, lanes), jnp.bfloat16),
                pltpu.VMEM((half, tokens), jnp.bfloat16),
                pltpu.SemaphoreType.DMA((count,)),
                pltpu.SemaphoreType.DMA((1,)),
                pltpu.SemaphoreType.DMA((copies,)),
            ],
            compiler_params=params,
            cost_estimate=pl.CostEstimate(flops=SPACE_FLOPS, bytes_accessed=8 * 1024 * 1024,
                                          transcendentals=0),
            name=("windowed", "shifted")[kind],
        )(own_index, *inputs, full, *operands)

    second_near, second_far = attention(1, blocks + [following])
    if shared:
        out_rest = hop(jnp.stack([narrow, out_far]), 2)
    second_near = to_neighbour(second_near, 1)
    first_near, first_far = attention(0, blocks)
    def merged(first_z, first, second, flops):
        return pl.pallas_call(
            functools.partial(merge_kernel, first_z),
            out_shape=[jax.ShapeDtypeStruct((2,) + block.shape, block.dtype)] * (chips // 2),
            in_specs=[smem] + [vmem] * 2,
            out_specs=[vmem] * (chips // 2),
            compiler_params=params,
            cost_estimate=pl.CostEstimate(flops=flops, bytes_accessed=4 * 1024 * 1024, transcendentals=0),
            name="merge",
        )(own_index, first, second)

    sent_far = merged(chips // 2, first_far, second_far, 0)
    if shared:
        out_rest, second_near = tie((out_rest, second_near))
    sent_near = merged(0, first_near, second_near, 0)
    sent = sent_near + sent_far
    arrived = [hop(sent[z], 2 * z) if z else sent[z] for z in range(chips // 2)]
    singles = [hop(sent[z][n], 2 * z + n)[None] for z in range(chips // 2, chips) for n in range(2)]
    if shared:
        out_rest, arrived, singles = tie((out_rest, arrived, singles))
    returned = []
    for value in arrived:
        returned += [value, hop(value, 1)]
    returned += singles
    if shared:
        out_operands = [narrow, narrow_other, out_far, hop(out_far, 1), out_rest, hop(out_rest, 1)]
        out_moves = [(0, (), (0,)), (1, (), (1,)), (2, (), (6,)), (3, (), (7,)), (4, (0,), (2,)), (5, (0,), (3,)),
                     (4, (1,), (4,)), (5, (1,), (5,))]

    plan = dict(count=count, weights=len(out_operands), moves=out_moves)
    return pl.pallas_call(
        functools.partial(restore_kernel, plan),
        out_shape=jax.ShapeDtypeStruct(video_tokens.shape, video_tokens.dtype),
        in_specs=[smem, vmem, vmem] + [vmem] * count + [anywhere] * len(out_operands),
        out_specs=vmem,
        scratch_shapes=[
            pltpu.VMEM((width, width), jnp.bfloat16),
            pltpu.VMEM((width // LANES, tokens, LANES), jnp.float32),
            pltpu.SemaphoreType.DMA((len(out_moves),)),
        ],
        compiler_params=params,
        name="restore",
    )(own_index, video_tokens, kinds, *returned, *out_operands)


def solution(mesh):
    return jax.shard_map(
        per_device,
        mesh=mesh,
        in_specs=(
            P(("slab", "seq"), None, None),
            P(("slab", "seq"), None, None),
            P(None, "seq"),
            P(None, "seq"),
        ),
        out_specs=P(("slab", "seq"), None, None),
        check_vma=False,
    )
```

```python
import functools

import jax
import jax.numpy as jnp
from jax import lax
from jax.experimental import pallas as pl
from jax.experimental.pallas import tpu as pltpu
from jax.sharding import PartitionSpec as P

H = 16
FRS = 32
EPSILON = 1e-06
LANES = 128
ROWS = 16
SPACE_FLOPS = 40 * 10**9
VMEM_BYTES = 24 * 1024 * 1024


def padded(width):
    return -(-width // LANES) * LANES


def norm_kernel(index_ref, tokens_ref, modulation_ref, keep_ref, give_ref, mixed):
    frames = tokens_ref.shape[0]
    chips, groups, rows, width = keep_ref.shape
    positions = groups * rows // frames
    index = index_ref[0]
    for d in range(2 * chips):
        out_ref = (keep_ref, give_ref)[d % 2]
        start = pl.multiple_of(lax.bitwise_xor(index, d) * positions, positions)
        for f in range(frames):
            values = tokens_ref[f, pl.ds(start, positions), :].astype(jnp.float32)
            average = jnp.mean(values, axis=-1, keepdims=True)
            centered = values - average
            variance = jnp.mean(centered * centered, axis=-1, keepdims=True)
            normed = centered * lax.rsqrt(variance + EPSILON)
            result = normed * (1.0 + modulation_ref[1, f : f + 1, :]) + modulation_ref[0, f : f + 1, :]
            for t in range(width // LANES):
                mixed[t, pl.ds(f, positions, stride=frames), :] = result[:, t * LANES : (t + 1) * LANES]
        for t in range(width // LANES):
            part = mixed[t].astype(out_ref.dtype).reshape(groups, rows, LANES)
            out_ref[d // 2, :, :, t * LANES : (t + 1) * LANES] = part


def nt_dot(left, right):
    return lax.dot_general(left, right, (((1,), (1,)), ((), ())), preferred_element_type=jnp.float32)


def head_window(head, head_size, shift):
    first = shift + head * head_size
    last = first + head_size
    low = first // LANES * LANES
    return first, last, low, padded(last)


def masked(values, first, last, low):
    lane = lax.broadcasted_iota(jnp.int32, values.shape, 1) + low
    return jnp.where((lane >= first) & (lane < last), values, jnp.zeros_like(values))


def softmax(scores, same, scale):
    scores = jnp.where(same, scores, -jnp.inf)
    top = jnp.max(scores, axis=0, keepdims=True)
    exponent = jnp.exp((scores - top) * scale)
    total = jnp.sum(exponent, axis=0, keepdims=True)
    return exponent * (1.0 / total)


def piece_moves(plan, index, slab, entries, w_refs, wall, first_row, rows):
    moves = []
    for operand, at, size, owner, part in entries:
        source = w_refs[operand]
        for step in at:
            source = source.at[step]
        base = lax.bitwise_xor(index, owner) * plan["columns"] - first_row
        if part is None:
            moves.append((source, wall.at[pl.ds(pl.multiple_of(base, ROWS), size)]))
            continue
        piece, over, spare = lax.bitwise_xor(slab, part[0]), plan["over"], part[1]
        ends = piece == plan["pieces"] - 1
        row = base + piece * size
        skip = jnp.where(ends, over, 0)
        moves.append((source.at[pl.ds(pl.multiple_of(skip, ROWS), size - over)],
                      wall.at[pl.ds(pl.multiple_of(row, ROWS), size - over)]))
        if over:
            row = jnp.where(ends, rows + spare * over, row + size - over)
            moves.append((source.at[pl.ds(size - over, over)], wall.at[pl.ds(pl.multiple_of(row, ROWS), over)]))
    return moves


def gather_kernel(plan, index_ref, *refs):
    w_refs, wall, sems = refs[:-2], refs[-2], refs[-1]
    moves = piece_moves(plan, index_ref[0], index_ref[1], plan["moves"], w_refs, wall, 0, 6 * plan["half"])
    moves = [pltpu.make_async_copy(a, b, sems.at[n]) for n, (a, b) in enumerate(moves)]
    for move in moves:
        move.start()
    for move in moves:
        move.wait()


def block_kernel(plan, frames, index_ref, *refs):
    kind, weights, half = plan["kind"], plan["weights"], plan["half"]
    refs = list(refs)
    x_refs = [refs.pop(0) for _ in range(plan["inputs"])]
    full_ref = refs.pop(0)
    w_refs = [refs.pop(0) for _ in range(weights)]
    out_refs = [refs.pop(0) for _ in range(2)]
    xs, wall, qt, kn, vt, sems, full_sem, wsems = refs
    groups, count, rows, width = xs.shape
    lanes = qt.shape[0]
    heads_half = H // 2
    head_size = width // H
    scale = head_size ** (-0.5)
    slot = count * rows
    index, slab = index_ref[0], index_ref[1]
    upper = index >= count // 2
    full = pltpu.make_async_copy(full_ref.at[pl.ds(3 * kind * half, 3 * half)], wall.at[pl.ds(0, 3 * half)], full_sem.at[0])
    full.start()

    sources = []
    for d in range(count):
        owner = lax.bitwise_xor(index, d)
        near = kind == 1 and d < count // 2
        source = x_refs[count // 2 + d // 2 if near else d // 2].at[pl.ds(d % 2 * groups, groups)]
        sources.append(pltpu.make_async_copy(source, xs.at[:, owner], sems.at[d]))
    for copy in sources:
        copy.start()
    full.wait()
    choices = []
    for chosen, entries in plan["moves"]:
        moves = piece_moves(plan, index, slab, entries, w_refs, wall, 3 * kind * half, 3 * half)
        choices.append((chosen, [pltpu.make_async_copy(a, b, wsems.at[n]) for n, (a, b) in enumerate(moves)]))

    def on_choice(act):
        for chosen, moves in choices:
            @pl.when(upper == chosen)
            def _():
                for copy in moves:
                    act(copy)

    on_choice(lambda copy: copy.start())
    gap = lanes - half
    if gap:
        qt[half:, :] = jnp.zeros((gap, qt.shape[1]), qt.dtype)
        kn[:, half:] = jnp.zeros((kn.shape[0], gap), kn.dtype)
    for copy in sources:
        copy.wait()
    on_choice(lambda copy: copy.wait())

    tokens = groups * slot
    own = xs[...].reshape(tokens, width)
    parts = [wall[n * half : (n + 1) * half, :] for n in range(3)]
    qt[:half, :] = nt_dot(parts[0], own).astype(qt.dtype)
    kn[:, :half] = nt_dot(own, parts[1]).astype(kn.dtype)
    vt[...] = nt_dot(parts[2], own).astype(vt.dtype)

    def one_group(g, carry):
        here = pl.ds(pl.multiple_of(g * slot, slot), slot)
        row = lax.broadcasted_iota(jnp.int32, (slot, slot), 0)
        column = lax.broadcasted_iota(jnp.int32, (slot, slot), 1)
        same = (row % rows) // frames == (column % rows) // frames
        scores = []
        for head in range(heads_half):
            first, last, low, high = head_window(head, head_size, 0)
            keys = masked(kn[here, low:high], first, last, low)
            scores.append(jnp.dot(keys, qt[low:high, here], preferred_element_type=jnp.float32))
        probs = [softmax(score, same, scale).astype(jnp.bfloat16) for score in scores]
        results = []
        for head, prob in enumerate(probs):
            values = vt[head * head_size : (head + 1) * head_size, here]
            results.append(jnp.dot(values, prob, preferred_element_type=jnp.float32))
        if gap:
            space = jnp.zeros((gap, slot), jnp.float32)
            results = [space] + results if kind else results + [space]
        result = jnp.concatenate(results, axis=0).T.astype(jnp.bfloat16)
        earlier, later = result[: slot // 2], result[slot // 2 :]
        out_refs[0][g] = jnp.where(upper, later, earlier).reshape(count // 2, rows, lanes)
        out_refs[1][g] = jnp.where(upper, earlier, later).reshape(count // 2, rows, lanes)
        return carry

    lax.fori_loop(0, groups, one_group, 0, unroll=True)


def merge_kernel(first_z, index_ref, first_ref, second_ref, *out_refs):
    index = index_ref[0]
    lanes = first_ref.shape[-1]
    for n, out_ref in enumerate(out_refs):
        cut = 2 * lanes - out_ref.shape[-1]
        for sibling in range(2):
            at = lax.rem(lax.bitwise_xor(index, 2 * (first_z + n) + sibling), 2 * len(out_refs))
            first, second = first_ref[:, at], second_ref[:, at]
            if cut:
                out_ref[sibling, ..., : lanes - cut] = first[..., : lanes - cut]
                out_ref[sibling, ..., lanes - cut : lanes] = first[..., lanes - cut :] + second[..., :cut]
                out_ref[sibling, ..., lanes:] = second[..., cut:]
            else:
                out_ref[sibling, ..., :lanes] = first
                out_ref[sibling, ..., lanes:] = second


def restore_kernel(plan, index_ref, tokens_ref, modulation_ref, *refs):
    count, moves = plan["count"], plan["moves"]
    refs = list(refs)
    in_refs = [refs.pop(0) for _ in range(count)]
    in_refs = [ref.at[n % ref.shape[0]] for n, ref in enumerate(in_refs)]
    w_refs = [refs.pop(0) for _ in range(plan["weights"])]
    out_ref, wall, mixed, sems = refs
    index = index_ref[0]
    copies = []
    for n, (operand, at, owner) in enumerate(moves):
        source = w_refs[operand]
        for step in at:
            source = source.at[step]
        size = source.shape[0]
        row = pl.multiple_of(lax.bitwise_xor(index, owner[0]) * size, ROWS) if isinstance(owner, tuple) else owner * size
        copies.append(pltpu.make_async_copy(source, wall.at[pl.ds(row, size)], sems.at[n]))
    for copy in copies:
        copy.start()
    for copy in copies:
        copy.wait()
    frames = tokens_ref.shape[0]
    groups, rows, width = in_refs[0].shape
    block_rows = groups * rows
    positions = block_rows // frames
    attended = jnp.concatenate([in_ref[...].reshape(block_rows, width) for in_ref in in_refs], axis=0)
    projected = nt_dot(attended, wall[...]).astype(jnp.bfloat16).astype(jnp.float32)
    for t in range(width // LANES):
        mixed[t] = projected[:, t * LANES : (t + 1) * LANES]
    for d in range(count):
        start = pl.multiple_of(lax.bitwise_xor(index, d) * positions, positions)
        for f in range(frames):
            values = tokens_ref[f, pl.ds(start, positions), :].astype(jnp.float32)
            rows_of = pl.ds(d * block_rows + f, positions, stride=frames)
            update = jnp.concatenate([mixed[t, rows_of, :] for t in range(width // LANES)], axis=1)
            result = values + modulation_ref[2, f : f + 1, :] * update
            out_ref[f, pl.ds(start, positions), :] = result.astype(out_ref.dtype)


def per_device(video_tokens, modulation, qkv_weight, out_weight):
    frames, positions, width = video_tokens.shape
    count, slabs = lax.axis_size("seq"), lax.axis_size("slab")
    index, slab = lax.axis_index("seq"), lax.axis_index("slab")
    block_positions = positions // count
    block_rows = block_positions * frames
    groups = block_rows // ROWS
    block = jax.ShapeDtypeStruct((groups, ROWS, width), jnp.bfloat16)
    own_index = jnp.stack([index, slab]).astype(jnp.int32)
    kinds = jnp.transpose(modulation, (1, 0, 2))
    smem = pl.BlockSpec(memory_space=pltpu.SMEM)
    vmem = pl.BlockSpec(memory_space=pltpu.VMEM)
    anywhere = pl.BlockSpec(memory_space=pl.ANY)
    params = pltpu.CompilerParams(vmem_limit_bytes=VMEM_BYTES)

    def hop(value, seq_xor, slab_xor=0):
        pairs = [(s * count + i, (s ^ slab_xor) * count + (i ^ seq_xor)) for s in range(slabs) for i in range(count)]
        return lax.ppermute(value, ("slab", "seq"), pairs)

    half = width // 2
    lanes = padded(half)
    columns, outs = qkv_weight.shape[1], out_weight.shape[1]
    chips = count // 2
    middle = chips
    size = -(-columns // (slabs * ROWS)) * ROWS
    over = slabs * size - columns
    shared = columns % ROWS == 0 and outs % ROWS == 0 and over < size and chips == 4 and slabs == 4
    tie = lax.optimization_barrier

    keep, give = pl.pallas_call(
        norm_kernel,
        out_shape=[jax.ShapeDtypeStruct((chips,) + block.shape, block.dtype)] * 2,
        in_specs=[smem, vmem, vmem],
        out_specs=[vmem] * 2,
        scratch_shapes=[pltpu.VMEM((width // LANES, block_rows, LANES), jnp.float32)],
        compiler_params=params,
        name="norm",
    )(own_index, video_tokens, kinds)
    swapped = hop(give, 1)
    pair = [jnp.stack([keep[z], swapped[z]]) for z in range(chips)]

    def to_neighbour(value, step):
        pairs = [(s * count + i, (s + (step if i < middle else -step)) % slabs * count + i)
                 for s in range(slabs) for i in range(count)]
        return lax.ppermute(value, ("slab", "seq"), pairs)

    def following_of(value):
        return to_neighbour(value, -1)

    wide, narrow = qkv_weight.T, out_weight.T
    out_operands, out_moves = [], []
    operands, moves = [], []
    if shared:
        mine = lax.dynamic_slice_in_dim(wide, jnp.minimum(slab * size, columns - size), size, 0)

        def with_sibling(value, entries, other):
            for sibling in range(2):
                operands.append(other if sibling else value)
                for at, length, z, part in entries:
                    part = part if part is None else (part, 2 * z + sibling)
                    moves.append((len(operands) - 1, at, length, (2 * z) ^ sibling, part))

        x, y = 1, 2
        blocks = [pair[0], None, None, None]
        far = hop(mine, 4)
        wide_other, narrow_other = hop(wide, 1), hop(narrow, 1)
        blocks[1] = hop(pair[1], 2)
        following = [following_of(pair[0])]
        near_and_far = jnp.stack([mine, far])
        blocks[1], far, near_and_far, pair, wide_other, narrow_other, following = tie(
            (blocks[1], far, near_and_far, pair, wide_other, narrow_other, following))
        ax, ay = hop(far, 0, x), hop(far, 0, y)
        rest = hop(near_and_far, 2)
        blocks[2] = hop(pair[2], 4)
        following.append(following_of(blocks[1]))
        ax, ay, rest, blocks[2], following, pair[3] = tie((ax, ay, rest, blocks[2], following, pair[3]))
        bx, by = hop(rest, 0, x), hop(rest, 0, y)
        both = jnp.concatenate([pair[3].reshape(-1, ROWS, width), narrow.reshape(-1, ROWS, width)], axis=0)
        blocks[3] = hop(both, 6)
        early = [hop(far, 1), hop(rest, 1)]
        ay, bx, by, early, ax = tie((ay, bx, by, early, ax))
        axy = hop(ay, 0, x)
        bxy = jnp.stack([hop(bx[0], 0, y), hop(by[1], 0, x)])
        swaps = [early[0], hop(ax, 1), hop(ay, 1), None]
        swaps += [early[1], hop(bx, 1), hop(by, 1)]
        with_sibling(wide, [((), columns, 0, None)], wide_other)
        for e, value in enumerate((far, ax, ay)):
            with_sibling(value, [((), size, 2, e)], swaps[e])
        for e, value in enumerate((rest, bx, by)):
            with_sibling(value, [((n,), size, z, e) for n, z in enumerate((1, 3))], swaps[4 + e])
        full_rows = 6 * half + count * over
        plan = dict(half=half, columns=columns, over=over, pieces=slabs, moves=moves)
        full = pl.pallas_call(
            functools.partial(gather_kernel, plan),
            out_shape=jax.ShapeDtypeStruct((full_rows, width), jnp.bfloat16),
            in_specs=[smem] + [anywhere] * len(operands),
            out_specs=anywhere,
            scratch_shapes=[pltpu.SemaphoreType.DMA((2 * len(moves),))],
            compiler_params=params,
            cost_estimate=pl.CostEstimate(flops=0, bytes_accessed=0, transcendentals=0),
            name="gather",
        )(own_index, *operands)
        operands.clear()
        moves.clear()
        bxy, swaps, blocks[3], full = tie((bxy, swaps, blocks[3], full))
        out_far = blocks[3][2 * groups :].reshape(narrow.shape)
        swaps.append(hop(bxy, 1))
        swaps[3] = hop(axy, 1)
        with_sibling(axy, [((), size, 2, 3)], swaps[3])
        with_sibling(bxy, [((n,), size, z, 3) for n, z in enumerate((1, 3))], swaps[7])
        near_half = [m for m in moves if m[3] < middle]
        far_half = [m for m in moves if m[3] >= middle]
        by_kind = [[(False, near_half), (True, far_half)], [(True, near_half), (False, far_half)]]
    else:
        full = lax.all_gather(wide, "seq", axis=0, tiled=True)
        by_kind = [[], []]
        out_operands = [lax.all_gather(narrow, "seq", axis=0, tiled=True)]
        out_moves = [(0, (), 0)]
        blocks = [hop(pair[z], 2 * z) if z else pair[z] for z in range(chips)]
        following = [following_of(value) for value in blocks[: chips // 2]]

    tokens = count * block_rows

    def attention(kind, inputs):
        inputs = [value.reshape((-1,) + block.shape[1:]) for value in inputs]
        plan = dict(kind=kind, weights=len(operands), inputs=len(inputs), half=half, moves=by_kind[kind],
                    columns=columns, over=over, pieces=slabs)
        copies = max([1] + [2 * len(entries) for _, entries in by_kind[kind]])
        return pl.pallas_call(
            functools.partial(block_kernel, plan, frames),
            out_shape=[jax.ShapeDtypeStruct((groups, middle, ROWS, lanes), jnp.bfloat16)] * 2,
            in_specs=[smem] + [anywhere] * (len(inputs) + 1 + len(operands)),
            out_specs=[vmem] * 2,
            scratch_shapes=[
                pltpu.VMEM((groups, count, ROWS, width), jnp.bfloat16),
                pltpu.VMEM((3 * half + count * over, width), jnp.bfloat16),
                pltpu.VMEM((lanes, tokens), jnp.bfloat16),
                pltpu.VMEM((tokens, lanes), jnp.bfloat16),
                pltpu.VMEM((half, tokens), jnp.bfloat16),
                pltpu.SemaphoreType.DMA((count,)),
                pltpu.SemaphoreType.DMA((1,)),
                pltpu.SemaphoreType.DMA((copies,)),
            ],
            compiler_params=params,
            cost_estimate=pl.CostEstimate(flops=SPACE_FLOPS, bytes_accessed=8 * 1024 * 1024,
                                          transcendentals=0),
            name=("windowed", "shifted")[kind],
        )(own_index, *inputs, full, *operands)

    second_near, second_far = attention(1, blocks + following)
    if shared:
        out_rest = hop(jnp.stack([narrow, out_far]), 2)
    second_near = to_neighbour(second_near, 1)
    first_near, first_far = attention(0, blocks)
    def merged(first_z, first, second, flops):
        return pl.pallas_call(
            functools.partial(merge_kernel, first_z),
            out_shape=[jax.ShapeDtypeStruct((2,) + block.shape, block.dtype)] * (chips // 2),
            in_specs=[smem] + [vmem] * 2,
            out_specs=[vmem] * (chips // 2),
            compiler_params=params,
            cost_estimate=pl.CostEstimate(flops=flops, bytes_accessed=4 * 1024 * 1024, transcendentals=0),
            name="merge",
        )(own_index, first, second)

    sent_far = merged(chips // 2, first_far, second_far, 0)
    if shared:
        out_rest, second_near = tie((out_rest, second_near))
    sent_near = merged(0, first_near, second_near, 0)
    sent = sent_near + sent_far
    arrived = [hop(sent[z], 2 * z) if z else sent[z] for z in range(chips // 2)]
    singles = [hop(sent[z][n], 2 * z + n)[None] for z in range(chips // 2, chips) for n in range(2)]
    if shared:
        arrived, singles = tie((arrived, singles))
    returned = []
    for value in arrived:
        returned += [value, hop(value, 1)]
    returned += singles
    if shared:
        out_operands = [narrow, narrow_other, out_far, hop(out_far, 1), out_rest, hop(out_rest, 1)]
        out_moves = [(0, (), (0,)), (1, (), (1,)), (2, (), (6,)), (3, (), (7,)), (4, (0,), (2,)), (5, (0,), (3,)),
                     (4, (1,), (4,)), (5, (1,), (5,))]

    plan = dict(count=count, weights=len(out_operands), moves=out_moves)
    return pl.pallas_call(
        functools.partial(restore_kernel, plan),
        out_shape=jax.ShapeDtypeStruct(video_tokens.shape, video_tokens.dtype),
        in_specs=[smem, vmem, vmem] + [vmem] * count + [anywhere] * len(out_operands),
        out_specs=vmem,
        scratch_shapes=[
            pltpu.VMEM((width, width), jnp.bfloat16),
            pltpu.VMEM((width // LANES, tokens, LANES), jnp.float32),
            pltpu.SemaphoreType.DMA((len(out_moves),)),
        ],
        compiler_params=params,
        name="restore",
    )(own_index, video_tokens, kinds, *returned, *out_operands)


def solution(mesh):
    return jax.shard_map(
        per_device,
        mesh=mesh,
        in_specs=(
            P(("slab", "seq"), None, None),
            P(("slab", "seq"), None, None),
            P(None, "seq"),
            P(None, "seq"),
        ),
        out_specs=P(("slab", "seq"), None, None),
        check_vma=False,
    )
```

```python
import functools

import jax
import jax.numpy as jnp
from jax import lax
from jax.experimental import pallas as pl
from jax.experimental.pallas import tpu as pltpu
from jax.sharding import PartitionSpec as P

H = 16
FRS = 32
EPSILON = 1e-06
LANES = 128
ROWS = 16
SPACE_FLOPS = 40 * 10**9
VMEM_BYTES = 24 * 1024 * 1024


def padded(width):
    return -(-width // LANES) * LANES


def norm_kernel(index_ref, tokens_ref, modulation_ref, keep_ref, give_ref, mixed):
    frames = tokens_ref.shape[0]
    chips, groups, rows, width = keep_ref.shape
    positions = groups * rows // frames
    index = index_ref[0]
    for d in range(2 * chips):
        out_ref = (keep_ref, give_ref)[d % 2]
        start = pl.multiple_of(lax.bitwise_xor(index, d) * positions, positions)
        for f in range(frames):
            values = tokens_ref[f, pl.ds(start, positions), :].astype(jnp.float32)
            average = jnp.mean(values, axis=-1, keepdims=True)
            centered = values - average
            variance = jnp.mean(centered * centered, axis=-1, keepdims=True)
            normed = centered * lax.rsqrt(variance + EPSILON)
            result = normed * (1.0 + modulation_ref[1, f : f + 1, :]) + modulation_ref[0, f : f + 1, :]
            for t in range(width // LANES):
                mixed[t, pl.ds(f, positions, stride=frames), :] = result[:, t * LANES : (t + 1) * LANES]
        for t in range(width // LANES):
            part = mixed[t].astype(out_ref.dtype).reshape(groups, rows, LANES)
            out_ref[d // 2, :, :, t * LANES : (t + 1) * LANES] = part


def nt_dot(left, right):
    return lax.dot_general(left, right, (((1,), (1,)), ((), ())), preferred_element_type=jnp.float32)


def head_window(head, head_size, shift):
    first = shift + head * head_size
    last = first + head_size
    low = first // LANES * LANES
    return first, last, low, padded(last)


def masked(values, first, last, low):
    lane = lax.broadcasted_iota(jnp.int32, values.shape, 1) + low
    return jnp.where((lane >= first) & (lane < last), values, jnp.zeros_like(values))


def softmax(scores, same, scale):
    scores = jnp.where(same, scores, -jnp.inf)
    top = jnp.max(scores, axis=0, keepdims=True)
    exponent = jnp.exp((scores - top) * scale)
    total = jnp.sum(exponent, axis=0, keepdims=True)
    return exponent * (1.0 / total)


def piece_moves(plan, index, slab, entries, w_refs, wall, first_row, rows):
    moves = []
    for operand, at, size, owner, part in entries:
        source = w_refs[operand]
        for step in at:
            source = source.at[step]
        base = lax.bitwise_xor(index, owner) * plan["columns"] - first_row
        if part is None:
            moves.append((source, wall.at[pl.ds(pl.multiple_of(base, ROWS), size)]))
            continue
        piece, over, spare = lax.bitwise_xor(slab, part[0]), plan["over"], part[1]
        ends = piece == plan["pieces"] - 1
        row = base + piece * size
        skip = jnp.where(ends, over, 0)
        moves.append((source.at[pl.ds(pl.multiple_of(skip, ROWS), size - over)],
                      wall.at[pl.ds(pl.multiple_of(row, ROWS), size - over)]))
        if over:
            row = jnp.where(ends, rows + spare * over, row + size - over)
            moves.append((source.at[pl.ds(size - over, over)], wall.at[pl.ds(pl.multiple_of(row, ROWS), over)]))
    return moves


def gather_kernel(plan, index_ref, *refs):
    w_refs, wall, sems = refs[:-2], refs[-2], refs[-1]
    moves = piece_moves(plan, index_ref[0], index_ref[1], plan["moves"], w_refs, wall, 0, 6 * plan["half"])
    moves = [pltpu.make_async_copy(a, b, sems.at[n]) for n, (a, b) in enumerate(moves)]
    for move in moves:
        move.start()
    for move in moves:
        move.wait()


def block_kernel(plan, frames, index_ref, *refs):
    kind, weights, half = plan["kind"], plan["weights"], plan["half"]
    refs = list(refs)
    x_refs = [refs.pop(0) for _ in range(plan["inputs"])]
    full_ref = refs.pop(0)
    w_refs = [refs.pop(0) for _ in range(weights)]
    out_refs = [refs.pop(0) for _ in range(2)]
    xs, wall, qt, kn, vt, sems, full_sem, wsems = refs
    groups, count, rows, width = xs.shape
    lanes = qt.shape[0]
    heads_half = H // 2
    head_size = width // H
    scale = head_size ** (-0.5)
    slot = count * rows
    index, slab = index_ref[0], index_ref[1]
    upper = index >= count // 2
    full = pltpu.make_async_copy(full_ref.at[pl.ds(3 * kind * half, 3 * half)], wall.at[pl.ds(0, 3 * half)], full_sem.at[0])
    full.start()

    sources = []
    for d in range(count):
        owner = lax.bitwise_xor(index, d)
        near = kind == 1 and d < count // 2
        source = x_refs[count // 2 + d // 2 if near else d // 2].at[pl.ds(d % 2 * groups, groups)]
        sources.append(pltpu.make_async_copy(source, xs.at[:, owner], sems.at[d]))
    for copy in sources:
        copy.start()
    full.wait()
    choices = []
    for chosen, entries in plan["moves"]:
        moves = piece_moves(plan, index, slab, entries, w_refs, wall, 3 * kind * half, 3 * half)
        choices.append((chosen, [pltpu.make_async_copy(a, b, wsems.at[n]) for n, (a, b) in enumerate(moves)]))

    def on_choice(act):
        for chosen, moves in choices:
            @pl.when(upper == chosen)
            def _():
                for copy in moves:
                    act(copy)

    on_choice(lambda copy: copy.start())
    gap = lanes - half
    if gap:
        qt[half:, :] = jnp.zeros((gap, qt.shape[1]), qt.dtype)
        kn[:, half:] = jnp.zeros((kn.shape[0], gap), kn.dtype)
    for copy in sources:
        copy.wait()
    on_choice(lambda copy: copy.wait())

    tokens = groups * slot
    own = xs[...].reshape(tokens, width)
    parts = [wall[n * half : (n + 1) * half, :] for n in range(3)]
    qt[:half, :] = nt_dot(parts[0], own).astype(qt.dtype)
    kn[:, :half] = nt_dot(own, parts[1]).astype(kn.dtype)
    vt[...] = nt_dot(parts[2], own).astype(vt.dtype)

    def one_group(g, carry):
        here = pl.ds(pl.multiple_of(g * slot, slot), slot)
        row = lax.broadcasted_iota(jnp.int32, (slot, slot), 0)
        column = lax.broadcasted_iota(jnp.int32, (slot, slot), 1)
        same = (row % rows) // frames == (column % rows) // frames
        scores = []
        for head in range(heads_half):
            first, last, low, high = head_window(head, head_size, 0)
            keys = masked(kn[here, low:high], first, last, low)
            scores.append(jnp.dot(keys, qt[low:high, here], preferred_element_type=jnp.float32))
        probs = [softmax(score, same, scale).astype(jnp.bfloat16) for score in scores]
        results = []
        for head, prob in enumerate(probs):
            values = vt[head * head_size : (head + 1) * head_size, here]
            results.append(jnp.dot(values, prob, preferred_element_type=jnp.float32))
        if gap:
            space = jnp.zeros((gap, slot), jnp.float32)
            results = [space] + results if kind else results + [space]
        result = jnp.concatenate(results, axis=0).T.astype(jnp.bfloat16)
        earlier, later = result[: slot // 2], result[slot // 2 :]
        out_refs[0][g] = jnp.where(upper, later, earlier).reshape(count // 2, rows, lanes)
        out_refs[1][g] = jnp.where(upper, earlier, later).reshape(count // 2, rows, lanes)
        return carry

    lax.fori_loop(0, groups, one_group, 0, unroll=True)


def merge_kernel(first_z, index_ref, first_ref, second_ref, *out_refs):
    index = index_ref[0]
    lanes = first_ref.shape[-1]
    for n, out_ref in enumerate(out_refs):
        cut = 2 * lanes - out_ref.shape[-1]
        for sibling in range(2):
            at = lax.rem(lax.bitwise_xor(index, 2 * (first_z + n) + sibling), 2 * len(out_refs))
            first, second = first_ref[:, at], second_ref[:, at]
            if cut:
                out_ref[sibling, ..., : lanes - cut] = first[..., : lanes - cut]
                out_ref[sibling, ..., lanes - cut : lanes] = first[..., lanes - cut :] + second[..., :cut]
                out_ref[sibling, ..., lanes:] = second[..., cut:]
            else:
                out_ref[sibling, ..., :lanes] = first
                out_ref[sibling, ..., lanes:] = second


def gather_out_kernel(moves, index_ref, *refs):
    w_refs, wall, sems = refs[:-2], refs[-2], refs[-1]
    copies = []
    for n, (operand, at, owner) in enumerate(moves):
        source = w_refs[operand]
        for step in at:
            source = source.at[step]
        size = source.shape[0]
        row = lax.bitwise_xor(index_ref[0], owner[0]) * size if isinstance(owner, tuple) else owner * size
        copies.append(pltpu.make_async_copy(source, wall.at[pl.ds(pl.multiple_of(row, ROWS), size)], sems.at[n]))
    for copy in copies:
        copy.start()
    for copy in copies:
        copy.wait()


def restore_kernel(count, index_ref, tokens_ref, modulation_ref, wall, *refs):
    refs = list(refs)
    in_refs = [refs.pop(0) for _ in range(count)]
    in_refs = [ref.at[n % ref.shape[0]] for n, ref in enumerate(in_refs)]
    out_ref, mixed = refs
    index = index_ref[0]
    frames = tokens_ref.shape[0]
    groups, rows, width = in_refs[0].shape
    block_rows = groups * rows
    positions = block_rows // frames
    attended = jnp.concatenate([in_ref[...].reshape(block_rows, width) for in_ref in in_refs], axis=0)
    projected = nt_dot(attended, wall[...]).astype(jnp.bfloat16).astype(jnp.float32)
    for t in range(width // LANES):
        mixed[t] = projected[:, t * LANES : (t + 1) * LANES]
    for d in range(count):
        start = pl.multiple_of(lax.bitwise_xor(index, d) * positions, positions)
        for f in range(frames):
            values = tokens_ref[f, pl.ds(start, positions), :].astype(jnp.float32)
            rows_of = pl.ds(d * block_rows + f, positions, stride=frames)
            update = jnp.concatenate([mixed[t, rows_of, :] for t in range(width // LANES)], axis=1)
            result = values + modulation_ref[2, f : f + 1, :] * update
            out_ref[f, pl.ds(start, positions), :] = result.astype(out_ref.dtype)


def per_device(video_tokens, modulation, qkv_weight, out_weight):
    frames, positions, width = video_tokens.shape
    count, slabs = lax.axis_size("seq"), lax.axis_size("slab")
    index, slab = lax.axis_index("seq"), lax.axis_index("slab")
    block_positions = positions // count
    block_rows = block_positions * frames
    groups = block_rows // ROWS
    block = jax.ShapeDtypeStruct((groups, ROWS, width), jnp.bfloat16)
    own_index = jnp.stack([index, slab]).astype(jnp.int32)
    kinds = jnp.transpose(modulation, (1, 0, 2))
    smem = pl.BlockSpec(memory_space=pltpu.SMEM)
    vmem = pl.BlockSpec(memory_space=pltpu.VMEM)
    anywhere = pl.BlockSpec(memory_space=pl.ANY)
    params = pltpu.CompilerParams(vmem_limit_bytes=VMEM_BYTES)

    def hop(value, seq_xor, slab_xor=0):
        pairs = [(s * count + i, (s ^ slab_xor) * count + (i ^ seq_xor)) for s in range(slabs) for i in range(count)]
        return lax.ppermute(value, ("slab", "seq"), pairs)

    half = width // 2
    lanes = padded(half)
    columns, outs = qkv_weight.shape[1], out_weight.shape[1]
    chips = count // 2
    middle = chips
    size = -(-columns // (slabs * ROWS)) * ROWS
    over = slabs * size - columns
    shared = columns % ROWS == 0 and outs % ROWS == 0 and over < size and chips == 4 and slabs == 4
    tie = lax.optimization_barrier

    keep, give = pl.pallas_call(
        norm_kernel,
        out_shape=[jax.ShapeDtypeStruct((chips,) + block.shape, block.dtype)] * 2,
        in_specs=[smem, vmem, vmem],
        out_specs=[vmem] * 2,
        scratch_shapes=[pltpu.VMEM((width // LANES, block_rows, LANES), jnp.float32)],
        compiler_params=params,
        name="norm",
    )(own_index, video_tokens, kinds)
    swapped = hop(give, 1)
    pair = [jnp.stack([keep[z], swapped[z]]) for z in range(chips)]

    def to_neighbour(value, step):
        pairs = [(s * count + i, (s + (step if i < middle else -step)) % slabs * count + i)
                 for s in range(slabs) for i in range(count)]
        return lax.ppermute(value, ("slab", "seq"), pairs)

    def following_of(value):
        return to_neighbour(value, -1)

    wide, narrow = qkv_weight.T, out_weight.T
    out_operands, out_moves = [], []
    operands, moves = [], []
    if shared:
        mine = lax.dynamic_slice_in_dim(wide, jnp.minimum(slab * size, columns - size), size, 0)

        def with_sibling(value, entries, other):
            for sibling in range(2):
                operands.append(other if sibling else value)
                for at, length, z, part in entries:
                    part = part if part is None else (part, 2 * z + sibling)
                    moves.append((len(operands) - 1, at, length, (2 * z) ^ sibling, part))

        x, y = 1, 2
        blocks = [pair[0], None, None, None]
        far = hop(mine, 4)
        wide_other, narrow_other = hop(wide, 1), hop(narrow, 1)
        blocks[1] = hop(pair[1], 2)
        following = [following_of(pair[0])]
        near_and_far = jnp.stack([mine, far])
        blocks[1], far, near_and_far, pair, wide_other, narrow_other, following = tie(
            (blocks[1], far, near_and_far, pair, wide_other, narrow_other, following))
        ax, ay = hop(far, 0, x), hop(far, 0, y)
        rest = hop(near_and_far, 2)
        blocks[2] = hop(pair[2], 4)
        following.append(following_of(blocks[1]))
        ax, ay, rest, blocks[2], following, pair[3] = tie((ax, ay, rest, blocks[2], following, pair[3]))
        bx, by = hop(rest, 0, x), hop(rest, 0, y)
        both = jnp.concatenate([pair[3].reshape(-1, ROWS, width), narrow.reshape(-1, ROWS, width)], axis=0)
        blocks[3] = hop(both, 6)
        early = [hop(far, 1), hop(rest, 1)]
        ay, bx, by, early, ax = tie((ay, bx, by, early, ax))
        axy = hop(ay, 0, x)
        bxy = jnp.stack([hop(bx[0], 0, y), hop(by[1], 0, x)])
        swaps = [early[0], hop(ax, 1), hop(ay, 1), None]
        swaps += [early[1], hop(bx, 1), hop(by, 1)]
        with_sibling(wide, [((), columns, 0, None)], wide_other)
        for e, value in enumerate((far, ax, ay)):
            with_sibling(value, [((), size, 2, e)], swaps[e])
        for e, value in enumerate((rest, bx, by)):
            with_sibling(value, [((n,), size, z, e) for n, z in enumerate((1, 3))], swaps[4 + e])
        full_rows = 6 * half + count * over
        plan = dict(half=half, columns=columns, over=over, pieces=slabs, moves=moves)
        full = pl.pallas_call(
            functools.partial(gather_kernel, plan),
            out_shape=jax.ShapeDtypeStruct((full_rows, width), jnp.bfloat16),
            in_specs=[smem] + [anywhere] * len(operands),
            out_specs=anywhere,
            scratch_shapes=[pltpu.SemaphoreType.DMA((2 * len(moves),))],
            compiler_params=params,
            cost_estimate=pl.CostEstimate(flops=0, bytes_accessed=0, transcendentals=0),
            name="gather",
        )(own_index, *operands)
        operands.clear()
        moves.clear()
        bxy, swaps, blocks[3], full = tie((bxy, swaps, blocks[3], full))
        out_far = blocks[3][2 * groups :].reshape(narrow.shape)
        swaps.append(hop(bxy, 1))
        swaps[3] = hop(axy, 1)
        with_sibling(axy, [((), size, 2, 3)], swaps[3])
        with_sibling(bxy, [((n,), size, z, 3) for n, z in enumerate((1, 3))], swaps[7])
        near_half = [m for m in moves if m[3] < middle]
        far_half = [m for m in moves if m[3] >= middle]
        by_kind = [[(False, near_half), (True, far_half)], [(True, near_half), (False, far_half)]]
    else:
        full = lax.all_gather(wide, "seq", axis=0, tiled=True)
        by_kind = [[], []]
        out_operands = [lax.all_gather(narrow, "seq", axis=0, tiled=True)]
        out_moves = [(0, (), 0)]
        blocks = [hop(pair[z], 2 * z) if z else pair[z] for z in range(chips)]
        following = [following_of(value) for value in blocks[: chips // 2]]

    tokens = count * block_rows

    def attention(kind, inputs):
        inputs = [value.reshape((-1,) + block.shape[1:]) for value in inputs]
        plan = dict(kind=kind, weights=len(operands), inputs=len(inputs), half=half, moves=by_kind[kind],
                    columns=columns, over=over, pieces=slabs)
        copies = max([1] + [2 * len(entries) for _, entries in by_kind[kind]])
        return pl.pallas_call(
            functools.partial(block_kernel, plan, frames),
            out_shape=[jax.ShapeDtypeStruct((groups, middle, ROWS, lanes), jnp.bfloat16)] * 2,
            in_specs=[smem] + [anywhere] * (len(inputs) + 1 + len(operands)),
            out_specs=[vmem] * 2,
            scratch_shapes=[
                pltpu.VMEM((groups, count, ROWS, width), jnp.bfloat16),
                pltpu.VMEM((3 * half + count * over, width), jnp.bfloat16),
                pltpu.VMEM((lanes, tokens), jnp.bfloat16),
                pltpu.VMEM((tokens, lanes), jnp.bfloat16),
                pltpu.VMEM((half, tokens), jnp.bfloat16),
                pltpu.SemaphoreType.DMA((count,)),
                pltpu.SemaphoreType.DMA((1,)),
                pltpu.SemaphoreType.DMA((copies,)),
            ],
            compiler_params=params,
            cost_estimate=pl.CostEstimate(flops=SPACE_FLOPS, bytes_accessed=8 * 1024 * 1024,
                                          transcendentals=0),
            name=("windowed", "shifted")[kind],
        )(own_index, *inputs, full, *operands)

    second_near, second_far = attention(1, blocks + following)
    if shared:
        out_rest = hop(jnp.stack([narrow, out_far]), 2)
    second_near = to_neighbour(second_near, 1)
    first_near, first_far = attention(0, blocks)
    def merged(first_z, first, second, flops):
        return pl.pallas_call(
            functools.partial(merge_kernel, first_z),
            out_shape=[jax.ShapeDtypeStruct((2,) + block.shape, block.dtype)] * (chips // 2),
            in_specs=[smem] + [vmem] * 2,
            out_specs=[vmem] * (chips // 2),
            compiler_params=params,
            cost_estimate=pl.CostEstimate(flops=flops, bytes_accessed=4 * 1024 * 1024, transcendentals=0),
            name="merge",
        )(own_index, first, second)

    sent_far = merged(chips // 2, first_far, second_far, 0)
    if shared:
        out_rest, second_near = tie((out_rest, second_near))
    sent_near = merged(0, first_near, second_near, 0)
    sent = sent_near + sent_far
    arrived = [hop(sent[z], 2 * z) if z else sent[z] for z in range(chips // 2)]
    singles = [hop(sent[z][n], 2 * z + n)[None] for z in range(chips // 2, chips) for n in range(2)]
    if shared:
        out_operands = [narrow, narrow_other, out_far, hop(out_far, 1), out_rest, hop(out_rest, 1)]
        out_moves = [(0, (), (0,)), (1, (), (1,)), (2, (), (6,)), (3, (), (7,)), (4, (0,), (2,)), (5, (0,), (3,)),
                     (4, (1,), (4,)), (5, (1,), (5,))]
    out_full = pl.pallas_call(
        functools.partial(gather_out_kernel, out_moves),
        out_shape=jax.ShapeDtypeStruct((width, width), jnp.bfloat16),
        in_specs=[smem] + [anywhere] * len(out_operands),
        out_specs=anywhere,
        scratch_shapes=[pltpu.SemaphoreType.DMA((len(out_moves),))],
        compiler_params=params,
        name="gather_out",
    )(own_index, *out_operands)
    if shared:
        arrived, singles = tie((arrived, singles))
    returned = []
    for value in arrived:
        returned += [value, hop(value, 1)]
    returned += singles
    return pl.pallas_call(
        functools.partial(restore_kernel, count),
        out_shape=jax.ShapeDtypeStruct(video_tokens.shape, video_tokens.dtype),
        in_specs=[smem] + [vmem] * (3 + count),
        out_specs=vmem,
        scratch_shapes=[pltpu.VMEM((width // LANES, tokens, LANES), jnp.float32)],
        compiler_params=params,
        name="restore",
    )(own_index, video_tokens, kinds, out_full, *returned)


def solution(mesh):
    return jax.shard_map(
        per_device,
        mesh=mesh,
        in_specs=(
            P(("slab", "seq"), None, None),
            P(("slab", "seq"), None, None),
            P(None, "seq"),
            P(None, "seq"),
        ),
        out_specs=P(("slab", "seq"), None, None),
        check_vma=False,
    )
```

```python
import functools

import jax
import jax.numpy as jnp
from jax import lax
from jax.experimental import pallas as pl
from jax.experimental.pallas import tpu as pltpu
from jax.sharding import PartitionSpec as P

H = 16
FRS = 32
EPSILON = 1e-06
LANES = 128
ROWS = 16
SPACE_FLOPS = 40 * 10**9
VMEM_BYTES = 24 * 1024 * 1024


def padded(width):
    return -(-width // LANES) * LANES


def norm_kernel(index_ref, tokens_ref, modulation_ref, keep_ref, give_ref, mixed):
    frames = tokens_ref.shape[0]
    chips, groups, rows, width = keep_ref.shape
    positions = groups * rows // frames
    index = index_ref[0]
    for d in range(2 * chips):
        out_ref = (keep_ref, give_ref)[d % 2]
        start = pl.multiple_of(lax.bitwise_xor(index, d) * positions, positions)
        for f in range(frames):
            values = tokens_ref[f, pl.ds(start, positions), :].astype(jnp.float32)
            average = jnp.mean(values, axis=-1, keepdims=True)
            centered = values - average
            variance = jnp.mean(centered * centered, axis=-1, keepdims=True)
            normed = centered * lax.rsqrt(variance + EPSILON)
            result = normed * (1.0 + modulation_ref[1, f : f + 1, :]) + modulation_ref[0, f : f + 1, :]
            for t in range(width // LANES):
                mixed[t, pl.ds(f, positions, stride=frames), :] = result[:, t * LANES : (t + 1) * LANES]
        for t in range(width // LANES):
            part = mixed[t].astype(out_ref.dtype).reshape(groups, rows, LANES)
            out_ref[d // 2, :, :, t * LANES : (t + 1) * LANES] = part


def nt_dot(left, right):
    return lax.dot_general(left, right, (((1,), (1,)), ((), ())), preferred_element_type=jnp.float32)


def head_window(head, head_size, shift):
    first = shift + head * head_size
    last = first + head_size
    low = first // LANES * LANES
    return first, last, low, padded(last)


def masked(values, first, last, low):
    lane = lax.broadcasted_iota(jnp.int32, values.shape, 1) + low
    return jnp.where((lane >= first) & (lane < last), values, jnp.zeros_like(values))


def softmax(scores, same, scale):
    scores = jnp.where(same, scores, -jnp.inf)
    top = jnp.max(scores, axis=0, keepdims=True)
    exponent = jnp.exp((scores - top) * scale)
    total = jnp.sum(exponent, axis=0, keepdims=True)
    return exponent * (1.0 / total)


def piece_moves(plan, index, slab, entries, w_refs, wall, first_row, rows):
    moves = []
    for operand, at, size, owner, part in entries:
        source = w_refs[operand]
        for step in at:
            source = source.at[step]
        base = lax.bitwise_xor(index, owner) * plan["columns"] - first_row
        if part is None:
            moves.append((source, wall.at[pl.ds(pl.multiple_of(base, ROWS), size)]))
            continue
        piece, over, spare = lax.bitwise_xor(slab, part[0]), plan["over"], part[1]
        ends = piece == plan["pieces"] - 1
        row = base + piece * size
        skip = jnp.where(ends, over, 0)
        moves.append((source.at[pl.ds(pl.multiple_of(skip, ROWS), size - over)],
                      wall.at[pl.ds(pl.multiple_of(row, ROWS), size - over)]))
        if over:
            row = jnp.where(ends, rows + spare * over, row + size - over)
            moves.append((source.at[pl.ds(size - over, over)], wall.at[pl.ds(pl.multiple_of(row, ROWS), over)]))
    return moves


def gather_kernel(plan, index_ref, *refs):
    w_refs, wall, sems = refs[:-2], refs[-2], refs[-1]
    moves = piece_moves(plan, index_ref[0], index_ref[1], plan["moves"], w_refs, wall, 0, 6 * plan["half"])
    moves = [pltpu.make_async_copy(a, b, sems.at[n]) for n, (a, b) in enumerate(moves)]
    for move in moves:
        move.start()
    for move in moves:
        move.wait()


def block_kernel(plan, frames, index_ref, *refs):
    kind, weights, half = plan["kind"], plan["weights"], plan["half"]
    refs = list(refs)
    x_refs = [refs.pop(0) for _ in range(plan["inputs"])]
    full_ref = refs.pop(0)
    w_refs = [refs.pop(0) for _ in range(weights)]
    out_refs = [refs.pop(0) for _ in range(2)]
    xs, wall, qt, kn, vt, sems, full_sem, wsems = refs
    groups, count, rows, width = xs.shape
    lanes = qt.shape[0]
    heads_half = H // 2
    head_size = width // H
    scale = head_size ** (-0.5)
    slot = count * rows
    index, slab = index_ref[0], index_ref[1]
    upper = index >= count // 2
    full = pltpu.make_async_copy(full_ref.at[pl.ds(3 * kind * half, 3 * half)], wall.at[pl.ds(0, 3 * half)], full_sem.at[0])
    full.start()

    sources = []
    for d in range(count):
        owner = lax.bitwise_xor(index, d)
        near = kind == 1 and d < count // 2
        source = x_refs[count // 2 + d // 2 if near else d // 2].at[pl.ds(d % 2 * groups, groups)]
        sources.append(pltpu.make_async_copy(source, xs.at[:, owner], sems.at[d]))
    for copy in sources:
        copy.start()
    full.wait()
    choices = []
    for chosen, entries in plan["moves"]:
        moves = piece_moves(plan, index, slab, entries, w_refs, wall, 3 * kind * half, 3 * half)
        choices.append((chosen, [pltpu.make_async_copy(a, b, wsems.at[n]) for n, (a, b) in enumerate(moves)]))

    def on_choice(act):
        for chosen, moves in choices:
            @pl.when(upper == chosen)
            def _():
                for copy in moves:
                    act(copy)

    on_choice(lambda copy: copy.start())
    gap = lanes - half
    if gap:
        qt[half:, :] = jnp.zeros((gap, qt.shape[1]), qt.dtype)
        kn[:, half:] = jnp.zeros((kn.shape[0], gap), kn.dtype)
    for copy in sources:
        copy.wait()
    on_choice(lambda copy: copy.wait())

    tokens = groups * slot
    own = xs[...].reshape(tokens, width)
    parts = [wall[n * half : (n + 1) * half, :] for n in range(3)]
    qt[:half, :] = nt_dot(parts[0], own).astype(qt.dtype)
    kn[:, :half] = nt_dot(own, parts[1]).astype(kn.dtype)
    vt[...] = nt_dot(parts[2], own).astype(vt.dtype)

    def one_group(g, carry):
        here = pl.ds(pl.multiple_of(g * slot, slot), slot)
        row = lax.broadcasted_iota(jnp.int32, (slot, slot), 0)
        column = lax.broadcasted_iota(jnp.int32, (slot, slot), 1)
        same = (row % rows) // frames == (column % rows) // frames
        scores = []
        for head in range(heads_half):
            first, last, low, high = head_window(head, head_size, 0)
            keys = masked(kn[here, low:high], first, last, low)
            scores.append(jnp.dot(keys, qt[low:high, here], preferred_element_type=jnp.float32))
        probs = [softmax(score, same, scale).astype(jnp.bfloat16) for score in scores]
        results = []
        for head, prob in enumerate(probs):
            values = vt[head * head_size : (head + 1) * head_size, here]
            results.append(jnp.dot(values, prob, preferred_element_type=jnp.float32))
        if gap:
            space = jnp.zeros((gap, slot), jnp.float32)
            results = [space] + results if kind else results + [space]
        result = jnp.concatenate(results, axis=0).T.astype(jnp.bfloat16)
        earlier, later = result[: slot // 2], result[slot // 2 :]
        out_refs[0][g] = jnp.where(upper, later, earlier).reshape(count // 2, rows, lanes)
        out_refs[1][g] = jnp.where(upper, earlier, later).reshape(count // 2, rows, lanes)
        return carry

    lax.fori_loop(0, groups, one_group, 0, unroll=True)


def merge_kernel(first_z, index_ref, first_ref, second_ref, *out_refs):
    index = index_ref[0]
    lanes = first_ref.shape[-1]
    for n, out_ref in enumerate(out_refs):
        cut = 2 * lanes - out_ref.shape[-1]
        for sibling in range(2):
            at = lax.rem(lax.bitwise_xor(index, 2 * (first_z + n) + sibling), 2 * len(out_refs))
            first, second = first_ref[:, at], second_ref[:, at]
            if cut:
                out_ref[sibling, ..., : lanes - cut] = first[..., : lanes - cut]
                out_ref[sibling, ..., lanes - cut : lanes] = first[..., lanes - cut :] + second[..., :cut]
                out_ref[sibling, ..., lanes:] = second[..., cut:]
            else:
                out_ref[sibling, ..., :lanes] = first
                out_ref[sibling, ..., lanes:] = second


def gather_out_kernel(moves, index_ref, *refs):
    w_refs, wall, sems = refs[:-2], refs[-2], refs[-1]
    copies = []
    for n, (operand, at, owner) in enumerate(moves):
        source = w_refs[operand]
        for step in at:
            source = source.at[step]
        size = source.shape[0]
        row = lax.bitwise_xor(index_ref[0], owner[0]) * size if isinstance(owner, tuple) else owner * size
        copies.append(pltpu.make_async_copy(source, wall.at[pl.ds(pl.multiple_of(row, ROWS), size)], sems.at[n]))
    for copy in copies:
        copy.start()
    for copy in copies:
        copy.wait()


def restore_kernel(count, index_ref, tokens_ref, modulation_ref, wall, *refs):
    refs = list(refs)
    in_refs = [refs.pop(0) for _ in range(count)]
    in_refs = [ref.at[n % ref.shape[0]] for n, ref in enumerate(in_refs)]
    out_ref, mixed = refs
    index = index_ref[0]
    frames = tokens_ref.shape[0]
    groups, rows, width = in_refs[0].shape
    block_rows = groups * rows
    positions = block_rows // frames
    attended = jnp.concatenate([in_ref[...].reshape(block_rows, width) for in_ref in in_refs], axis=0)
    projected = nt_dot(attended, wall[...]).astype(jnp.bfloat16).astype(jnp.float32)
    for t in range(width // LANES):
        mixed[t] = projected[:, t * LANES : (t + 1) * LANES]
    for d in range(count):
        start = pl.multiple_of(lax.bitwise_xor(index, d) * positions, positions)
        for f in range(frames):
            values = tokens_ref[f, pl.ds(start, positions), :].astype(jnp.float32)
            rows_of = pl.ds(d * block_rows + f, positions, stride=frames)
            update = jnp.concatenate([mixed[t, rows_of, :] for t in range(width // LANES)], axis=1)
            result = values + modulation_ref[2, f : f + 1, :] * update
            out_ref[f, pl.ds(start, positions), :] = result.astype(out_ref.dtype)


def per_device(video_tokens, modulation, qkv_weight, out_weight):
    frames, positions, width = video_tokens.shape
    count, slabs = lax.axis_size("seq"), lax.axis_size("slab")
    index, slab = lax.axis_index("seq"), lax.axis_index("slab")
    block_positions = positions // count
    block_rows = block_positions * frames
    groups = block_rows // ROWS
    block = jax.ShapeDtypeStruct((groups, ROWS, width), jnp.bfloat16)
    own_index = jnp.stack([index, slab]).astype(jnp.int32)
    kinds = jnp.transpose(modulation, (1, 0, 2))
    smem = pl.BlockSpec(memory_space=pltpu.SMEM)
    vmem = pl.BlockSpec(memory_space=pltpu.VMEM)
    anywhere = pl.BlockSpec(memory_space=pl.ANY)
    params = pltpu.CompilerParams(vmem_limit_bytes=VMEM_BYTES)

    def hop(value, seq_xor, slab_xor=0):
        pairs = [(s * count + i, (s ^ slab_xor) * count + (i ^ seq_xor)) for s in range(slabs) for i in range(count)]
        return lax.ppermute(value, ("slab", "seq"), pairs)

    half = width // 2
    lanes = padded(half)
    columns, outs = qkv_weight.shape[1], out_weight.shape[1]
    chips = count // 2
    middle = chips
    size = -(-columns // (slabs * ROWS)) * ROWS
    over = slabs * size - columns
    shared = columns % ROWS == 0 and outs % ROWS == 0 and over < size and chips == 4 and slabs == 4
    tie = lax.optimization_barrier

    keep, give = pl.pallas_call(
        norm_kernel,
        out_shape=[jax.ShapeDtypeStruct((chips,) + block.shape, block.dtype)] * 2,
        in_specs=[smem, vmem, vmem],
        out_specs=[vmem] * 2,
        scratch_shapes=[pltpu.VMEM((width // LANES, block_rows, LANES), jnp.float32)],
        compiler_params=params,
        name="norm",
    )(own_index, video_tokens, kinds)
    swapped = hop(give, 1)
    pair = [jnp.stack([keep[z], swapped[z]]) for z in range(chips)]

    def to_neighbour(value, step):
        pairs = [(s * count + i, (s + (step if i < middle else -step)) % slabs * count + i)
                 for s in range(slabs) for i in range(count)]
        return lax.ppermute(value, ("slab", "seq"), pairs)

    def following_of(value):
        return to_neighbour(value, -1)

    wide, narrow = qkv_weight.T, out_weight.T
    out_operands, out_moves = [], []
    operands, moves = [], []
    if shared:
        mine = lax.dynamic_slice_in_dim(wide, jnp.minimum(slab * size, columns - size), size, 0)

        def with_sibling(value, entries, other):
            for sibling in range(2):
                operands.append(other if sibling else value)
                for at, length, z, part in entries:
                    part = part if part is None else (part, 2 * z + sibling)
                    moves.append((len(operands) - 1, at, length, (2 * z) ^ sibling, part))

        x, y = 1, 2
        blocks = [pair[0], None, None, None]
        far = hop(mine, 4)
        wide_other = hop(wide, 1)
        blocks[1] = hop(pair[1], 2)
        following = [following_of(pair[0])]
        near_and_far = jnp.stack([mine, far])
        blocks[1], far, near_and_far, pair, wide_other, following, narrow = tie(
            (blocks[1], far, near_and_far, pair, wide_other, following, narrow))
        ax, ay = hop(far, 0, x), hop(far, 0, y)
        rest = hop(near_and_far, 2)
        blocks[2] = hop(pair[2], 4)
        following.append(following_of(blocks[1]))
        ax, ay, rest, blocks[2], following, pair[3] = tie((ax, ay, rest, blocks[2], following, pair[3]))
        bx, by = hop(rest, 0, x), hop(rest, 0, y)
        both = jnp.concatenate([pair[3].reshape(-1, ROWS, width), narrow.reshape(-1, ROWS, width)], axis=0)
        blocks[3] = hop(both, 6)
        early = [hop(far, 1), hop(rest, 1)]
        narrow_other = hop(narrow, 1)
        ay, bx, by, early, ax = tie((ay, bx, by, early, ax))
        axy = hop(ay, 0, x)
        bxy = jnp.stack([hop(bx[0], 0, y), hop(by[1], 0, x)])
        swaps = [early[0], hop(ax, 1), hop(ay, 1), None]
        swaps += [early[1], hop(bx, 1), hop(by, 1)]
        with_sibling(wide, [((), columns, 0, None)], wide_other)
        for e, value in enumerate((far, ax, ay)):
            with_sibling(value, [((), size, 2, e)], swaps[e])
        for e, value in enumerate((rest, bx, by)):
            with_sibling(value, [((n,), size, z, e) for n, z in enumerate((1, 3))], swaps[4 + e])
        full_rows = 6 * half + count * over
        plan = dict(half=half, columns=columns, over=over, pieces=slabs, moves=moves)
        full = pl.pallas_call(
            functools.partial(gather_kernel, plan),
            out_shape=jax.ShapeDtypeStruct((full_rows, width), jnp.bfloat16),
            in_specs=[smem] + [anywhere] * len(operands),
            out_specs=anywhere,
            scratch_shapes=[pltpu.SemaphoreType.DMA((2 * len(moves),))],
            compiler_params=params,
            cost_estimate=pl.CostEstimate(flops=0, bytes_accessed=0, transcendentals=0),
            name="gather",
        )(own_index, *operands)
        operands.clear()
        moves.clear()
        bxy, swaps, blocks[3], full = tie((bxy, swaps, blocks[3], full))
        out_far = blocks[3][2 * groups :].reshape(narrow.shape)
        swaps.append(hop(bxy, 1))
        swaps[3] = hop(axy, 1)
        with_sibling(axy, [((), size, 2, 3)], swaps[3])
        with_sibling(bxy, [((n,), size, z, 3) for n, z in enumerate((1, 3))], swaps[7])
        near_half = [m for m in moves if m[3] < middle]
        far_half = [m for m in moves if m[3] >= middle]
        by_kind = [[(False, near_half), (True, far_half)], [(True, near_half), (False, far_half)]]
    else:
        full = lax.all_gather(wide, "seq", axis=0, tiled=True)
        by_kind = [[], []]
        out_operands = [lax.all_gather(narrow, "seq", axis=0, tiled=True)]
        out_moves = [(0, (), 0)]
        blocks = [hop(pair[z], 2 * z) if z else pair[z] for z in range(chips)]
        following = [following_of(value) for value in blocks[: chips // 2]]

    tokens = count * block_rows

    def attention(kind, inputs):
        inputs = [value.reshape((-1,) + block.shape[1:]) for value in inputs]
        plan = dict(kind=kind, weights=len(operands), inputs=len(inputs), half=half, moves=by_kind[kind],
                    columns=columns, over=over, pieces=slabs)
        copies = max([1] + [2 * len(entries) for _, entries in by_kind[kind]])
        return pl.pallas_call(
            functools.partial(block_kernel, plan, frames),
            out_shape=[jax.ShapeDtypeStruct((groups, middle, ROWS, lanes), jnp.bfloat16)] * 2,
            in_specs=[smem] + [anywhere] * (len(inputs) + 1 + len(operands)),
            out_specs=[vmem] * 2,
            scratch_shapes=[
                pltpu.VMEM((groups, count, ROWS, width), jnp.bfloat16),
                pltpu.VMEM((3 * half + count * over, width), jnp.bfloat16),
                pltpu.VMEM((lanes, tokens), jnp.bfloat16),
                pltpu.VMEM((tokens, lanes), jnp.bfloat16),
                pltpu.VMEM((half, tokens), jnp.bfloat16),
                pltpu.SemaphoreType.DMA((count,)),
                pltpu.SemaphoreType.DMA((1,)),
                pltpu.SemaphoreType.DMA((copies,)),
            ],
            compiler_params=params,
            cost_estimate=pl.CostEstimate(flops=SPACE_FLOPS, bytes_accessed=8 * 1024 * 1024,
                                          transcendentals=0),
            name=("windowed", "shifted")[kind],
        )(own_index, *inputs, full, *operands)

    second_near, second_far = attention(1, blocks + following)
    if shared:
        out_rest = hop(jnp.stack([narrow, out_far]), 2)
    second_near = to_neighbour(second_near, 1)
    first_near, first_far = attention(0, blocks)
    def merged(first_z, first, second, flops):
        return pl.pallas_call(
            functools.partial(merge_kernel, first_z),
            out_shape=[jax.ShapeDtypeStruct((2,) + block.shape, block.dtype)] * (chips // 2),
            in_specs=[smem] + [vmem] * 2,
            out_specs=[vmem] * (chips // 2),
            compiler_params=params,
            cost_estimate=pl.CostEstimate(flops=flops, bytes_accessed=4 * 1024 * 1024, transcendentals=0),
            name="merge",
        )(own_index, first, second)

    sent_far = merged(chips // 2, first_far, second_far, 0)
    if shared:
        out_rest, second_near = tie((out_rest, second_near))
    sent_near = merged(0, first_near, second_near, 0)
    sent = sent_near + sent_far
    arrived = [hop(sent[z], 2 * z) if z else sent[z] for z in range(chips // 2)]
    singles = [hop(sent[z][n], 2 * z + n)[None] for z in range(chips // 2, chips) for n in range(2)]
    if shared:
        out_operands = [narrow, narrow_other, out_far, hop(out_far, 1), out_rest, hop(out_rest, 1)]
        out_moves = [(0, (), (0,)), (1, (), (1,)), (2, (), (6,)), (3, (), (7,)), (4, (0,), (2,)), (5, (0,), (3,)),
                     (4, (1,), (4,)), (5, (1,), (5,))]
    out_full = pl.pallas_call(
        functools.partial(gather_out_kernel, out_moves),
        out_shape=jax.ShapeDtypeStruct((width, width), jnp.bfloat16),
        in_specs=[smem] + [anywhere] * len(out_operands),
        out_specs=anywhere,
        scratch_shapes=[pltpu.SemaphoreType.DMA((len(out_moves),))],
        compiler_params=params,
        name="gather_out",
    )(own_index, *out_operands)
    if shared:
        arrived, singles = tie((arrived, singles))
    returned = []
    for value in arrived:
        returned += [value, hop(value, 1)]
    returned += singles
    return pl.pallas_call(
        functools.partial(restore_kernel, count),
        out_shape=jax.ShapeDtypeStruct(video_tokens.shape, video_tokens.dtype),
        in_specs=[smem] + [vmem] * (3 + count),
        out_specs=vmem,
        scratch_shapes=[pltpu.VMEM((width // LANES, tokens, LANES), jnp.float32)],
        compiler_params=params,
        name="restore",
    )(own_index, video_tokens, kinds, out_full, *returned)


def solution(mesh):
    return jax.shard_map(
        per_device,
        mesh=mesh,
        in_specs=(
            P(("slab", "seq"), None, None),
            P(("slab", "seq"), None, None),
            P(None, "seq"),
            P(None, "seq"),
        ),
        out_specs=P(("slab", "seq"), None, None),
        check_vma=False,
    )
```

```python
import functools

import jax
import jax.numpy as jnp
from jax import lax
from jax.experimental import pallas as pl
from jax.experimental.pallas import tpu as pltpu
from jax.sharding import PartitionSpec as P

H = 16
FRS = 32
EPSILON = 1e-06
LANES = 128
ROWS = 16
SPACE_FLOPS = 40 * 10**9
VMEM_BYTES = 24 * 1024 * 1024


def padded(width):
    return -(-width // LANES) * LANES


def norm_kernel(index_ref, tokens_ref, modulation_ref, keep_ref, give_ref, mixed):
    frames = tokens_ref.shape[0]
    chips, groups, rows, width = keep_ref.shape
    positions = groups * rows // frames
    index = index_ref[0]
    for d in range(2 * chips):
        out_ref = (keep_ref, give_ref)[d % 2]
        start = pl.multiple_of(lax.bitwise_xor(index, d) * positions, positions)
        for f in range(frames):
            values = tokens_ref[f, pl.ds(start, positions), :].astype(jnp.float32)
            average = jnp.mean(values, axis=-1, keepdims=True)
            centered = values - average
            variance = jnp.mean(centered * centered, axis=-1, keepdims=True)
            normed = centered * lax.rsqrt(variance + EPSILON)
            result = normed * (1.0 + modulation_ref[1, f : f + 1, :]) + modulation_ref[0, f : f + 1, :]
            for t in range(width // LANES):
                mixed[t, pl.ds(f, positions, stride=frames), :] = result[:, t * LANES : (t + 1) * LANES]
        for t in range(width // LANES):
            part = mixed[t].astype(out_ref.dtype).reshape(groups, rows, LANES)
            out_ref[d // 2, :, :, t * LANES : (t + 1) * LANES] = part


def nt_dot(left, right):
    return lax.dot_general(left, right, (((1,), (1,)), ((), ())), preferred_element_type=jnp.float32)


def head_window(head, head_size, shift):
    first = shift + head * head_size
    last = first + head_size
    low = first // LANES * LANES
    return first, last, low, padded(last)


def masked(values, first, last, low):
    lane = lax.broadcasted_iota(jnp.int32, values.shape, 1) + low
    return jnp.where((lane >= first) & (lane < last), values, jnp.zeros_like(values))


def softmax(scores, same, scale):
    scores = jnp.where(same, scores, -jnp.inf)
    top = jnp.max(scores, axis=0, keepdims=True)
    exponent = jnp.exp((scores - top) * scale)
    total = jnp.sum(exponent, axis=0, keepdims=True)
    return exponent * (1.0 / total)


def piece_moves(plan, index, slab, entries, w_refs, wall, first_row, sems):
    moves = []
    for n, (operand, at, size, owner, part) in enumerate(entries):
        source = w_refs[operand]
        for step in at:
            source = source.at[step]
        base = lax.bitwise_xor(index, owner) * plan["columns"] - first_row
        if part is None:
            moves.append((None, pltpu.make_async_copy(source, wall.at[pl.ds(pl.multiple_of(base, ROWS), size)], sems.at[n])))
            continue
        piece, over = lax.bitwise_xor(slab, part), plan["over"]
        row = pl.multiple_of(base + piece * size, ROWS)
        whole = pltpu.make_async_copy(source, wall.at[pl.ds(row, size)], sems.at[n])
        if not over:
            moves.append((None, whole))
            continue
        ends = piece == plan["pieces"] - 1
        rest = pltpu.make_async_copy(source.at[pl.ds(over, size - over)], wall.at[pl.ds(row, size - over)], sems.at[n])
        moves += [(jnp.logical_not(ends), whole), (ends, rest)]
    return moves


def on_moves(moves, act):
    for condition, copy in moves:
        if condition is None:
            act(copy)
        else:
            pl.when(condition)(functools.partial(act, copy))


def gather_kernel(plan, index_ref, *refs):
    w_refs, wall, sems = refs[:-2], refs[-2], refs[-1]
    moves = piece_moves(plan, index_ref[0], index_ref[1], plan["moves"], w_refs, wall, 0, sems)
    on_moves(moves, lambda copy: copy.start())
    on_moves(moves, lambda copy: copy.wait())


def block_kernel(plan, frames, index_ref, *refs):
    kind, weights, half = plan["kind"], plan["weights"], plan["half"]
    refs = list(refs)
    x_refs = [refs.pop(0) for _ in range(plan["inputs"])]
    refs.pop(0)
    w_refs = [refs.pop(0) for _ in range(weights)]
    out_refs = [refs.pop(0) for _ in range(2)]
    wall = refs.pop(0)
    xs, qt, kn, vt, sems, wsems = refs
    groups, count, rows, width = xs.shape
    lanes = qt.shape[0]
    heads_half = H // 2
    head_size = width // H
    scale = head_size ** (-0.5)
    slot = count * rows
    index, slab = index_ref[0], index_ref[1]
    upper = index >= count // 2
    sources = []
    for d in range(count):
        owner = lax.bitwise_xor(index, d)
        near = kind == 1 and d < count // 2
        source = x_refs[count // 2 + d // 2 if near else d // 2].at[pl.ds(d % 2 * groups, groups)]
        sources.append(pltpu.make_async_copy(source, xs.at[:, owner], sems.at[d]))
    for copy in sources:
        copy.start()
    choices = []
    for chosen, entries in plan["moves"]:
        choices.append((chosen, piece_moves(plan, index, slab, entries, w_refs, wall, 0, wsems)))

    def on_choice(act):
        for chosen, moves in choices:
            pl.when(upper == chosen)(functools.partial(on_moves, moves, act))

    on_choice(lambda copy: copy.start())
    gap = lanes - half
    if gap:
        qt[half:, :] = jnp.zeros((gap, qt.shape[1]), qt.dtype)
        kn[:, half:] = jnp.zeros((kn.shape[0], gap), kn.dtype)
    for copy in sources:
        copy.wait()
    on_choice(lambda copy: copy.wait())

    tokens = groups * slot
    own = xs[...].reshape(tokens, width)
    parts = [wall[(3 * kind + n) * half : (3 * kind + n + 1) * half, :] for n in range(3)]
    qt[:half, :] = nt_dot(parts[0], own).astype(qt.dtype)
    kn[:, :half] = nt_dot(own, parts[1]).astype(kn.dtype)
    vt[...] = nt_dot(parts[2], own).astype(vt.dtype)

    def one_group(g, carry):
        here = pl.ds(pl.multiple_of(g * slot, slot), slot)
        row = lax.broadcasted_iota(jnp.int32, (slot, slot), 0)
        column = lax.broadcasted_iota(jnp.int32, (slot, slot), 1)
        same = (row % rows) // frames == (column % rows) // frames
        scores = []
        for head in range(heads_half):
            first, last, low, high = head_window(head, head_size, 0)
            keys = masked(kn[here, low:high], first, last, low)
            scores.append(jnp.dot(keys, qt[low:high, here], preferred_element_type=jnp.float32))
        probs = [softmax(score, same, scale).astype(jnp.bfloat16) for score in scores]
        results = []
        for head, prob in enumerate(probs):
            values = vt[head * head_size : (head + 1) * head_size, here]
            results.append(jnp.dot(values, prob, preferred_element_type=jnp.float32))
        if gap:
            space = jnp.zeros((gap, slot), jnp.float32)
            results = [space] + results if kind else results + [space]
        result = jnp.concatenate(results, axis=0).T.astype(jnp.bfloat16)
        earlier, later = result[: slot // 2], result[slot // 2 :]
        out_refs[0][g] = jnp.where(upper, later, earlier).reshape(count // 2, rows, lanes)
        out_refs[1][g] = jnp.where(upper, earlier, later).reshape(count // 2, rows, lanes)
        return carry

    lax.fori_loop(0, groups, one_group, 0, unroll=True)


def merge_kernel(first_z, index_ref, first_ref, second_ref, *out_refs):
    index = index_ref[0]
    lanes = first_ref.shape[-1]
    for n, out_ref in enumerate(out_refs):
        cut = 2 * lanes - out_ref.shape[-1]
        for sibling in range(2):
            at = lax.rem(lax.bitwise_xor(index, 2 * (first_z + n) + sibling), 2 * len(out_refs))
            first, second = first_ref[:, at], second_ref[:, at]
            if cut:
                out_ref[sibling, ..., : lanes - cut] = first[..., : lanes - cut]
                out_ref[sibling, ..., lanes - cut : lanes] = first[..., lanes - cut :] + second[..., :cut]
                out_ref[sibling, ..., lanes:] = second[..., cut:]
            else:
                out_ref[sibling, ..., :lanes] = first
                out_ref[sibling, ..., lanes:] = second


def gather_out_kernel(moves, index_ref, *refs):
    w_refs, wall, sems = refs[:-2], refs[-2], refs[-1]
    copies = []
    for n, (operand, at, owner) in enumerate(moves):
        source = w_refs[operand]
        for step in at:
            source = source.at[step]
        size = source.shape[0]
        row = lax.bitwise_xor(index_ref[0], owner[0]) * size if isinstance(owner, tuple) else owner * size
        copies.append(pltpu.make_async_copy(source, wall.at[pl.ds(pl.multiple_of(row, ROWS), size)], sems.at[n]))
    for copy in copies:
        copy.start()
    for copy in copies:
        copy.wait()


def restore_kernel(count, index_ref, tokens_ref, modulation_ref, wall, *refs):
    refs = list(refs)
    in_refs = [refs.pop(0) for _ in range(count)]
    in_refs = [ref.at[n % ref.shape[0]] for n, ref in enumerate(in_refs)]
    out_ref, mixed = refs
    index = index_ref[0]
    frames = tokens_ref.shape[0]
    groups, rows, width = in_refs[0].shape
    block_rows = groups * rows
    positions = block_rows // frames
    attended = jnp.concatenate([in_ref[...].reshape(block_rows, width) for in_ref in in_refs], axis=0)
    projected = nt_dot(attended, wall[...]).astype(jnp.bfloat16).astype(jnp.float32)
    for t in range(width // LANES):
        mixed[t] = projected[:, t * LANES : (t + 1) * LANES]
    for d in range(count):
        start = pl.multiple_of(lax.bitwise_xor(index, d) * positions, positions)
        for f in range(frames):
            values = tokens_ref[f, pl.ds(start, positions), :].astype(jnp.float32)
            rows_of = pl.ds(d * block_rows + f, positions, stride=frames)
            update = jnp.concatenate([mixed[t, rows_of, :] for t in range(width // LANES)], axis=1)
            result = values + modulation_ref[2, f : f + 1, :] * update
            out_ref[f, pl.ds(start, positions), :] = result.astype(out_ref.dtype)


def per_device(video_tokens, modulation, qkv_weight, out_weight):
    frames, positions, width = video_tokens.shape
    count, slabs = lax.axis_size("seq"), lax.axis_size("slab")
    index, slab = lax.axis_index("seq"), lax.axis_index("slab")
    block_positions = positions // count
    block_rows = block_positions * frames
    groups = block_rows // ROWS
    block = jax.ShapeDtypeStruct((groups, ROWS, width), jnp.bfloat16)
    own_index = jnp.stack([index, slab]).astype(jnp.int32)
    kinds = jnp.transpose(modulation, (1, 0, 2))
    smem = pl.BlockSpec(memory_space=pltpu.SMEM)
    vmem = pl.BlockSpec(memory_space=pltpu.VMEM)
    anywhere = pl.BlockSpec(memory_space=pl.ANY)
    params = pltpu.CompilerParams(vmem_limit_bytes=VMEM_BYTES)

    def hop(value, seq_xor, slab_xor=0):
        pairs = [(s * count + i, (s ^ slab_xor) * count + (i ^ seq_xor)) for s in range(slabs) for i in range(count)]
        return lax.ppermute(value, ("slab", "seq"), pairs)

    half = width // 2
    lanes = padded(half)
    columns, outs = qkv_weight.shape[1], out_weight.shape[1]
    chips = count // 2
    middle = chips
    size = -(-columns // (slabs * ROWS)) * ROWS
    over = slabs * size - columns
    shared = columns % ROWS == 0 and outs % ROWS == 0 and over < size and chips == 4 and slabs == 4
    tie = lax.optimization_barrier

    keep, give = pl.pallas_call(
        norm_kernel,
        out_shape=[jax.ShapeDtypeStruct((chips,) + block.shape, block.dtype)] * 2,
        in_specs=[smem, vmem, vmem],
        out_specs=[vmem] * 2,
        scratch_shapes=[pltpu.VMEM((width // LANES, block_rows, LANES), jnp.float32)],
        compiler_params=params,
        name="norm",
    )(own_index, video_tokens, kinds)
    swapped = hop(give, 1)
    pair = [jnp.stack([keep[z], swapped[z]]) for z in range(chips)]

    def to_neighbour(value, step):
        pairs = [(s * count + i, (s + (step if i < middle else -step)) % slabs * count + i)
                 for s in range(slabs) for i in range(count)]
        return lax.ppermute(value, ("slab", "seq"), pairs)

    def following_of(value):
        return to_neighbour(value, -1)

    wide, narrow = qkv_weight.T, out_weight.T
    out_operands, out_moves = [], []
    operands, moves = [], []
    if shared:
        mine = lax.dynamic_slice_in_dim(wide, jnp.minimum(slab * size, columns - size), size, 0)

        def with_sibling(value, entries, other):
            for sibling in range(2):
                operands.append(other if sibling else value)
                for at, length, z, part in entries:
                    moves.append((len(operands) - 1, at, length, (2 * z) ^ sibling, part))

        x, y = 1, 2
        blocks = [pair[0], None, None, None]
        far = hop(mine, 4)
        wide_other = hop(wide, 1)
        blocks[1] = hop(pair[1], 2)
        following = [following_of(pair[0])]
        near_and_far = jnp.stack([mine, far])
        blocks[1], far, near_and_far, pair, wide_other, following, narrow = tie(
            (blocks[1], far, near_and_far, pair, wide_other, following, narrow))
        ax, ay = hop(far, 0, x), hop(far, 0, y)
        rest = hop(near_and_far, 2)
        blocks[2] = hop(pair[2], 4)
        following.append(following_of(blocks[1]))
        ax, ay, rest, blocks[2], following, pair[3] = tie((ax, ay, rest, blocks[2], following, pair[3]))
        bx, by = hop(rest, 0, x), hop(rest, 0, y)
        both = jnp.concatenate([pair[3].reshape(-1, ROWS, width), narrow.reshape(-1, ROWS, width)], axis=0)
        blocks[3] = hop(both, 6)
        early = [hop(far, 1), hop(rest, 1)]
        narrow_other = hop(narrow, 1)
        ay, bx, by, early, ax = tie((ay, bx, by, early, ax))
        axy = hop(ay, 0, x)
        bxy = jnp.stack([hop(bx[0], 0, y), hop(by[1], 0, x)])
        swaps = [early[0], hop(ax, 1), hop(ay, 1), None]
        swaps += [early[1], hop(bx, 1), hop(by, 1)]
        with_sibling(wide, [((), columns, 0, None)], wide_other)
        for e, value in enumerate((far, ax, ay)):
            with_sibling(value, [((), size, 2, e)], swaps[e])
        for e, value in enumerate((rest, bx, by)):
            with_sibling(value, [((n,), size, z, e) for n, z in enumerate((1, 3))], swaps[4 + e])
        full_rows = 6 * half
        plan = dict(half=half, columns=columns, over=over, pieces=slabs, moves=moves)
        full = pl.pallas_call(
            functools.partial(gather_kernel, plan),
            out_shape=jax.ShapeDtypeStruct((full_rows, width), jnp.bfloat16),
            in_specs=[smem] + [anywhere] * len(operands),
            out_specs=anywhere,
            scratch_shapes=[pltpu.SemaphoreType.DMA((len(moves),))],
            compiler_params=params,
            cost_estimate=pl.CostEstimate(flops=0, bytes_accessed=0, transcendentals=0),
            name="gather",
        )(own_index, *operands)
        operands.clear()
        moves.clear()
        bxy, swaps, blocks[3], full = tie((bxy, swaps, blocks[3], full))
        out_far = blocks[3][2 * groups :].reshape(narrow.shape)
        swaps.append(hop(bxy, 1))
        swaps[3] = hop(axy, 1)
        with_sibling(axy, [((), size, 2, 3)], swaps[3])
        with_sibling(bxy, [((n,), size, z, 3) for n, z in enumerate((1, 3))], swaps[7])
        near_half = [m for m in moves if m[3] < middle]
        far_half = [m for m in moves if m[3] >= middle]
        by_kind = [[(False, near_half), (True, far_half)], [(True, near_half), (False, far_half)]]
    else:
        full = lax.all_gather(wide, "seq", axis=0, tiled=True)
        by_kind = [[], []]
        out_operands = [lax.all_gather(narrow, "seq", axis=0, tiled=True)]
        out_moves = [(0, (), 0)]
        blocks = [hop(pair[z], 2 * z) if z else pair[z] for z in range(chips)]
        following = [following_of(value) for value in blocks[: chips // 2]]

    tokens = count * block_rows

    def attention(kind, inputs, full):
        inputs = [value.reshape((-1,) + block.shape[1:]) for value in inputs]
        plan = dict(kind=kind, weights=len(operands), inputs=len(inputs), half=half, moves=by_kind[kind],
                    columns=columns, over=over, pieces=slabs)
        copies = max([1] + [len(entries) for _, entries in by_kind[kind]])
        return pl.pallas_call(
            functools.partial(block_kernel, plan, frames),
            out_shape=[jax.ShapeDtypeStruct((groups, middle, ROWS, lanes), jnp.bfloat16)] * 2
            + [jax.ShapeDtypeStruct(full.shape, full.dtype)],
            in_specs=[smem] + [anywhere] * len(inputs) + [vmem] + [anywhere] * len(operands),
            out_specs=[vmem] * 3,
            input_output_aliases={1 + len(inputs): 2},
            scratch_shapes=[
                pltpu.VMEM((groups, count, ROWS, width), jnp.bfloat16),
                pltpu.VMEM((lanes, tokens), jnp.bfloat16),
                pltpu.VMEM((tokens, lanes), jnp.bfloat16),
                pltpu.VMEM((half, tokens), jnp.bfloat16),
                pltpu.SemaphoreType.DMA((count,)),
                pltpu.SemaphoreType.DMA((copies,)),
            ],
            compiler_params=params,
            cost_estimate=pl.CostEstimate(flops=SPACE_FLOPS, bytes_accessed=8 * 1024 * 1024,
                                          transcendentals=0),
            name=("windowed", "shifted")[kind],
        )(own_index, *inputs, full, *operands)

    second_near, second_far, full = attention(1, blocks + following, full)
    if shared:
        out_rest = hop(jnp.stack([narrow, out_far]), 2)
    second_near = to_neighbour(second_near, 1)
    first_near, first_far, full = attention(0, blocks, full)
    def merged(first_z, first, second, flops):
        return pl.pallas_call(
            functools.partial(merge_kernel, first_z),
            out_shape=[jax.ShapeDtypeStruct((2,) + block.shape, block.dtype)] * (chips // 2),
            in_specs=[smem] + [vmem] * 2,
            out_specs=[vmem] * (chips // 2),
            compiler_params=params,
            cost_estimate=pl.CostEstimate(flops=flops, bytes_accessed=4 * 1024 * 1024, transcendentals=0),
            name="merge",
        )(own_index, first, second)

    sent_far = merged(chips // 2, first_far, second_far, 0)
    if shared:
        out_rest, second_near = tie((out_rest, second_near))
    sent_near = merged(0, first_near, second_near, 0)
    sent = sent_near + sent_far
    arrived = [hop(sent[z], 2 * z) if z else sent[z] for z in range(chips // 2)]
    singles = [hop(sent[z][n], 2 * z + n)[None] for z in range(chips // 2, chips) for n in range(2)]
    if shared:
        out_operands = [narrow, narrow_other, out_far, hop(out_far, 1), out_rest, hop(out_rest, 1)]
        out_moves = [(0, (), (0,)), (1, (), (1,)), (2, (), (6,)), (3, (), (7,)), (4, (0,), (2,)), (5, (0,), (3,)),
                     (4, (1,), (4,)), (5, (1,), (5,))]
    out_full = pl.pallas_call(
        functools.partial(gather_out_kernel, out_moves),
        out_shape=jax.ShapeDtypeStruct((width, width), jnp.bfloat16),
        in_specs=[smem] + [anywhere] * len(out_operands),
        out_specs=anywhere,
        scratch_shapes=[pltpu.SemaphoreType.DMA((len(out_moves),))],
        compiler_params=params,
        name="gather_out",
    )(own_index, *out_operands)
    if shared:
        arrived, singles = tie((arrived, singles))
    returned = []
    for value in arrived:
        returned += [value, hop(value, 1)]
    returned += singles
    return pl.pallas_call(
        functools.partial(restore_kernel, count),
        out_shape=jax.ShapeDtypeStruct(video_tokens.shape, video_tokens.dtype),
        in_specs=[smem] + [vmem] * (3 + count),
        out_specs=vmem,
        scratch_shapes=[pltpu.VMEM((width // LANES, tokens, LANES), jnp.float32)],
        compiler_params=params,
        name="restore",
    )(own_index, video_tokens, kinds, out_full, *returned)


def solution(mesh):
    return jax.shard_map(
        per_device,
        mesh=mesh,
        in_specs=(
            P(("slab", "seq"), None, None),
            P(("slab", "seq"), None, None),
            P(None, "seq"),
            P(None, "seq"),
        ),
        out_specs=P(("slab", "seq"), None, None),
        check_vma=False,
    )
```

```python
import functools

import jax
import jax.numpy as jnp
from jax import lax
from jax.experimental import pallas as pl
from jax.experimental.pallas import tpu as pltpu
from jax.sharding import PartitionSpec as P

H = 16
FRS = 32
EPSILON = 1e-06
LANES = 128
ROWS = 16
SPACE_FLOPS = 40 * 10**9
VMEM_BYTES = 24 * 1024 * 1024


def padded(width):
    return -(-width // LANES) * LANES


def norm_kernel(index_ref, tokens_ref, modulation_ref, keep_ref, give_ref, mixed):
    frames = tokens_ref.shape[0]
    chips, groups, rows, width = keep_ref.shape
    positions = groups * rows // frames
    index = index_ref[0]
    for d in range(2 * chips):
        out_ref = (keep_ref, give_ref)[d % 2]
        start = pl.multiple_of(lax.bitwise_xor(index, d) * positions, positions)
        for f in range(frames):
            values = tokens_ref[f, pl.ds(start, positions), :].astype(jnp.float32)
            average = jnp.mean(values, axis=-1, keepdims=True)
            centered = values - average
            variance = jnp.mean(centered * centered, axis=-1, keepdims=True)
            normed = centered * lax.rsqrt(variance + EPSILON)
            result = normed * (1.0 + modulation_ref[1, f : f + 1, :]) + modulation_ref[0, f : f + 1, :]
            for t in range(width // LANES):
                mixed[t, pl.ds(f, positions, stride=frames), :] = result[:, t * LANES : (t + 1) * LANES]
        for t in range(width // LANES):
            part = mixed[t].astype(out_ref.dtype).reshape(groups, rows, LANES)
            out_ref[d // 2, :, :, t * LANES : (t + 1) * LANES] = part


def nt_dot(left, right):
    return lax.dot_general(left, right, (((1,), (1,)), ((), ())), preferred_element_type=jnp.float32)


def head_window(head, head_size, shift):
    first = shift + head * head_size
    last = first + head_size
    low = first // LANES * LANES
    return first, last, low, padded(last)


def masked(values, first, last, low):
    lane = lax.broadcasted_iota(jnp.int32, values.shape, 1) + low
    return jnp.where((lane >= first) & (lane < last), values, jnp.zeros_like(values))


def softmax(scores, same, scale):
    scores = jnp.where(same, scores, -jnp.inf)
    top = jnp.max(scores, axis=0, keepdims=True)
    exponent = jnp.exp((scores - top) * scale)
    total = jnp.sum(exponent, axis=0, keepdims=True)
    return exponent * (1.0 / total)


def piece_moves(plan, index, slab, entries, w_refs, wall, first_row, sems):
    moves = []
    for n, (operand, at, size, owner, part) in enumerate(entries):
        source = w_refs[operand]
        for step in at:
            source = source.at[step]
        base = lax.bitwise_xor(index, owner) * plan["columns"] - first_row
        if part is None:
            moves.append((None, pltpu.make_async_copy(source, wall.at[pl.ds(pl.multiple_of(base, ROWS), size)], sems.at[n])))
            continue
        piece, over = lax.bitwise_xor(slab, part), plan["over"]
        row = pl.multiple_of(base + piece * size, ROWS)
        whole = pltpu.make_async_copy(source, wall.at[pl.ds(row, size)], sems.at[n])
        if not over:
            moves.append((None, whole))
            continue
        ends = piece == plan["pieces"] - 1
        rest = pltpu.make_async_copy(source.at[pl.ds(over, size - over)], wall.at[pl.ds(row, size - over)], sems.at[n])
        moves += [(jnp.logical_not(ends), whole), (ends, rest)]
    return moves


def on_moves(moves, act):
    for condition, copy in moves:
        if condition is None:
            act(copy)
        else:
            pl.when(condition)(functools.partial(act, copy))


def gather_kernel(plan, index_ref, *refs):
    w_refs, wall, sems = refs[:-2], refs[-2], refs[-1]
    moves = piece_moves(plan, index_ref[0], index_ref[1], plan["moves"], w_refs, wall, 0, sems)
    on_moves(moves, lambda copy: copy.start())
    on_moves(moves, lambda copy: copy.wait())


def block_kernel(plan, frames, index_ref, *refs):
    kind, weights, half = plan["kind"], plan["weights"], plan["half"]
    refs = list(refs)
    x_refs = [refs.pop(0) for _ in range(plan["inputs"])]
    refs.pop(0)
    w_refs = [refs.pop(0) for _ in range(weights)]
    out_refs = [refs.pop(0) for _ in range(2)]
    wall = refs.pop(0)
    xs, qt, kn, vt, sems, wsems = refs
    groups, count, rows, width = xs.shape
    lanes = qt.shape[0]
    heads_half = H // 2
    head_size = width // H
    scale = head_size ** (-0.5)
    slot = count * rows
    index, slab = index_ref[0], index_ref[1]
    upper = index >= count // 2
    sources = []
    for d in range(count):
        owner = lax.bitwise_xor(index, d)
        near = kind == 1 and d < count // 2
        source = x_refs[count // 2 + d // 2 if near else d // 2].at[pl.ds(d % 2 * groups, groups)]
        sources.append(pltpu.make_async_copy(source, xs.at[:, owner], sems.at[d]))
    for copy in sources:
        copy.start()
    choices = []
    for chosen, entries in plan["moves"]:
        choices.append((chosen, piece_moves(plan, index, slab, entries, w_refs, wall, 0, wsems)))

    def on_choice(act):
        for chosen, moves in choices:
            pl.when(upper == chosen)(functools.partial(on_moves, moves, act))

    on_choice(lambda copy: copy.start())
    gap = lanes - half
    if gap:
        qt[half:, :] = jnp.zeros((gap, qt.shape[1]), qt.dtype)
        kn[:, half:] = jnp.zeros((kn.shape[0], gap), kn.dtype)
    for copy in sources:
        copy.wait()
    on_choice(lambda copy: copy.wait())

    tokens = groups * slot
    own = xs[...].reshape(tokens, width)
    parts = [wall[(3 * kind + n) * half : (3 * kind + n + 1) * half, :] for n in range(3)]
    qt[:half, :] = nt_dot(parts[0], own).astype(qt.dtype)
    kn[:, :half] = nt_dot(own, parts[1]).astype(kn.dtype)
    vt[...] = nt_dot(parts[2], own).astype(vt.dtype)

    def one_group(g, carry):
        here = pl.ds(pl.multiple_of(g * slot, slot), slot)
        row = lax.broadcasted_iota(jnp.int32, (slot, slot), 0)
        column = lax.broadcasted_iota(jnp.int32, (slot, slot), 1)
        same = (row % rows) // frames == (column % rows) // frames
        scores = []
        for head in range(heads_half):
            first, last, low, high = head_window(head, head_size, 0)
            keys = masked(kn[here, low:high], first, last, low)
            scores.append(jnp.dot(keys, qt[low:high, here], preferred_element_type=jnp.float32))
        probs = [softmax(score, same, scale).astype(jnp.bfloat16) for score in scores]
        results = []
        for head, prob in enumerate(probs):
            values = vt[head * head_size : (head + 1) * head_size, here]
            results.append(jnp.dot(values, prob, preferred_element_type=jnp.float32))
        if gap:
            space = jnp.zeros((gap, slot), jnp.float32)
            results = [space] + results if kind else results + [space]
        result = jnp.concatenate(results, axis=0).T.astype(jnp.bfloat16)
        earlier, later = result[: slot // 2], result[slot // 2 :]
        out_refs[0][g] = jnp.where(upper, later, earlier).reshape(count // 2, rows, lanes)
        out_refs[1][g] = jnp.where(upper, earlier, later).reshape(count // 2, rows, lanes)
        return carry

    lax.fori_loop(0, groups, one_group, 0, unroll=True)


def merge_kernel(first_z, index_ref, first_ref, second_ref, *out_refs):
    index = index_ref[0]
    lanes = first_ref.shape[-1]
    for n, out_ref in enumerate(out_refs):
        cut = 2 * lanes - out_ref.shape[-1]
        for sibling in range(2):
            at = lax.rem(lax.bitwise_xor(index, 2 * (first_z + n) + sibling), 2 * len(out_refs))
            first, second = first_ref[:, at], second_ref[:, at]
            if cut:
                out_ref[sibling, ..., : lanes - cut] = first[..., : lanes - cut]
                out_ref[sibling, ..., lanes - cut : lanes] = first[..., lanes - cut :] + second[..., :cut]
                out_ref[sibling, ..., lanes:] = second[..., cut:]
            else:
                out_ref[sibling, ..., :lanes] = first
                out_ref[sibling, ..., lanes:] = second


def gather_out_kernel(moves, index_ref, *refs):
    w_refs, wall, sems = refs[:-2], refs[-2], refs[-1]
    copies = []
    for n, (operand, at, owner) in enumerate(moves):
        source = w_refs[operand]
        for step in at:
            source = source.at[step]
        size = source.shape[0]
        row = lax.bitwise_xor(index_ref[0], owner[0]) * size if isinstance(owner, tuple) else owner * size
        copies.append(pltpu.make_async_copy(source, wall.at[pl.ds(pl.multiple_of(row, ROWS), size)], sems.at[n]))
    for copy in copies:
        copy.start()
    for copy in copies:
        copy.wait()


def restore_kernel(count, index_ref, tokens_ref, modulation_ref, wall, *refs):
    refs = list(refs)
    in_refs = [refs.pop(0) for _ in range(count)]
    in_refs = [ref.at[n % ref.shape[0]] for n, ref in enumerate(in_refs)]
    out_ref, mixed = refs
    index = index_ref[0]
    frames = tokens_ref.shape[0]
    groups, rows, width = in_refs[0].shape
    block_rows = groups * rows
    positions = block_rows // frames
    attended = jnp.concatenate([in_ref[...].reshape(block_rows, width) for in_ref in in_refs], axis=0)
    projected = nt_dot(attended, wall[...]).astype(jnp.bfloat16).astype(jnp.float32)
    for t in range(width // LANES):
        mixed[t] = projected[:, t * LANES : (t + 1) * LANES]
    for d in range(count):
        start = pl.multiple_of(lax.bitwise_xor(index, d) * positions, positions)
        for f in range(frames):
            values = tokens_ref[f, pl.ds(start, positions), :].astype(jnp.float32)
            rows_of = pl.ds(d * block_rows + f, positions, stride=frames)
            update = jnp.concatenate([mixed[t, rows_of, :] for t in range(width // LANES)], axis=1)
            result = values + modulation_ref[2, f : f + 1, :] * update
            out_ref[f, pl.ds(start, positions), :] = result.astype(out_ref.dtype)


def per_device(video_tokens, modulation, qkv_weight, out_weight):
    frames, positions, width = video_tokens.shape
    count, slabs = lax.axis_size("seq"), lax.axis_size("slab")
    index, slab = lax.axis_index("seq"), lax.axis_index("slab")
    block_positions = positions // count
    block_rows = block_positions * frames
    groups = block_rows // ROWS
    block = jax.ShapeDtypeStruct((groups, ROWS, width), jnp.bfloat16)
    own_index = jnp.stack([index, slab]).astype(jnp.int32)
    kinds = jnp.transpose(modulation, (1, 0, 2))
    smem = pl.BlockSpec(memory_space=pltpu.SMEM)
    vmem = pl.BlockSpec(memory_space=pltpu.VMEM)
    anywhere = pl.BlockSpec(memory_space=pl.ANY)
    params = pltpu.CompilerParams(vmem_limit_bytes=VMEM_BYTES)

    def hop(value, seq_xor, slab_xor=0):
        pairs = [(s * count + i, (s ^ slab_xor) * count + (i ^ seq_xor)) for s in range(slabs) for i in range(count)]
        return lax.ppermute(value, ("slab", "seq"), pairs)

    half = width // 2
    lanes = padded(half)
    columns, outs = qkv_weight.shape[1], out_weight.shape[1]
    chips = count // 2
    middle = chips
    size = -(-columns // (slabs * ROWS)) * ROWS
    over = slabs * size - columns
    shared = columns % ROWS == 0 and outs % ROWS == 0 and over < size and chips == 4 and slabs == 4
    tie = lax.optimization_barrier

    keep, give = pl.pallas_call(
        norm_kernel,
        out_shape=[jax.ShapeDtypeStruct((chips,) + block.shape, block.dtype)] * 2,
        in_specs=[smem, vmem, vmem],
        out_specs=[vmem] * 2,
        scratch_shapes=[pltpu.VMEM((width // LANES, block_rows, LANES), jnp.float32)],
        compiler_params=params,
        name="norm",
    )(own_index, video_tokens, kinds)
    swapped = hop(give, 1)
    pair = [jnp.stack([keep[z], swapped[z]]) for z in range(chips)]

    def to_neighbour(value, step):
        pairs = [(s * count + i, (s + (step if i < middle else -step)) % slabs * count + i)
                 for s in range(slabs) for i in range(count)]
        return lax.ppermute(value, ("slab", "seq"), pairs)

    def following_of(value):
        return to_neighbour(value, -1)

    wide, narrow = qkv_weight.T, out_weight.T
    out_operands, out_moves = [], []
    operands, moves = [], []
    if shared:
        mine = lax.dynamic_slice_in_dim(wide, jnp.minimum(slab * size, columns - size), size, 0)

        def with_sibling(value, entries, other):
            for sibling in range(2):
                operands.append(other if sibling else value)
                for at, length, z, part in entries:
                    moves.append((len(operands) - 1, at, length, (2 * z) ^ sibling, part))

        x, y = 1, 2
        blocks = [pair[0], None, None, None]
        far = hop(mine, 4)
        wide_other = hop(wide, 1)
        blocks[1] = hop(pair[1], 2)
        following = [following_of(pair[0])]
        near_and_far = jnp.stack([mine, far])
        blocks[1], far, near_and_far, pair, wide_other, following, narrow = tie(
            (blocks[1], far, near_and_far, pair, wide_other, following, narrow))
        ax, ay = hop(far, 0, x), hop(far, 0, y)
        rest = hop(near_and_far, 2)
        blocks[2] = hop(pair[2], 4)
        following.append(following_of(blocks[1]))
        ax, ay, rest, blocks[2], following, pair[3] = tie((ax, ay, rest, blocks[2], following, pair[3]))
        bx, by = hop(rest, 0, x), hop(rest, 0, y)
        both = jnp.concatenate([pair[3].reshape(-1, ROWS, width), narrow.reshape(-1, ROWS, width)], axis=0)
        blocks[3] = hop(both, 6)
        early = [hop(far, 1), hop(rest, 1)]
        narrow_other = hop(narrow, 1)
        ay, bx, by, early, ax = tie((ay, bx, by, early, ax))
        axy = hop(ax, 0, y)
        bxy = jnp.stack([hop(bx[0], 0, y), hop(by[1], 0, x)])
        swaps = [early[0], hop(ax, 1), hop(ay, 1), None]
        swaps += [early[1], hop(bx, 1), hop(by, 1)]
        with_sibling(wide, [((), columns, 0, None)], wide_other)
        for e, value in enumerate((far, ax, ay)):
            with_sibling(value, [((), size, 2, e)], swaps[e])
        for e, value in enumerate((rest, bx, by)):
            with_sibling(value, [((n,), size, z, e) for n, z in enumerate((1, 3))], swaps[4 + e])
        full_rows = 6 * half
        plan = dict(half=half, columns=columns, over=over, pieces=slabs, moves=moves)
        full = pl.pallas_call(
            functools.partial(gather_kernel, plan),
            out_shape=jax.ShapeDtypeStruct((full_rows, width), jnp.bfloat16),
            in_specs=[smem] + [anywhere] * len(operands),
            out_specs=anywhere,
            scratch_shapes=[pltpu.SemaphoreType.DMA((len(moves),))],
            compiler_params=params,
            cost_estimate=pl.CostEstimate(flops=0, bytes_accessed=0, transcendentals=0),
            name="gather",
        )(own_index, *operands)
        operands.clear()
        moves.clear()
        bxy, swaps, blocks[3], full = tie((bxy, swaps, blocks[3], full))
        out_far = blocks[3][2 * groups :].reshape(narrow.shape)
        swaps.append(hop(bxy, 1))
        swaps[3] = hop(axy, 1)
        with_sibling(axy, [((), size, 2, 3)], swaps[3])
        with_sibling(bxy, [((n,), size, z, 3) for n, z in enumerate((1, 3))], swaps[7])
        near_half = [m for m in moves if m[3] < middle]
        far_half = [m for m in moves if m[3] >= middle]
        by_kind = [[(False, near_half), (True, far_half)], [(True, near_half), (False, far_half)]]
    else:
        full = lax.all_gather(wide, "seq", axis=0, tiled=True)
        by_kind = [[], []]
        out_operands = [lax.all_gather(narrow, "seq", axis=0, tiled=True)]
        out_moves = [(0, (), 0)]
        blocks = [hop(pair[z], 2 * z) if z else pair[z] for z in range(chips)]
        following = [following_of(value) for value in blocks[: chips // 2]]

    tokens = count * block_rows

    def attention(kind, inputs, full):
        inputs = [value.reshape((-1,) + block.shape[1:]) for value in inputs]
        plan = dict(kind=kind, weights=len(operands), inputs=len(inputs), half=half, moves=by_kind[kind],
                    columns=columns, over=over, pieces=slabs)
        copies = max([1] + [len(entries) for _, entries in by_kind[kind]])
        return pl.pallas_call(
            functools.partial(block_kernel, plan, frames),
            out_shape=[jax.ShapeDtypeStruct((groups, middle, ROWS, lanes), jnp.bfloat16)] * 2
            + [jax.ShapeDtypeStruct(full.shape, full.dtype)],
            in_specs=[smem] + [anywhere] * len(inputs) + [vmem] + [anywhere] * len(operands),
            out_specs=[vmem] * 3,
            input_output_aliases={1 + len(inputs): 2},
            scratch_shapes=[
                pltpu.VMEM((groups, count, ROWS, width), jnp.bfloat16),
                pltpu.VMEM((lanes, tokens), jnp.bfloat16),
                pltpu.VMEM((tokens, lanes), jnp.bfloat16),
                pltpu.VMEM((half, tokens), jnp.bfloat16),
                pltpu.SemaphoreType.DMA((count,)),
                pltpu.SemaphoreType.DMA((copies,)),
            ],
            compiler_params=params,
            cost_estimate=pl.CostEstimate(flops=SPACE_FLOPS, bytes_accessed=8 * 1024 * 1024,
                                          transcendentals=0),
            name=("windowed", "shifted")[kind],
        )(own_index, *inputs, full, *operands)

    second_near, second_far, full = attention(1, blocks + following, full)
    if shared:
        out_rest = hop(jnp.stack([narrow, out_far]), 2)
    second_near = to_neighbour(second_near, 1)
    first_near, first_far, full = attention(0, blocks, full)
    def merged(first_z, first, second, flops):
        return pl.pallas_call(
            functools.partial(merge_kernel, first_z),
            out_shape=[jax.ShapeDtypeStruct((2,) + block.shape, block.dtype)] * (chips // 2),
            in_specs=[smem] + [vmem] * 2,
            out_specs=[vmem] * (chips // 2),
            compiler_params=params,
            cost_estimate=pl.CostEstimate(flops=flops, bytes_accessed=4 * 1024 * 1024, transcendentals=0),
            name="merge",
        )(own_index, first, second)

    sent_far = merged(chips // 2, first_far, second_far, 0)
    if shared:
        out_rest, second_near = tie((out_rest, second_near))
    sent_near = merged(0, first_near, second_near, 0)
    sent = sent_near + sent_far
    arrived = [hop(sent[z], 2 * z) if z else sent[z] for z in range(chips // 2)]
    singles = [hop(sent[z][n], 2 * z + n)[None] for z in range(chips // 2, chips) for n in range(2)]
    if shared:
        out_operands = [narrow, narrow_other, out_far, hop(out_far, 1), out_rest, hop(out_rest, 1)]
        out_moves = [(0, (), (0,)), (1, (), (1,)), (2, (), (6,)), (3, (), (7,)), (4, (0,), (2,)), (5, (0,), (3,)),
                     (4, (1,), (4,)), (5, (1,), (5,))]
    out_full = pl.pallas_call(
        functools.partial(gather_out_kernel, out_moves),
        out_shape=jax.ShapeDtypeStruct((width, width), jnp.bfloat16),
        in_specs=[smem] + [anywhere] * len(out_operands),
        out_specs=anywhere,
        scratch_shapes=[pltpu.SemaphoreType.DMA((len(out_moves),))],
        compiler_params=params,
        name="gather_out",
    )(own_index, *out_operands)
    if shared:
        arrived, singles = tie((arrived, singles))
    returned = []
    for value in arrived:
        returned += [value, hop(value, 1)]
    returned += singles
    return pl.pallas_call(
        functools.partial(restore_kernel, count),
        out_shape=jax.ShapeDtypeStruct(video_tokens.shape, video_tokens.dtype),
        in_specs=[smem] + [vmem] * (3 + count),
        out_specs=vmem,
        scratch_shapes=[pltpu.VMEM((width // LANES, tokens, LANES), jnp.float32)],
        compiler_params=params,
        name="restore",
    )(own_index, video_tokens, kinds, out_full, *returned)


def solution(mesh):
    return jax.shard_map(
        per_device,
        mesh=mesh,
        in_specs=(
            P(("slab", "seq"), None, None),
            P(("slab", "seq"), None, None),
            P(None, "seq"),
            P(None, "seq"),
        ),
        out_specs=P(("slab", "seq"), None, None),
        check_vma=False,
    )
```
